32 devices in a mesh: gx: 4 (over z), gy: 8 (over y, x, core).
Axes of the slice: x: 2, y: 2, z: 4, core: 2. Of those that a mesh axis runs over, the one named last changes fastest.
Arguments:
- tokens: bfloat16 [64, 1024, 512], P(('gx', 'gy')), may hold values from -6 to 6
- segment_ids: int32 [64, 1024], P(('gx', 'gy')), may hold values from 0 to 5, never falling along the last dimension, each value on 1 to 512 neighbouring positions
- fill_lengths: int32 [64], P(('gx', 'gy')), may hold values from 256 to 1024
- joint_weight: bfloat16 [512, 1536], P(('gx', 'gy')), may hold values from -0.25 to 0.25
- joint_bias: bfloat16 [2, 512], P(None, ('gx', 'gy')), may hold values from -3 to 3
- mix_weight: bfloat16 [512, 512], P(('gx', 'gy')), may hold values from -1 to 1
- mix_bias: bfloat16 [512], P(('gx', 'gy')), may hold values from -3 to 3
- lift_weight: bfloat16 [512, 2048], P(('gx', 'gy')), may hold values from -0.25 to 0.25
- lift_bias: bfloat16 [2048], P(('gx', 'gy')), may hold values from -3 to 3
- drop_weight: bfloat16 [2048, 512], P(('gx', 'gy')), may hold values from -0.125 to 0.125
- drop_bias: bfloat16 [512], P(('gx', 'gy')), may hold values from -3 to 3
- cotangent: bfloat16 [64, 1024, 512], P(('gx', 'gy')), may hold values from -6 to 6
Outputs:
- layer_output: bfloat16 [64, 1024, 512], P(('gx', 'gy'))
- token_grad: float32 [64, 1024, 512], P(('gx', 'gy'))
- joint_weight_grad: float32 [512, 1536], P(('gx', 'gy'))
- joint_bias_grad: float32 [2, 512], P(None, ('gx', 'gy'))
- mix_weight_grad: float32 [512, 512], P(('gx', 'gy'))
- mix_bias_grad: float32 [512], P(('gx', 'gy'))
- lift_weight_grad: float32 [512, 2048], P(('gx', 'gy'))
- lift_bias_grad: float32 [2048], P(('gx', 'gy'))
- drop_weight_grad: float32 [2048, 512], P(('gx', 'gy'))
- drop_bias_grad: float32 [512], P(('gx', 'gy'))
The draws below stay inside these ranges and needn't reach their ends.
Inputs may be any that keep to these rules, and one draw needn't show every extreme that they name: `segment_ids`: along each row the pair numbers never fall, and a pair holds 1 to 512 positions.
All inputs are finite; a program needn't handle non-finite values.
Results may differ from the reference program's by a relative error of at most 0.012.
The reference program's roundings to bfloat16 on the way count: a program that leaves them out, or rounds other values in their place, can miss the bound.
Values may be sent and summed in bfloat16 or wider, within the bound.
A program may use at most 192 MiB of HBM per device.

```python
import math
import jax
import jax.numpy as jnp
import numpy as np
from jax import lax

D = 512
HEADS = 8
HEAD = 64
FF = 2048
SEQ = 1024
SEGS = 6
ROWS = 64


def draw_fill_lengths(key, part):
    key = jax.random.fold_in(key, 7)
    first_key, second_key, third_key = jax.random.split(key, 3)
    base_fill = jax.random.randint(first_key, (ROWS,), SEQ // 4, SEQ + 1)
    top_row = jax.random.randint(second_key, (), 0, ROWS)
    short_row = (top_row + 1 + jax.random.randint(third_key, (), 0, ROWS - 1)) % ROWS
    positions = jnp.arange(ROWS)
    base_fill = jnp.where(positions == top_row, SEQ, base_fill)
    return jnp.where(positions == short_row, SEQ // 4, base_fill).astype(jnp.int32)


def strengthened(array, rng, source, target, parts, factor):
    owner, partner = [(jnp.arange(array.shape[dim]) // (array.shape[dim] // parts)).reshape([-1 if axis == dim else 1 for axis in range(array.ndim)]) for dim in (source, target)]
    chosen = jax.random.permutation(rng, parts)[partner]
    strong = (owner == chosen) | (owner == (partner + parts // 2) % parts)
    return jnp.where(strong, factor * array, array)


def block_levels(own_key, dims, cuts, smallest, high):
    def one(dim, shards_of):
        heights = jax.random.uniform(jax.random.fold_in(jax.random.fold_in(own_key, 6), dim), (shards_of,), jnp.float32, smallest / len(cuts), high / len(cuts))
        return jnp.repeat(jnp.exp(heights), dims[dim] // shards_of).reshape((-1,) + (1,) * (len(dims) - dim - 1))

    level = one(*cuts[0])
    for cut in cuts[1:]:
        level = level * one(*cut)
    return level


def length_profile(number_of, total, most, skew):
    weights = [(1 << 20) // math.isqrt(rank ** skew) + 1 for rank in range(2, number_of + 1)]
    spare, holding = total - most - (number_of - 1), [1] * (number_of - 1)
    while spare > 0:
        candidates = [i for i in range(number_of - 1) if holding[i] < most]
        mass, left = sum([weights[i] for i in candidates]), spare
        for i in candidates:
            more = min(most - holding[i], max(1, left * weights[i] // mass), spare)
            holding[i] = holding[i] + more
            spare = spare - more
    return np.array([most] + holding)


def ragged(own_key, number_of, total, bound, lean):
    if number_of == 2:
        one = jax.random.randint(own_key, (), max(1, total - bound), min(bound, total - 1) + 1)
        return jnp.stack([one, total - one])
    sizes = jnp.asarray(length_profile(number_of, total, bound, lean), jnp.int32)
    twos = (number_of - 1) // 2
    giver, sink = sizes[1:1 + 2 * twos:2], sizes[2:2 + 2 * twos:2]
    margin = jnp.minimum(giver - 1, bound - sink)
    passed = jax.random.randint(jax.random.fold_in(own_key, 1), (twos,), 0, 1 << 20) % (margin + 1)
    sizes = sizes.at[1:1 + 2 * twos:2].set(giver - passed).at[2:2 + 2 * twos:2].set(sink + passed)
    return sizes[jax.random.permutation(jax.random.fold_in(own_key, 2), number_of)]


def centred(stream_key, dims, width, most, cuts=(), held_as=jnp.bfloat16):
    entries = jax.random.normal(stream_key, dims, jnp.float32) * width
    if len(cuts) > 0:
        entries = block_levels(stream_key, dims, cuts, -0.22, 0.18) * entries
    return jnp.clip(entries, min=-most, max=most).astype(held_as)


def heavy_noise(rng, dims, scale, most, cuts, heavy, kind=jnp.bfloat16):
    entries = scale * jax.random.normal(rng, dims, jnp.float32)
    if cuts:
        entries = entries * block_levels(rng, dims, cuts, -0.22, 0.18)
    return jnp.clip(strengthened(entries, jax.random.fold_in(rng, 3), *heavy), -most, most).astype(kind)


def setup_inputs(seed: int = 0) -> dict:
    seeds = jax.random.split(jax.random.key(seed), 13)
    tokens = centred(seeds[0], (ROWS, SEQ, D), 1.0, 6.0, ((0, 32),))
    segment_ids = jax.vmap(lambda own: jnp.searchsorted(jnp.cumsum(ragged(own, SEGS, SEQ, SEQ // 2, 0)), jnp.arange(SEQ), side="right"))(jax.random.split(seeds[1], ROWS)).reshape((ROWS, SEQ)).astype(jnp.int32)
    fill_lengths = draw_fill_lengths(jax.random.fold_in(seeds[12], 71), 0)
    joint_weight = centred(seeds[3], (D, 3 * D), D ** -0.5, 0.25, ((0, 32),))
    joint_bias = centred(seeds[4], (2, D), 0.5, 3.0, ((1, 32),))
    mix_weight = centred(seeds[5], (D, D), (D // 16) ** -0.5, 1.0, ((0, 32),))
    mix_bias = centred(seeds[6], (D,), 0.5, 3.0, ((0, 32),))
    lift_weight = centred(seeds[7], (D, FF), D ** -0.5, 0.25, ((0, 32),))
    lift_bias = centred(seeds[8], (FF,), 0.5, 3.0, ((0, 32),))
    drop_weight = centred(seeds[9], (FF, D), FF ** -0.5, 0.125, ((0, 32),))
    drop_bias = centred(seeds[10], (D,), 0.5, 3.0, ((0, 32),))
    cotangent = heavy_noise(seeds[11], (ROWS, SEQ, D), 1.0, 6.0, ((0, 32),), (0, 2, 32, 2.75))
    return dict(tokens=tokens, segment_ids=segment_ids, fill_lengths=fill_lengths, joint_weight=joint_weight, joint_bias=joint_bias, mix_weight=mix_weight, mix_bias=mix_bias, lift_weight=lift_weight, lift_bias=lift_bias, drop_weight=drop_weight, drop_bias=drop_bias, cotangent=cotangent)


@jax.custom_vjp
def low(v):
    return lax.optimization_barrier(v.astype(jnp.bfloat16)).astype(jnp.float32)

@jax.custom_vjp
def low_back(v):
    return v

def low_keep(v):
    return (low(v), None)

def low_pass(kept, grad):
    return (grad,)

def back_keep(v):
    return (v, None)

def back_low(kept, grad):
    return (low(grad),)
low.defvjp(low_keep, low_pass)
low_back.defvjp(back_keep, back_low)

def matmul(left, right):
    return jnp.dot(left, right, precision=lax.Precision.HIGHEST)

def row_attention(joint_rows, seg_row, fill_len):
    length = joint_rows.shape[0]
    block_size = min(512, length)
    block_count = length // block_size
    score_scale = 1.0 / math.sqrt(HEAD)
    row_parts = joint_rows.reshape(length, 3, HEADS, HEAD)
    key_rows = row_parts[:, 1]
    value_rows = row_parts[:, 2]
    query_blocks = row_parts[:, 0].reshape(block_count, block_size, HEADS, HEAD)
    seg_blocks = seg_row.reshape(block_count, block_size)
    starts = jnp.arange(block_count, dtype=jnp.int32) * block_size
    positions = jnp.arange(length, dtype=jnp.int32)

    def one_block(block_args):
        query_block, seg_query, start = block_args
        row_ids = start + jnp.arange(block_size, dtype=jnp.int32)
        allowed = (seg_query[:, None] == seg_row[None, :]) & (positions < fill_len)[None, :] | (row_ids[:, None] == positions[None, :])
        raw_scores = jnp.einsum('qhd,khd->hqk', query_block, key_rows, precision=lax.Precision.HIGHEST)
        scores = low_back(jnp.where(allowed[None], raw_scores * score_scale, -1000000000.0))
        weights = low(jax.nn.softmax(scores, axis=-1))
        return jnp.einsum('hqk,khd->qhd', weights, value_rows, precision=lax.Precision.HIGHEST)
    result = lax.map(jax.checkpoint(one_block), (query_blocks, seg_blocks, starts))
    return result.reshape(length, HEADS * HEAD)

def row_layer(row_tokens, seg_row, fill_len, params):
    joint_weight, joint_bias, mix_weight, mix_bias, lift_weight, lift_bias, drop_weight, drop_bias = params
    model_width = row_tokens.shape[1]
    joint_shift = jnp.concatenate([joint_bias[0], jnp.zeros((model_width,), row_tokens.dtype), joint_bias[1]])
    joint_rows = low(low_back(matmul(row_tokens, joint_weight) + joint_shift))
    context = low(low_back(row_attention(joint_rows, seg_row, fill_len)))
    branch = low_back(matmul(context, mix_weight) + mix_bias)
    middle = row_tokens + branch
    hidden_in = low(middle)
    lifted = low_back(matmul(hidden_in, lift_weight) + lift_bias)
    active = low(jax.nn.gelu(lifted))
    dropped = low_back(matmul(active, drop_weight) + drop_bias)
    return middle + dropped

def reference(tokens, segment_ids, fill_lengths, joint_weight, joint_bias, mix_weight, mix_bias, lift_weight, lift_bias, drop_weight, drop_bias, cotangent):
    params = tuple((p.astype(jnp.float32) for p in (joint_weight, joint_bias, mix_weight, mix_bias, lift_weight, lift_bias, drop_weight, drop_bias)))

    def forward(all_tokens, *weights):

        def one_row(row_args):
            row_tokens, seg_row, fill_len = row_args
            return row_layer(row_tokens, seg_row, fill_len, weights)
        return lax.map(jax.checkpoint(one_row), (all_tokens, segment_ids, fill_lengths))
    output, pullback = jax.vjp(forward, tokens.astype(jnp.float32), *params)
    gradients = pullback(cotangent.astype(jnp.float32))
    return (output.astype(jnp.bfloat16), gradients[0], gradients[1], gradients[2], gradients[3], gradients[4], gradients[5], gradients[6], gradients[7], gradients[8])
```

```python
import functools
import math

import jax
import jax.numpy as jnp
from jax import lax
from jax.experimental import pallas as pl
from jax.experimental.pallas import tpu as pltpu
from jax.sharding import PartitionSpec as P

BF = jnp.bfloat16
F32 = jnp.float32
NT = (((1,), (1,)), ((), ()))
NN = (((1,), (0,)), ((), ()))
NEG = -float(2**30)
C0 = math.sqrt(2.0 / math.pi)
C1 = 0.044715
CUT = 2
VMEM_LIMIT = 60 * 2**20


def mm(a, b, dims=NN):
    return lax.dot_general(a, b, dims, preferred_element_type=F32)


def split_heads(x):
    lane = lax.broadcasted_iota(jnp.int32, x.shape, 1)
    zero = jnp.zeros_like(x)
    return jnp.concatenate([jnp.where(lane < 64, x, zero), jnp.where(lane < 64, zero, x)], axis=0)


def diag_blocks(y):
    return jnp.concatenate([y[:64, :128], y[64:, 128:]], axis=0)


def window(starts_ref, fill_ref, row, t, length):
    first = t * 128
    last = first + 127
    fill = fill_ref[row]
    lo = jnp.int32(0)
    hi = jnp.int32(length)
    for v in range(1, 6):
        s = starts_ref[row, v]
        lo = jnp.where(s <= first, jnp.maximum(lo, s), lo)
        hi = jnp.where(s > last, jnp.minimum(hi, s), hi)
    hi = jnp.minimum(hi, fill)
    alone = lo >= fill
    hi = jnp.where(last >= fill, jnp.maximum(hi, last + 1), hi)
    lo = jnp.where(alone, first, lo)
    lo_b = lo // 128
    return lo_b, (hi + 127) // 128 - lo_b


def write_mask(mask_ref, segk_ref, seg_ref, fill, t, lo_b, n):
    segq = seg_ref[0, :, pl.ds(pl.multiple_of(t * 128, 128), 128)]
    segq = jnp.broadcast_to(segq, (128, 128))
    qi = t * 128 + lax.broadcasted_iota(jnp.int32, (128, 128), 1)
    ki0 = lax.broadcasted_iota(jnp.int32, (128, 128), 0)
    for c in range(n):
        off = pl.multiple_of((lo_b + c) * 128, 128)
        ki = ki0 + off
        ok = ((segk_ref[pl.ds(off, 128), :] == segq) & (ki < fill)) | (ki == qi)
        mask_ref[c * 128 : (c + 1) * 128, :] = jnp.where(ok, 0.0, NEG)


def spread_segments(seg_ref, segk_ref, length):
    for b in range(length // 128):
        row = seg_ref[0, :, b * 128 : (b + 1) * 128].astype(F32)
        segk_ref[b * 128 : (b + 1) * 128, :] = jnp.broadcast_to(row, (128, 128)).T.astype(jnp.int32)


def attend_kernel(
    starts_ref, fill_ref, seg_ref, qkv_ref, ctx_ref, lse_ref, vt_ref, segk_ref, mask_ref, s_ref, p_ref, *, length
):
    row = pl.program_id(0)
    fill = fill_ref[row]
    spread_segments(seg_ref, segk_ref, length)
    for b in range(length // 128):
        for p in range(4):
            v = qkv_ref[0, b * 128 : (b + 1) * 128, 1024 + p * 128 : 1024 + (p + 1) * 128]
            vt_ref[p * 128 : (p + 1) * 128, b * 128 : (b + 1) * 128] = v.T

    def tile(t, lo_b, n):
        tq = pl.ds(pl.multiple_of(t * 128, 128), 128)
        win = pl.ds(pl.multiple_of(lo_b * 128, 128), n * 128)
        cuts = [(c, min(CUT, n - c)) for c in range(0, n, CUT)]
        tops, sums = [], []
        for p in range(4):
            lanes = slice(p * 128, (p + 1) * 128)
            qbd = split_heads(qkv_ref[0, tq, lanes] * jnp.asarray(0.125, BF))
            top = None
            for c, w in cuts:
                rows = pl.ds(pl.multiple_of((lo_b + c) * 128, 128), w * 128)
                s = mm(qkv_ref[0, rows, 512 + p * 128 : 512 + (p + 1) * 128], qbd, NT)
                mask = mask_ref[c * 128 : (c + w) * 128, :]
                s = s + jnp.concatenate([mask, mask], axis=1)
                s_ref[p, c * 128 : (c + w) * 128, :] = s
                part = jnp.max(s.reshape(w * 16, 8, 256), axis=0)
                top = part if top is None else jnp.maximum(top, part)
            tops.append(jnp.max(top, axis=0, keepdims=True))
        for p in range(4):
            total = None
            for c, w in cuts:
                e = jnp.exp(s_ref[p, c * 128 : (c + w) * 128, :] - tops[p])
                p_ref[p, c * 128 : (c + w) * 128, :] = e.astype(BF)
                part = jnp.sum(e.reshape(w * 16, 8, 256), axis=0)
                total = part if total is None else total + part
            sums.append(jnp.sum(total, axis=0, keepdims=True))
        for p in range(4):
            o = mm(vt_ref[p * 128 : (p + 1) * 128, win], p_ref[p, : n * 128, :]) * (1.0 / sums[p])
            ctx_ref[0, tq, p * 128 : (p + 1) * 128] = diag_blocks(o).T.astype(BF)
            lse_ref[0, p, pl.ds(t, 1), :] = tops[p] + jnp.log(sums[p])

    @pl.loop(0, length // 128)
    def _(t):
        lo_b, n = window(starts_ref, fill_ref, row, t, length)
        for k in range(1, length // 128 + 1):

            @pl.when(n == k)
            def _(k=k):
                write_mask(mask_ref, segk_ref, seg_ref, fill, t, lo_b, k)
                tile(t, lo_b, k)


def attend(starts, fill, seg, qkv):
    rows, length, _ = qkv.shape
    blocks = length // 128
    return pl.pallas_call(
        functools.partial(attend_kernel, length=length),
        grid_spec=pltpu.PrefetchScalarGridSpec(
            num_scalar_prefetch=2,
            grid=(rows,),
            in_specs=[
                pl.BlockSpec((1, 1, length), lambda r, *_: (r, 0, 0)),
                pl.BlockSpec((1, length, 1536), lambda r, *_: (r, 0, 0)),
            ],
            out_specs=[
                pl.BlockSpec((1, length, 512), lambda r, *_: (r, 0, 0)),
                pl.BlockSpec((1, 4, blocks, 256), lambda r, *_: (r, 0, 0, 0)),
            ],
            scratch_shapes=[
                pltpu.VMEM((512, length), BF),
                pltpu.VMEM((length, 128), jnp.int32),
                pltpu.VMEM((length, 128), F32),
                pltpu.VMEM((4, length, 256), F32),
                pltpu.VMEM((4, length, 256), BF),
            ],
        ),
        out_shape=[
            jax.ShapeDtypeStruct((rows, length, 512), BF),
            jax.ShapeDtypeStruct((rows, 4, blocks, 256), F32),
        ],
        compiler_params=pltpu.CompilerParams(vmem_limit_bytes=VMEM_LIMIT),
        name="attend",
    )(starts, fill, seg, qkv)


def attend_back_kernel(
    starts_ref,
    fill_ref,
    seg_ref,
    qkv_ref,
    lse_ref,
    ctx_ref,
    do_ref,
    out_ref,
    kt_ref,
    segk_ref,
    mask_ref,
    dk_ref,
    dv_ref,
    p_ref,
    ds_ref,
    *,
    length,
):
    row = pl.program_id(0)
    fill = fill_ref[row]
    spread_segments(seg_ref, segk_ref, length)
    for b in range(length // 128):
        for p in range(4):
            k = qkv_ref[0, b * 128 : (b + 1) * 128, 512 + p * 128 : 512 + (p + 1) * 128]
            kt_ref[p * 128 : (p + 1) * 128, b * 128 : (b + 1) * 128] = k.T
    dk_ref[...] = jnp.zeros_like(dk_ref)
    dv_ref[...] = jnp.zeros_like(dv_ref)

    def tile(t, lo_b, n):
        tq = pl.ds(pl.multiple_of(t * 128, 128), 128)
        win = pl.ds(pl.multiple_of(lo_b * 128, 128), n * 128)
        ready = []
        for p in range(4):
            lanes = slice(p * 128, (p + 1) * 128)
            qbd = split_heads(qkv_ref[0, tq, lanes] * jnp.asarray(0.125, BF))
            do = do_ref[0, tq, lanes]
            prod = (do.astype(F32) * ctx_ref[0, tq, lanes].astype(F32)).T
            delta = jnp.concatenate(
                [jnp.sum(prod[:64], axis=0, keepdims=True), jnp.sum(prod[64:], axis=0, keepdims=True)], axis=1
            )
            ready.append((qbd, split_heads(do), delta, lse_ref[0, p, pl.ds(t, 1), :]))
        for c in range(0, n, CUT):
            w = min(CUT, n - c)
            rows = pl.ds(pl.multiple_of((lo_b + c) * 128, 128), w * 128)
            here = slice(c * 128, (c + w) * 128)
            for p in range(4):
                qbd, dobd, delta, lse = ready[p]
                s = mm(qkv_ref[0, rows, 512 + p * 128 : 512 + (p + 1) * 128], qbd, NT)
                dp = mm(qkv_ref[0, rows, 1024 + p * 128 : 1024 + (p + 1) * 128], dobd, NT)
                mask = mask_ref[here, :]
                e = jnp.exp(s + jnp.concatenate([mask, mask], axis=1) - lse)
                p_ref[p, here, :] = e.astype(BF)
                ds_ref[p, here, :] = (e * (dp - delta)).astype(BF)
            for p in range(4):
                qbd, dobd, _, _ = ready[p]
                lanes = slice(p * 128, (p + 1) * 128)
                dv_ref[rows, lanes] += mm(p_ref[p, here, :], dobd)
                dk_ref[rows, lanes] += mm(ds_ref[p, here, :], qbd)
        for p in range(4):
            lanes = slice(p * 128, (p + 1) * 128)
            dq = mm(kt_ref[lanes, win], ds_ref[p, : n * 128, :])
            out_ref[0, tq, lanes] = (diag_blocks(dq) * 0.125).T.astype(BF)

    @pl.loop(0, length // 128)
    def _(t):
        lo_b, n = window(starts_ref, fill_ref, row, t, length)
        for k in range(1, length // 128 + 1):

            @pl.when(n == k)
            def _(k=k):
                write_mask(mask_ref, segk_ref, seg_ref, fill, t, lo_b, k)
                tile(t, lo_b, k)

    out_ref[0, :, 512:1024] = dk_ref[...].astype(BF)
    out_ref[0, :, 1024:1536] = dv_ref[...].astype(BF)


def attend_back(starts, fill, seg, qkv, lse, ctx, do):
    rows, length, _ = qkv.shape
    blocks = length // 128
    return pl.pallas_call(
        functools.partial(attend_back_kernel, length=length),
        grid_spec=pltpu.PrefetchScalarGridSpec(
            num_scalar_prefetch=2,
            grid=(rows,),
            in_specs=[
                pl.BlockSpec((1, 1, length), lambda r, *_: (r, 0, 0)),
                pl.BlockSpec((1, length, 1536), lambda r, *_: (r, 0, 0)),
                pl.BlockSpec((1, 4, blocks, 256), lambda r, *_: (r, 0, 0, 0)),
                pl.BlockSpec((1, length, 512), lambda r, *_: (r, 0, 0)),
                pl.BlockSpec((1, length, 512), lambda r, *_: (r, 0, 0)),
            ],
            out_specs=pl.BlockSpec((1, length, 1536), lambda r, *_: (r, 0, 0)),
            scratch_shapes=[
                pltpu.VMEM((512, length), BF),
                pltpu.VMEM((length, 128), jnp.int32),
                pltpu.VMEM((length, 128), F32),
                pltpu.VMEM((length, 512), F32),
                pltpu.VMEM((length, 512), F32),
                pltpu.VMEM((4, length, 256), BF),
                pltpu.VMEM((4, length, 256), BF),
            ],
        ),
        out_shape=jax.ShapeDtypeStruct((rows, length, 1536), BF),
        compiler_params=pltpu.CompilerParams(vmem_limit_bytes=VMEM_LIMIT),
        name="attend_back",
    )(starts, fill, seg, qkv, lse, ctx, do)


def gelu_pair(x, grad):
    x2 = x * x
    h = 0.5 + 0.5 * jnp.tanh(x * (C0 + (C0 * C1) * x2))
    act = x * h
    slope = h + act * (1.0 - h) * (2.0 * C0 + (6.0 * C0 * C1) * x2)
    return act.astype(BF), (grad * slope).astype(BF)


def feed_kernel(
    tok_ref,
    ctx_ref,
    cot_ref,
    mix_ref,
    lift_ref,
    drop_ref,
    bias_ref,
    out_ref,
    gmid_ref,
    gctx_ref,
    glift_ref,
    gdrop_ref,
    gmix_ref,
    gbias_ref,
    hid_ref,
    hidt_ref,
    cott_ref,
    acc_ref,
    act_ref,
    gl_ref,
    *,
    tb,
):
    tokens, width = tok_ref.shape
    nf = lift_ref.shape[0]
    nb = tokens // tb
    ones = jnp.ones((16, tb), BF)

    @pl.loop(0, nb)
    def _(b):
        rows = pl.ds(pl.multiple_of(b * tb, tb), tb)
        mid = tok_ref[rows, :].astype(F32) + mm(ctx_ref[rows, :], mix_ref[...]) + bias_ref[5:6, :]
        acc_ref[rows, :] = mid + bias_ref[4:5, :]
        h = mid.astype(BF)
        hid_ref[rows, :] = h
        hidt_ref[0:width, rows] = h.T
        hidt_ref[width : width + 16, rows] = ones
        c = cot_ref[rows, :]
        cott_ref[:, rows] = c.T
        gmid_ref[rows, :] = c.astype(F32)

    def stage1(f, b):
        rows = pl.ds(b * tb, tb)
        for n in range(0, 512, 256):
            x = mm(hid_ref[rows, :], lift_ref[f, :, n : n + 256]) + bias_ref[pl.ds(f, 1), n : n + 256]
            grad = mm(cot_ref[rows, :], drop_ref[f, n : n + 256, :], NT)
            a, g = gelu_pair(x, grad)
            act_ref[b, :, n : n + 256] = a
            gl_ref[b, :, n : n + 256] = g

    def stage2(f, b):
        rows = pl.ds(b * tb, tb)
        act = act_ref[b]
        gl = gl_ref[b]
        acc_ref[rows, :] += mm(act, drop_ref[f])
        gmid_ref[rows, :] += mm(gl, lift_ref[f], NT)
        gd = mm(cott_ref[:, rows], act)
        gf = mm(hidt_ref[:, rows], gl)
        if b == 0:
            gdrop_ref[f] = gd
            glift_ref[f] = gf
        else:
            gdrop_ref[f] += gd
            glift_ref[f] += gf

    @pl.loop(0, nf)
    def _(f):
        stage1(f, 0)
        for b in range(1, nb):
            stage1(f, b)
            stage2(f, b - 1)
        stage2(f, nb - 1)

    gmix_ref[...] = jnp.zeros_like(gmix_ref)
    gbias_ref[...] = jnp.zeros_like(gbias_ref)

    @pl.loop(0, nb)
    def _(b):
        rows = pl.ds(pl.multiple_of(b * tb, tb), tb)
        out_ref[rows, :] = acc_ref[rows, :].astype(BF)
        gb = gmid_ref[rows, :].astype(BF)
        gctx_ref[rows, :] = mm(gb, mix_ref[...], NT).astype(BF)
        gmix_ref[...] += mm(ctx_ref[rows, :].T, gb)
        gbias_ref[5:6, :] += mm(ones, gb)[0:1]
        gbias_ref[4:5, :] += mm(ones, cot_ref[rows, :])[0:1]

    for f in range(nf):
        gbias_ref[f : f + 1, :] = glift_ref[f, width : width + 1, :]


def feed(tok, ctx, cot, mix, lift, drop, bias):
    tokens, width = tok.shape
    nf = lift.shape[0]
    tb = 512
    vmem = pl.BlockSpec(memory_space=pltpu.VMEM)
    return pl.pallas_call(
        functools.partial(feed_kernel, tb=tb),
        in_specs=[vmem] * 7,
        out_specs=[vmem] * 7,
        out_shape=[
            jax.ShapeDtypeStruct((tokens, width), BF),
            jax.ShapeDtypeStruct((tokens, width), F32),
            jax.ShapeDtypeStruct((tokens, width), BF),
            jax.ShapeDtypeStruct((nf, width + 16, 512), F32),
            jax.ShapeDtypeStruct((nf, width, 512), F32),
            jax.ShapeDtypeStruct((width, width), F32),
            jax.ShapeDtypeStruct((8, 512), F32),
        ],
        scratch_shapes=[
            pltpu.VMEM((tokens, width), BF),
            pltpu.VMEM((width + 16, tokens), BF),
            pltpu.VMEM((width, tokens), BF),
            pltpu.VMEM((tokens, width), F32),
            pltpu.VMEM((tokens // tb, tb, 512), BF),
            pltpu.VMEM((tokens // tb, tb, 512), BF),
        ],
        compiler_params=pltpu.CompilerParams(vmem_limit_bytes=VMEM_LIMIT),
        name="feed",
    )(tok, ctx, cot, mix, lift, drop, bias)


BOTH = ("gx", "gy")


def body(
    tokens,
    segment_ids,
    fill_lengths,
    joint_weight,
    joint_bias,
    mix_weight,
    mix_bias,
    lift_weight,
    lift_bias,
    drop_weight,
    drop_bias,
    cotangent,
):
    rows, length, width = tokens.shape
    n_tok = rows * length
    tok = tokens.reshape(n_tok, width)
    cot = cotangent.reshape(n_tok, width)
    seg = segment_ids.reshape(rows, 1, length)
    starts = jnp.sum(
        segment_ids[:, None, :] < jnp.arange(8, dtype=jnp.int32)[None, :, None], axis=-1, dtype=jnp.int32
    )

    joint_w = lax.all_gather(joint_weight, BOTH, axis=0, tiled=True)
    mix_w = lax.all_gather(mix_weight, BOTH, axis=0, tiled=True)
    lift_w = lax.all_gather(lift_weight, BOTH, axis=0, tiled=True)
    drop_w = lax.all_gather(drop_weight, BOTH, axis=0, tiled=True)
    own_bias = jnp.concatenate([joint_bias.reshape(-1), mix_bias, lift_bias, drop_bias])
    sizes = [joint_bias.shape[1], joint_bias.shape[1], mix_bias.size, lift_bias.size, drop_bias.size]
    all_bias = lax.all_gather(own_bias, BOTH, axis=0)
    parts, at = [], 0
    for size in sizes:
        parts.append(all_bias[:, at : at + size].reshape(-1).astype(F32))
        at += size
    bq, bv, bm, bl, bd = parts
    nf = bl.size // 512
    bias = jnp.concatenate(
        [jnp.concatenate([bl.reshape(nf, 512), jnp.zeros((4 - nf, 512), F32)]), bd[None], bm[None], bq[None], bv[None]]
    )

    shift = jnp.concatenate([bq, jnp.zeros_like(bq), bv])
    qkv = (mm(tok, joint_w) + shift).astype(BF)
    qkv3 = qkv.reshape(rows, length, 3 * width)
    ctx, lse = attend(starts, fill_lengths, seg, qkv3)
    lift_units = lift_w.reshape(width, nf, 512).transpose(1, 0, 2)
    out, gmid, gctx, glift, gdrop, gmix, gbias = feed(
        tok, ctx.reshape(n_tok, width), cot, mix_w, lift_units, drop_w.reshape(nf, 512, width), bias
    )
    gjoint = attend_back(
        starts, fill_lengths, seg, qkv3, lse, ctx, gctx.reshape(rows, length, width)
    ).reshape(n_tok, 3 * width)
    gjoint_w = lax.dot_general(tok, gjoint, (((0,), (0,)), ((), ())), preferred_element_type=F32)
    sums = jnp.sum(gjoint.astype(F32), axis=0)
    token_grad = gmid + mm(gjoint, joint_w, NT)

    glift_w = glift[:, :width].transpose(1, 0, 2).reshape(width, nf * 512)
    gdrop_w = gdrop.transpose(0, 2, 1).reshape(nf * 512, width)
    scatter = functools.partial(lax.psum_scatter, axis_name=BOTH, scatter_dimension=0, tiled=True)
    n_dev = all_bias.shape[0]
    packed = jnp.concatenate(
        [
            g.reshape(n_dev, -1)
            for g in (sums[:width], sums[2 * width :], gbias[5], gbias[:nf].reshape(-1), gbias[4])
        ],
        axis=1,
    )
    own = scatter(packed)[0]
    cuts, at = [], 0
    for size in sizes:
        cuts.append(own[at : at + size])
        at += size
    return (
        out.reshape(rows, length, width),
        token_grad.reshape(rows, length, width),
        scatter(gjoint_w),
        jnp.stack([cuts[0], cuts[1]]),
        scatter(gmix),
        cuts[2],
        scatter(glift_w),
        cuts[3],
        scatter(gdrop_w),
        cuts[4],
    )


def solution(mesh):
    wide = P(BOTH, None, None)
    rows = P(BOTH, None)
    flat = P(BOTH)
    bias = P(None, BOTH)
    in_specs = (wide, rows, flat, rows, bias, rows, flat, rows, flat, rows, flat, wide)
    out_specs = (wide, wide, rows, bias, rows, flat, rows, flat, rows, flat)
    return jax.shard_map(body, mesh=mesh, in_specs=in_specs, out_specs=out_specs, check_vma=False)
```

```python
import functools
import math

import jax
import jax.numpy as jnp
from jax import lax
from jax.experimental import pallas as pl
from jax.experimental.pallas import tpu as pltpu
from jax.sharding import PartitionSpec as P

BF = jnp.bfloat16
F32 = jnp.float32
NT = (((1,), (1,)), ((), ()))
NN = (((1,), (0,)), ((), ()))
NEG = -float(2**30)
C0 = math.sqrt(2.0 / math.pi)
C1 = 0.044715
CUT = 2
VMEM_LIMIT = 60 * 2**20


def mm(a, b, dims=NN):
    return lax.dot_general(a, b, dims, preferred_element_type=F32)


def split_heads(x):
    lane = lax.broadcasted_iota(jnp.int32, x.shape, 1)
    zero = jnp.zeros_like(x)
    return jnp.concatenate([jnp.where(lane < 64, x, zero), jnp.where(lane < 64, zero, x)], axis=0)


def diag_blocks(y):
    return jnp.concatenate([y[:64, :128], y[64:, 128:]], axis=0)


def window(starts_ref, fill_ref, row, t, length):
    first = t * 128
    last = first + 127
    fill = fill_ref[row]
    lo = jnp.int32(0)
    hi = jnp.int32(length)
    for v in range(1, 6):
        s = starts_ref[row, v]
        lo = jnp.where(s <= first, jnp.maximum(lo, s), lo)
        hi = jnp.where(s > last, jnp.minimum(hi, s), hi)
    hi = jnp.minimum(hi, fill)
    alone = lo >= fill
    hi = jnp.where(last >= fill, jnp.maximum(hi, last + 1), hi)
    lo = jnp.where(alone, first, lo)
    lo_b = lo // 128
    return lo_b, (hi + 127) // 128 - lo_b


def write_mask(mask_ref, segk_ref, seg_ref, fill, t, lo_b, n):
    segq = seg_ref[0, :, pl.ds(pl.multiple_of(t * 128, 128), 128)]
    segq = jnp.broadcast_to(segq, (128, 128))
    qi = t * 128 + lax.broadcasted_iota(jnp.int32, (128, 128), 1)
    ki0 = lax.broadcasted_iota(jnp.int32, (128, 128), 0)
    for c in range(n):
        off = pl.multiple_of((lo_b + c) * 128, 128)
        ki = ki0 + off
        ok = ((segk_ref[pl.ds(off, 128), :] == segq) & (ki < fill)) | (ki == qi)
        mask_ref[c * 128 : (c + 1) * 128, :] = jnp.where(ok, 0.0, NEG)


def spread_segments(seg_ref, segk_ref, length):
    for b in range(length // 128):
        row = seg_ref[0, :, b * 128 : (b + 1) * 128].astype(F32)
        segk_ref[b * 128 : (b + 1) * 128, :] = jnp.broadcast_to(row, (128, 128)).T.astype(jnp.int32)


def attend_kernel(
    starts_ref, fill_ref, seg_ref, qkv_ref, ctx_ref, lse_ref, vt_ref, segk_ref, mask_ref, s_ref, p_ref, *, length
):
    row = pl.program_id(0)
    fill = fill_ref[row]
    spread_segments(seg_ref, segk_ref, length)
    for b in range(length // 128):
        for p in range(4):
            v = qkv_ref[0, b * 128 : (b + 1) * 128, 1024 + p * 128 : 1024 + (p + 1) * 128]
            vt_ref[p * 128 : (p + 1) * 128, b * 128 : (b + 1) * 128] = v.T

    def tile(t, lo_b, n):
        tq = pl.ds(pl.multiple_of(t * 128, 128), 128)
        win = pl.ds(pl.multiple_of(lo_b * 128, 128), n * 128)
        cuts = [(c, min(CUT, n - c)) for c in range(0, n, CUT)]
        tops, sums = [], []
        for p in range(4):
            lanes = slice(p * 128, (p + 1) * 128)
            qbd = split_heads(qkv_ref[0, tq, lanes] * jnp.asarray(0.125, BF))
            top = None
            for c, w in cuts:
                rows = pl.ds(pl.multiple_of((lo_b + c) * 128, 128), w * 128)
                s = mm(qkv_ref[0, rows, 512 + p * 128 : 512 + (p + 1) * 128], qbd, NT)
                mask = mask_ref[c * 128 : (c + w) * 128, :]
                s = s + jnp.concatenate([mask, mask], axis=1)
                s_ref[p, c * 128 : (c + w) * 128, :] = s
                part = jnp.max(s.reshape(w * 16, 8, 256), axis=0)
                top = part if top is None else jnp.maximum(top, part)
            tops.append(jnp.max(top, axis=0, keepdims=True))
        for p in range(4):
            total = None
            for c, w in cuts:
                e = jnp.exp(s_ref[p, c * 128 : (c + w) * 128, :] - tops[p])
                p_ref[p, c * 128 : (c + w) * 128, :] = e.astype(BF)
                part = jnp.sum(e.reshape(w * 16, 8, 256), axis=0)
                total = part if total is None else total + part
            sums.append(jnp.sum(total, axis=0, keepdims=True))
        for p in range(4):
            o = mm(vt_ref[p * 128 : (p + 1) * 128, win], p_ref[p, : n * 128, :]) * (1.0 / sums[p])
            ctx_ref[0, tq, p * 128 : (p + 1) * 128] = diag_blocks(o).T.astype(BF)
            lse_ref[0, p, pl.ds(t, 1), :] = tops[p] + jnp.log(sums[p])

    @pl.loop(0, length // 128)
    def _(t):
        lo_b, n = window(starts_ref, fill_ref, row, t, length)
        for k in range(1, length // 128 + 1):

            @pl.when(n == k)
            def _(k=k):
                write_mask(mask_ref, segk_ref, seg_ref, fill, t, lo_b, k)
                tile(t, lo_b, k)


def attend(starts, fill, seg, qkv):
    rows, length, _ = qkv.shape
    blocks = length // 128
    return pl.pallas_call(
        functools.partial(attend_kernel, length=length),
        grid_spec=pltpu.PrefetchScalarGridSpec(
            num_scalar_prefetch=2,
            grid=(rows,),
            in_specs=[
                pl.BlockSpec((1, 1, length), lambda r, *_: (r, 0, 0)),
                pl.BlockSpec((1, length, 1536), lambda r, *_: (r, 0, 0)),
            ],
            out_specs=[
                pl.BlockSpec((1, length, 512), lambda r, *_: (r, 0, 0)),
                pl.BlockSpec((1, 4, blocks, 256), lambda r, *_: (r, 0, 0, 0)),
            ],
            scratch_shapes=[
                pltpu.VMEM((512, length), BF),
                pltpu.VMEM((length, 128), jnp.int32),
                pltpu.VMEM((length, 128), F32),
                pltpu.VMEM((4, length, 256), F32),
                pltpu.VMEM((4, length, 256), BF),
            ],
        ),
        out_shape=[
            jax.ShapeDtypeStruct((rows, length, 512), BF),
            jax.ShapeDtypeStruct((rows, 4, blocks, 256), F32),
        ],
        compiler_params=pltpu.CompilerParams(vmem_limit_bytes=VMEM_LIMIT),
        name="attend",
    )(starts, fill, seg, qkv)


def attend_back_kernel(
    starts_ref,
    fill_ref,
    seg_ref,
    qkv_ref,
    lse_ref,
    ctx_ref,
    do_ref,
    out_ref,
    kt_ref,
    segk_ref,
    mask_ref,
    dk_ref,
    dv_ref,
    p_ref,
    ds_ref,
    *,
    length,
):
    row = pl.program_id(0)
    fill = fill_ref[row]
    spread_segments(seg_ref, segk_ref, length)
    for b in range(length // 128):
        for p in range(4):
            k = qkv_ref[0, b * 128 : (b + 1) * 128, 512 + p * 128 : 512 + (p + 1) * 128]
            kt_ref[p * 128 : (p + 1) * 128, b * 128 : (b + 1) * 128] = k.T
    dk_ref[...] = jnp.zeros_like(dk_ref)
    dv_ref[...] = jnp.zeros_like(dv_ref)

    def tile(t, lo_b, n):
        tq = pl.ds(pl.multiple_of(t * 128, 128), 128)
        win = pl.ds(pl.multiple_of(lo_b * 128, 128), n * 128)
        ready = []
        for p in range(4):
            lanes = slice(p * 128, (p + 1) * 128)
            qbd = split_heads(qkv_ref[0, tq, lanes] * jnp.asarray(0.125, BF))
            do = do_ref[0, tq, lanes]
            prod = (do.astype(F32) * ctx_ref[0, tq, lanes].astype(F32)).T
            delta = jnp.concatenate(
                [jnp.sum(prod[:64], axis=0, keepdims=True), jnp.sum(prod[64:], axis=0, keepdims=True)], axis=1
            )
            ready.append((qbd, split_heads(do), delta, lse_ref[0, p, pl.ds(t, 1), :]))
        for c in range(0, n, CUT):
            w = min(CUT, n - c)
            rows = pl.ds(pl.multiple_of((lo_b + c) * 128, 128), w * 128)
            here = slice(c * 128, (c + w) * 128)
            for p in range(4):
                qbd, dobd, delta, lse = ready[p]
                s = mm(qkv_ref[0, rows, 512 + p * 128 : 512 + (p + 1) * 128], qbd, NT)
                dp = mm(qkv_ref[0, rows, 1024 + p * 128 : 1024 + (p + 1) * 128], dobd, NT)
                mask = mask_ref[here, :]
                e = jnp.exp(s + jnp.concatenate([mask, mask], axis=1) - lse)
                p_ref[p, here, :] = e.astype(BF)
                ds_ref[p, here, :] = (e * (dp - delta)).astype(BF)
            for p in range(4):
                qbd, dobd, _, _ = ready[p]
                lanes = slice(p * 128, (p + 1) * 128)
                dv_ref[rows, lanes] += mm(p_ref[p, here, :], dobd)
                dk_ref[rows, lanes] += mm(ds_ref[p, here, :], qbd)
        for p in range(4):
            lanes = slice(p * 128, (p + 1) * 128)
            dq = mm(kt_ref[lanes, win], ds_ref[p, : n * 128, :])
            out_ref[0, tq, lanes] = (diag_blocks(dq) * 0.125).T.astype(BF)

    @pl.loop(0, length // 128)
    def _(t):
        lo_b, n = window(starts_ref, fill_ref, row, t, length)
        for k in range(1, length // 128 + 1):

            @pl.when(n == k)
            def _(k=k):
                write_mask(mask_ref, segk_ref, seg_ref, fill, t, lo_b, k)
                tile(t, lo_b, k)

    out_ref[0, :, 512:1024] = dk_ref[...].astype(BF)
    out_ref[0, :, 1024:1536] = dv_ref[...].astype(BF)


def attend_back(starts, fill, seg, qkv, lse, ctx, do):
    rows, length, _ = qkv.shape
    blocks = length // 128
    return pl.pallas_call(
        functools.partial(attend_back_kernel, length=length),
        grid_spec=pltpu.PrefetchScalarGridSpec(
            num_scalar_prefetch=2,
            grid=(rows,),
            in_specs=[
                pl.BlockSpec((1, 1, length), lambda r, *_: (r, 0, 0)),
                pl.BlockSpec((1, length, 1536), lambda r, *_: (r, 0, 0)),
                pl.BlockSpec((1, 4, blocks, 256), lambda r, *_: (r, 0, 0, 0)),
                pl.BlockSpec((1, length, 512), lambda r, *_: (r, 0, 0)),
                pl.BlockSpec((1, length, 512), lambda r, *_: (r, 0, 0)),
            ],
            out_specs=pl.BlockSpec((1, length, 1536), lambda r, *_: (r, 0, 0)),
            scratch_shapes=[
                pltpu.VMEM((512, length), BF),
                pltpu.VMEM((length, 128), jnp.int32),
                pltpu.VMEM((length, 128), F32),
                pltpu.VMEM((length, 512), F32),
                pltpu.VMEM((length, 512), F32),
                pltpu.VMEM((4, length, 256), BF),
                pltpu.VMEM((4, length, 256), BF),
            ],
        ),
        out_shape=jax.ShapeDtypeStruct((rows, length, 1536), BF),
        compiler_params=pltpu.CompilerParams(vmem_limit_bytes=VMEM_LIMIT),
        name="attend_back",
    )(starts, fill, seg, qkv, lse, ctx, do)


def gelu_pair(x, grad):
    x2 = x * x
    h = 0.5 + 0.5 * jnp.tanh(x * (C0 + (C0 * C1) * x2))
    act = x * h
    slope = h + act * (1.0 - h) * (2.0 * C0 + (6.0 * C0 * C1) * x2)
    return act.astype(BF), (grad * slope).astype(BF)


def feed_kernel(
    tok_ref,
    ctx_ref,
    cot_ref,
    mix_ref,
    lift_ref,
    drop_ref,
    bias_ref,
    out_ref,
    gmid_ref,
    gctx_ref,
    glift_ref,
    gdrop_ref,
    gmix_ref,
    gbias_ref,
    hid_ref,
    hidt_ref,
    cott_ref,
    acc_ref,
    act_ref,
    gl_ref,
    *,
    tb,
):
    tokens, width = tok_ref.shape
    nf = lift_ref.shape[0]
    nb = tokens // tb
    ones = jnp.ones((16, tb), BF)

    @pl.loop(0, nb)
    def _(b):
        rows = pl.ds(pl.multiple_of(b * tb, tb), tb)
        mid = tok_ref[rows, :].astype(F32) + mm(ctx_ref[rows, :], mix_ref[...]) + bias_ref[5:6, :]
        acc_ref[rows, :] = mid + bias_ref[4:5, :]
        h = mid.astype(BF)
        hid_ref[rows, :] = h
        hidt_ref[0:width, rows] = h.T
        hidt_ref[width : width + 16, rows] = ones
        c = cot_ref[rows, :]
        cott_ref[:, rows] = c.T
        gmid_ref[rows, :] = c.astype(F32)

    def stage1(f, b):
        rows = pl.ds(b * tb, tb)
        for n in range(0, 512, 256):
            x = mm(hid_ref[rows, :], lift_ref[f, :, n : n + 256]) + bias_ref[pl.ds(f, 1), n : n + 256]
            grad = mm(cot_ref[rows, :], drop_ref[f, n : n + 256, :], NT)
            a, g = gelu_pair(x, grad)
            act_ref[b, :, n : n + 256] = a
            gl_ref[b, :, n : n + 256] = g

    def stage2(f, b):
        rows = pl.ds(b * tb, tb)
        act = act_ref[b]
        gl = gl_ref[b]
        acc_ref[rows, :] += mm(act, drop_ref[f])
        gmid_ref[rows, :] += mm(gl, lift_ref[f], NT)
        gd = mm(cott_ref[:, rows], act)
        gf = mm(hidt_ref[:, rows], gl)
        if b == 0:
            gdrop_ref[f] = gd
            glift_ref[f] = gf
        else:
            gdrop_ref[f] += gd
            glift_ref[f] += gf

    @pl.loop(0, nf)
    def _(f):
        stage1(f, 0)
        for b in range(1, nb):
            stage1(f, b)
            stage2(f, b - 1)
        stage2(f, nb - 1)

    gmix_ref[...] = jnp.zeros_like(gmix_ref)
    gbias_ref[...] = jnp.zeros_like(gbias_ref)

    @pl.loop(0, nb)
    def _(b):
        rows = pl.ds(pl.multiple_of(b * tb, tb), tb)
        out_ref[rows, :] = acc_ref[rows, :].astype(BF)
        gb = gmid_ref[rows, :].astype(BF)
        gctx_ref[rows, :] = mm(gb, mix_ref[...], NT).astype(BF)
        gmix_ref[...] += mm(ctx_ref[rows, :].T, gb)
        gbias_ref[5:6, :] += mm(ones, gb)[0:1]
        gbias_ref[4:5, :] += mm(ones, cot_ref[rows, :])[0:1]

    for f in range(nf):
        gbias_ref[f : f + 1, :] = glift_ref[f, width : width + 1, :]


def feed(tok, ctx, cot, mix, lift, drop, bias):
    tokens, width = tok.shape
    nf = lift.shape[0]
    tb = 512
    vmem = pl.BlockSpec(memory_space=pltpu.VMEM)
    return pl.pallas_call(
        functools.partial(feed_kernel, tb=tb),
        in_specs=[vmem] * 7,
        out_specs=[vmem] * 7,
        out_shape=[
            jax.ShapeDtypeStruct((tokens, width), BF),
            jax.ShapeDtypeStruct((tokens, width), F32),
            jax.ShapeDtypeStruct((tokens, width), BF),
            jax.ShapeDtypeStruct((nf, width + 16, 512), F32),
            jax.ShapeDtypeStruct((nf, width, 512), F32),
            jax.ShapeDtypeStruct((width, width), F32),
            jax.ShapeDtypeStruct((8, 512), F32),
        ],
        scratch_shapes=[
            pltpu.VMEM((tokens, width), BF),
            pltpu.VMEM((width + 16, tokens), BF),
            pltpu.VMEM((width, tokens), BF),
            pltpu.VMEM((tokens, width), F32),
            pltpu.VMEM((tokens // tb, tb, 512), BF),
            pltpu.VMEM((tokens // tb, tb, 512), BF),
        ],
        compiler_params=pltpu.CompilerParams(vmem_limit_bytes=VMEM_LIMIT),
        name="feed",
    )(tok, ctx, cot, mix, lift, drop, bias)


MESH = pl.DeviceIdType.MESH


class Place:
    def __init__(self, nz):
        self.nz = nz
        self.z = lax.axis_index("gx")
        g = lax.axis_index("gy")
        self.c = g % 2
        self.x = (g // 2) % 2
        self.y = g // 4
        self.oc = 1 - self.c
        self.y1 = self.y + self.oc * (1 - 2 * self.y)
        self.x1 = self.x + self.c * (1 - 2 * self.x)
        self.y2 = self.y + self.c * (1 - 2 * self.y)
        self.x2 = self.x + self.oc * (1 - 2 * self.x)
        self.core = (self.z, self.y * 4 + self.x * 2 + self.oc)
        self.near1 = (self.z, self.y1 * 4 + self.x1 * 2 + self.c)
        self.near2 = (self.z, self.y2 * 4 + self.x2 * 2 + self.c)

    def at_z(self, z):
        return (z, self.y * 4 + self.x * 2 + self.c)

    def up(self, k):
        return (self.z + k) % self.nz

    def down(self, k):
        return (self.z + self.nz - k) % self.nz

    def greet(self):
        barrier = pltpu.get_barrier_semaphore()
        others = [self.core, self.near1, self.near2] + [self.at_z(self.up(k)) for k in range(1, self.nz)]
        for other in others:
            pl.semaphore_signal(barrier, inc=1, device_id=other, device_id_type=MESH)
        pl.semaphore_wait(barrier, len(others))


def remote(src, dst, send, recv, u, k, device):
    return pltpu.make_async_remote_copy(
        src_ref=src,
        dst_ref=dst,
        send_sem=send.at[u, k],
        recv_sem=recv.at[u, k],
        device_id=device,
        device_id_type=MESH,
    )


class Gather:
    def __init__(self, me, buf, send, recv, u):
        nz = me.nz
        own = buf.at[:, me.y, me.x, me.c]
        other = buf.at[:, me.y1, me.x1, me.c]
        mine = buf.at[me.z, me.y, me.x, me.c]
        half = buf.at[:, :, :, me.c]
        self.along_z = lambda: [remote(mine, mine, send, recv, u, k - 1, me.at_z(me.up(k))) for k in range(1, nz)]
        self.first = lambda: remote(own, own, send, recv, u, nz - 1, me.near1)
        self.second = lambda: remote(own, own, send, recv, u, nz, me.near2)
        self.passed = lambda: remote(other, other, send, recv, u, nz + 1, me.near2)
        self.core = lambda: remote(half, half, send, recv, u, nz + 2, me.core)

    def start(self):
        for copy in self.along_z():
            copy.start()

    def step1(self):
        for copy in self.along_z():
            copy.wait_recv()
        self.first().start()
        self.second().start()

    def step2(self):
        self.first().wait_recv()
        self.passed().start()

    def step3(self):
        self.second().wait_recv()
        self.passed().wait_recv()
        self.core().start()

    def step4(self):
        self.core().wait_recv()

    def finish(self):
        for copy in self.along_z() + [self.first(), self.second(), self.passed(), self.core()]:
            copy.wait_send()


class Reduce:
    def __init__(self, me, bufs, u, send, recv):
        self.me = me
        nz = me.nz
        self.sc, self.rc, self.s1, self.r1, self.s2, self.r2, self.sz, self.rz, self.hold = [b.at[u] for b in bufs]
        self.core = lambda: remote(self.sc, self.rc, send, recv, u, 0, me.core)
        self.first = lambda: remote(self.s1, self.r1, send, recv, u, 1, me.near2)
        self.second = lambda: remote(self.s2, self.r2, send, recv, u, 2, me.near1)
        self.along_z = lambda: [
            remote(self.sz.at[me.up(k)], self.rz.at[me.z], send, recv, u, 2 + k, me.at_z(me.up(k)))
            for k in range(1, nz)
        ]

    def start(self, unit):
        me = self.me
        self.sc[...] = unit[:, :, :, me.oc].astype(BF)
        self.core().start()

    def step1(self, unit):
        me = self.me
        self.core().wait_recv()

        def total(y, x):
            return unit[:, y, x, me.c] + self.rc[:, y, x].astype(F32)

        self.s1[0] = total(me.y2, me.x2).astype(BF)
        self.s1[1] = total(1 - me.y, 1 - me.x).astype(BF)
        self.first().start()
        self.hold[0] = total(me.y, me.x)
        self.hold[1] = total(me.y1, me.x1)

    def step2(self):
        self.first().wait_recv()
        self.s2[...] = (self.hold[1] + self.r1[1].astype(F32)).astype(BF)
        self.second().start()
        self.hold[0] = self.hold[0] + self.r1[0].astype(F32)

    def step3(self):
        self.second().wait_recv()
        total = self.hold[0] + self.r2[...].astype(F32)
        self.sz[...] = total.astype(BF)
        self.hold[0] = total
        for copy in self.along_z():
            copy.start()

    def step4(self):
        me = self.me
        for copy in self.along_z():
            copy.wait_recv()
        total = self.hold[0, me.z]
        for k in range(1, me.nz):
            total = total + self.rz[me.down(k)].astype(F32)
        return total

    def finish(self):
        for copy in [self.core(), self.first(), self.second()] + self.along_z():
            copy.wait_send()


def reduce_bufs(n, nz, w):
    return [
        pltpu.VMEM((n, nz, 2, 2, 16, w), BF),
        pltpu.VMEM((n, nz, 2, 2, 16, w), BF),
        pltpu.VMEM((n, 2, nz, 16, w), BF),
        pltpu.VMEM((n, 2, nz, 16, w), BF),
        pltpu.VMEM((n, nz, 16, w), BF),
        pltpu.VMEM((n, nz, 16, w), BF),
        pltpu.VMEM((n, nz, 16, w), BF),
        pltpu.VMEM((n, nz, 16, w), BF),
        pltpu.VMEM((n, 2, nz, 16, w), F32),
    ]


def sems(n, nz):
    return [pltpu.SemaphoreType.DMA((n, nz + 3)), pltpu.SemaphoreType.DMA((n, nz + 3))]


def first_kernel(nz, tok_ref, own_ref, bias_own_ref, qkv_ref, w_ref, bias_ref, bw_ref, send, recv, bsend, brecv):
    me = Place(nz)
    units = own_ref.shape[0]
    tokens, width = tok_ref.shape
    for u in range(units):
        w_ref[u, me.z, me.y, me.x, me.c] = own_ref[u]
    bw_ref[0, me.z, me.y, me.x, me.c] = bias_own_ref[...]
    me.greet()
    jobs = [Gather(me, bw_ref.at[0], bsend, brecv, 0)] + [Gather(me, w_ref.at[u], send, recv, u) for u in range(units)]
    for job in jobs:
        job.start()
    n = len(jobs)
    for s in range(n + 3):
        if s < n:
            jobs[s].step1()
        if 0 <= s - 1 < n:
            jobs[s - 1].step2()
        if 0 <= s - 2 < n:
            jobs[s - 2].step3()
        if 0 <= s - 3 < n:
            jobs[s - 3].step4()
            u = s - 4
            if u < 0:
                bias_ref[...] = bw_ref[0].reshape(512, 128).astype(F32).T[:8]
            elif u < 3:

                @pl.loop(0, tokens // 512)
                def _(b, u=u):
                    rows = pl.ds(pl.multiple_of(b * 512, 512), 512)
                    y = mm(tok_ref[rows, :], w_ref[u].reshape(512, 512))
                    if u == 0:
                        y = y + bias_ref[6:7, :]
                    if u == 2:
                        y = y + bias_ref[7:8, :]
                    qkv_ref[rows, u * 512 : (u + 1) * 512] = y.astype(BF)

    for job in jobs:
        job.finish()


def first(nz, tok, own, bias_own):
    units = own.shape[0]
    tokens = tok.shape[0]
    vmem = pl.BlockSpec(memory_space=pltpu.VMEM)
    return pl.pallas_call(
        functools.partial(first_kernel, nz),
        in_specs=[vmem] * 3,
        out_specs=[vmem] * 3,
        out_shape=[
            jax.ShapeDtypeStruct((tokens, 1536), BF),
            jax.ShapeDtypeStruct((units, nz, 2, 2, 2, 16, 512), BF),
            jax.ShapeDtypeStruct((8, 512), F32),
        ],
        scratch_shapes=[pltpu.VMEM((1, nz, 2, 2, 2, 16, 128), BF)] + sems(units, nz) + sems(1, nz),
        compiler_params=pltpu.CompilerParams(vmem_limit_bytes=VMEM_LIMIT, collective_id=1, has_side_effects=True),
        name="gather_joint",
    )(tok, own, bias_own)


def middle_kernel(
    nz,
    tb,
    tok_ref,
    ctx_ref,
    cot_ref,
    mix_ref,
    early_ref,
    own_ref,
    bias_ref,
    out_ref,
    gmid_ref,
    gctx_ref,
    gmix_ref,
    gbias_ref,
    grad_ref,
    w_ref,
    hid_ref,
    hidt_ref,
    cott_ref,
    acc_ref,
    act_ref,
    gl_ref,
    gdt_ref,
    sum_ref,
    early_sem,
    gsend,
    grecv,
    rsend,
    rrecv,
    *bufs,
):
    me = Place(nz)
    tokens, width = tok_ref.shape
    nf = w_ref.shape[0] // 2
    nb = tokens // tb
    early = early_ref.shape[0]
    load = pltpu.make_async_copy(early_ref, w_ref.at[0:early], early_sem)
    load.start()
    ones = jnp.ones((16, tb), BF)

    def gathers(f):
        return [Gather(me, w_ref.at[2 * f + i], gsend, grecv, 2 * f + i) for i in range(2)]

    def reduces(f):
        return [Reduce(me, bufs, 2 * f + i, rsend, rrecv) for i in range(2)]

    for u in range(early, 2 * nf):
        w_ref[u, me.z, me.y, me.x, me.c] = own_ref[u - early]
    me.greet()
    for f in range(early // 2, nf):
        for job in gathers(f):
            job.start()

    @pl.loop(0, nb)
    def _(b):
        rows = pl.ds(pl.multiple_of(b * tb, tb), tb)
        mid = tok_ref[rows, :].astype(F32) + mm(ctx_ref[rows, :], mix_ref[...]) + bias_ref[5:6, :]
        acc_ref[rows, :] = mid + bias_ref[4:5, :]
        h = mid.astype(BF)
        hid_ref[rows, :] = h
        hidt_ref[0:width, rows] = h.T
        hidt_ref[width : width + 16, rows] = ones
        c = cot_ref[rows, :]
        cott_ref[:, rows] = c.T
        gmid_ref[rows, :] = c.astype(F32)

    gbias_ref[...] = jnp.zeros_like(gbias_ref)
    load.wait()

    def lift(f):
        return w_ref.at[2 * f]

    def drop(f):
        return w_ref.at[2 * f + 1]

    def stage1(f, b):
        rows = pl.ds(b * tb, tb)
        lw = w_ref[2 * f].reshape(512, 512)
        dw = w_ref[2 * f + 1].reshape(512, 512)
        for n in range(0, 512, 256):
            x = mm(hid_ref[rows, :], lw[:, n : n + 256]) + bias_ref[pl.ds(f, 1), n : n + 256]
            grad = mm(cot_ref[rows, :], dw[n : n + 256, :], NT)
            a, g = gelu_pair(x, grad)
            act_ref[b, :, n : n + 256] = a
            gl_ref[b, :, n : n + 256] = g

    def stage2(f, b):
        slot = f % 2
        rows = pl.ds(b * tb, tb)
        act = act_ref[b]
        gl = gl_ref[b]
        acc_ref[rows, :] += mm(act, w_ref[2 * f + 1].reshape(512, 512))
        gmid_ref[rows, :] += mm(gl, w_ref[2 * f].reshape(512, 512), NT)
        gd = mm(cott_ref[:, rows], act)
        gf = mm(hidt_ref[:, rows], gl)
        unit = gf[:width].reshape(nz, 2, 2, 2, 16, 512)
        if b == 0:
            gdt_ref[...] = gd
            sum_ref[slot, 0] = unit
        elif b < nb - 1:
            gdt_ref[...] += gd
            sum_ref[slot, 0] += unit
        else:
            sum_ref[slot, 1] = (gdt_ref[...] + gd).T.reshape(nz, 2, 2, 2, 16, 512)
            sum_ref[slot, 0] += unit
        gbias_ref[pl.ds(f, 1), :] += gf[width : width + 1]

    def reduce_step(f, k):
        slot = f % 2
        for i, job in enumerate(reduces(f)):
            if k == 0:
                job.start(sum_ref.at[slot, i])
            elif k == 1:
                job.step1(sum_ref.at[slot, i])
            elif k == 2:
                job.step2()
            elif k == 3:
                job.step3()
            else:
                grad_ref[2 * f + i] = job.step4()

    def gather_step(f, k):
        for job in gathers(f):
            (job.step1, job.step2, job.step3, job.step4)[k]()

    @pl.loop(0, nf)
    def _(f):
        for k in range(nb):

            @pl.when(f > 0)
            def _(k=k):
                if k == 0:
                    gather_step(f, 3)
                reduce_step(f - 1, k)

            @pl.when(f + 1 < nf)
            def _(k=k):
                if k < 3:
                    gather_step(f + 1, k)

            if k == 0:

                @pl.when(f > 1)
                def _():
                    reduce_step(f - 2, 4)

            stage1(f, k)
            if k > 0:
                stage2(f, k - 1)
        stage2(f, nb - 1)

    gmix_ref[...] = jnp.zeros_like(gmix_ref)
    for b in range(nb):
        if b == 0:
            reduce_step(nf - 2, 4)
        reduce_step(nf - 1, b)
        rows = pl.ds(b * tb, tb)
        out_ref[rows, :] = acc_ref[rows, :].astype(BF)
        gb = gmid_ref[rows, :].astype(BF)
        gctx_ref[rows, :] = mm(gb, mix_ref[...], NT).astype(BF)
        gmix_ref[...] += mm(ctx_ref[rows, :].T, gb)
        gbias_ref[5:6, :] += mm(ones, gb)[0:1]
        gbias_ref[4:5, :] += mm(ones, cot_ref[rows, :])[0:1]
    reduce_step(nf - 1, 4)
    for f in range(nf):
        if f >= early // 2:
            for job in gathers(f):
                job.finish()
        for job in reduces(f):
            job.finish()


def middle(nz, tok, ctx, cot, mix, early, own, bias):
    tokens, width = tok.shape
    n = early.shape[0] + own.shape[0]
    tb = tokens // 4
    vmem = pl.BlockSpec(memory_space=pltpu.VMEM)
    return pl.pallas_call(
        functools.partial(middle_kernel, nz, tb),
        in_specs=[vmem] * 4 + [pl.BlockSpec(memory_space=pl.ANY)] + [vmem] * 2,
        out_specs=[vmem] * 6,
        out_shape=[
            jax.ShapeDtypeStruct((tokens, width), BF),
            jax.ShapeDtypeStruct((tokens, width), F32),
            jax.ShapeDtypeStruct((tokens, width), BF),
            jax.ShapeDtypeStruct((width, width), F32),
            jax.ShapeDtypeStruct((8, 512), F32),
            jax.ShapeDtypeStruct((n, 16, 512), F32),
        ],
        scratch_shapes=[
            pltpu.VMEM((n, nz, 2, 2, 2, 16, 512), BF),
            pltpu.VMEM((tokens, width), BF),
            pltpu.VMEM((width + 16, tokens), BF),
            pltpu.VMEM((width, tokens), BF),
            pltpu.VMEM((tokens, width), F32),
            pltpu.VMEM((4, tb, 512), BF),
            pltpu.VMEM((4, tb, 512), BF),
            pltpu.VMEM((width, 512), F32),
            pltpu.VMEM((2, 2, nz, 2, 2, 2, 16, 512), F32),
            pltpu.SemaphoreType.DMA,
        ]
        + sems(n, nz)
        + sems(n, nz)
        + reduce_bufs(n, nz, 512),
        compiler_params=pltpu.CompilerParams(vmem_limit_bytes=VMEM_LIMIT, collective_id=2, has_side_effects=True),
        name="feed",
    )(tok, ctx, cot, mix, early, own, bias)


def last_kernel(
    nz,
    tok_ref,
    gj_ref,
    gmid_ref,
    jw_ref,
    gmix_ref,
    gbias_ref,
    tg_ref,
    own_ref,
    obias_ref,
    tokt_ref,
    sum_ref,
    bsum_ref,
    brow_ref,
    send,
    recv,
    bsend,
    brecv,
    *bufs,
):
    me = Place(nz)
    tokens, width = tok_ref.shape
    me.greet()
    jobs = [Reduce(me, bufs[:9], u, send, recv) for u in range(4)] + [Reduce(me, bufs[9:], 0, bsend, brecv)]
    units = [gmix_ref] + [sum_ref.at[j] for j in range(3)] + [bsum_ref]
    n = 5
    jobs[0].start(units[0])

    @pl.loop(0, tokens // 512)
    def _(b):
        rows = pl.ds(pl.multiple_of(b * 512, 512), 512)
        tokt_ref[0:width, rows] = tok_ref[rows, :].T
        tokt_ref[width : width + 16, rows] = jnp.ones((16, 512), BF)

    def token_block(b):
        rows = pl.ds(pl.multiple_of(b * 512, 512), 512)
        total = gmid_ref[rows, :]
        for j in range(3):
            total = total + mm(gj_ref[rows, j * 512 : (j + 1) * 512], jw_ref[j], NT)
        tg_ref[rows, :] = total

    brow_ref[...] = jnp.zeros_like(brow_ref)
    brow_ref[0:8, :] = gbias_ref[...]
    done = 0
    for s in range(n + 4):
        if 0 <= s - 4 < n:
            u = s - 4
            total = jobs[u].step4()
            if u < 4:
                own_ref[u] = total
            else:
                obias_ref[...] = total
        if 0 <= s - 3 < n:
            jobs[s - 3].step3()
        if 0 <= s - 2 < n:
            jobs[s - 2].step2()
        if 0 <= s - 1 < n:
            jobs[s - 1].step1(units[s - 1])
        if s < 3:
            g = mm(tokt_ref[...], gj_ref[:, s * 512 : (s + 1) * 512])
            sum_ref[s] = g[:width].reshape(nz, 2, 2, 2, 16, 512)
            if s != 1:
                brow_ref[6 + s // 2 : 7 + s // 2, :] = g[width : width + 1]
            jobs[s + 1].start(units[s + 1])
        elif s == 3:
            bsum_ref[...] = brow_ref[...].T.reshape(nz, 2, 2, 2, 16, 128)
            jobs[4].start(units[4])
        if s >= 3 and done < tokens // 512:
            token_block(done)
            done += 1
    while done < tokens // 512:
        token_block(done)
        done += 1
    for job in jobs:
        job.finish()


def last(nz, tok, gj, gmid, jw, gmix, gbias):
    tokens, width = tok.shape
    vmem = pl.BlockSpec(memory_space=pltpu.VMEM)
    return pl.pallas_call(
        functools.partial(last_kernel, nz),
        in_specs=[vmem] * 6,
        out_specs=[vmem] * 3,
        out_shape=[
            jax.ShapeDtypeStruct((tokens, width), F32),
            jax.ShapeDtypeStruct((4, 16, 512), F32),
            jax.ShapeDtypeStruct((16, 128), F32),
        ],
        scratch_shapes=[
            pltpu.VMEM((width + 16, tokens), BF),
            pltpu.VMEM((3, nz, 2, 2, 2, 16, 512), F32),
            pltpu.VMEM((nz, 2, 2, 2, 16, 128), F32),
            pltpu.VMEM((128, 512), F32),
        ]
        + sems(4, nz)
        + sems(1, nz)
        + reduce_bufs(4, nz, 512)
        + reduce_bufs(1, nz, 128),
        compiler_params=pltpu.CompilerParams(vmem_limit_bytes=VMEM_LIMIT, collective_id=3, has_side_effects=True),
        name="joint_grads",
    )(tok, gj, gmid, jw, gmix.reshape(nz, 2, 2, 2, 16, 512), gbias)


EARLY = 2


def remote_body(
    tokens,
    segment_ids,
    fill_lengths,
    joint_weight,
    joint_bias,
    mix_weight,
    mix_bias,
    lift_weight,
    lift_bias,
    drop_weight,
    drop_bias,
    cotangent,
):
    rows, length, width = tokens.shape
    nz = lax.axis_size("gx")
    n_tok = rows * length
    tok = tokens.reshape(n_tok, width)
    cot = cotangent.reshape(n_tok, width)
    seg = segment_ids.reshape(rows, 1, length)
    starts = jnp.sum(
        segment_ids[:, None, :] < jnp.arange(8, dtype=jnp.int32)[None, :, None], axis=-1, dtype=jnp.int32
    )
    nf = drop_weight.shape[0] // 16
    lift_own = lift_weight.reshape(16, -1, nf, 16).transpose(2, 0, 1, 3).reshape(nf, 16, 512)
    drop_own = drop_weight.reshape(nf, 16, 512)
    joint_own = joint_weight.reshape(16, 3, 512).transpose(1, 0, 2)
    feed_own = jnp.stack([lift_own, drop_own], axis=1).reshape(2 * nf, 16, 512)
    first_own = jnp.concatenate([joint_own, mix_weight[None], feed_own[:EARLY]])
    bias_own = jnp.concatenate([lift_bias.reshape(nf, 16), drop_bias[None], mix_bias[None], joint_bias])
    bias_own = jnp.pad(bias_own, ((0, 120), (0, 0))).T

    qkv, weights, bias = first(nz, tok, first_own, bias_own)
    qkv3 = qkv.reshape(rows, length, 3 * width)
    ctx, lse = attend(starts, fill_lengths, seg, qkv3)
    out, gmid, gctx, gmix, gbias, feed_grads = middle(
        nz, tok, ctx.reshape(n_tok, width), cot, weights[3].reshape(width, width), weights[4:], feed_own[EARLY:], bias
    )
    gjoint = attend_back(
        starts, fill_lengths, seg, qkv3, lse, ctx, gctx.reshape(rows, length, width)
    ).reshape(n_tok, 3 * width)
    token_grad, grads, gb = last(nz, tok, gjoint, gmid, weights[:3].reshape(3, width, width), gmix, gbias)
    feed_grads = feed_grads.reshape(nf, 2, 16, 512)
    glift = feed_grads[:, 0].reshape(nf, 16, -1, 16).transpose(1, 2, 0, 3).reshape(16, nf * 512)
    gdrop = feed_grads[:, 1].reshape(nf * 16, 512)
    gb = gb[:, :8].T
    return (
        out.reshape(rows, length, width),
        token_grad.reshape(rows, length, width),
        grads[1:4].transpose(1, 0, 2).reshape(16, 3 * width),
        gb[6:8],
        grads[0],
        gb[5],
        glift,
        gb[:nf].reshape(-1),
        gdrop,
        gb[4],
    )


BOTH = ("gx", "gy")


def body(
    tokens,
    segment_ids,
    fill_lengths,
    joint_weight,
    joint_bias,
    mix_weight,
    mix_bias,
    lift_weight,
    lift_bias,
    drop_weight,
    drop_bias,
    cotangent,
):
    rows, length, width = tokens.shape
    n_tok = rows * length
    tok = tokens.reshape(n_tok, width)
    cot = cotangent.reshape(n_tok, width)
    seg = segment_ids.reshape(rows, 1, length)
    starts = jnp.sum(
        segment_ids[:, None, :] < jnp.arange(8, dtype=jnp.int32)[None, :, None], axis=-1, dtype=jnp.int32
    )

    joint_w = lax.all_gather(joint_weight, BOTH, axis=0, tiled=True)
    mix_w = lax.all_gather(mix_weight, BOTH, axis=0, tiled=True)
    lift_w = lax.all_gather(lift_weight, BOTH, axis=0, tiled=True)
    drop_w = lax.all_gather(drop_weight, BOTH, axis=0, tiled=True)
    own_bias = jnp.concatenate([joint_bias.reshape(-1), mix_bias, lift_bias, drop_bias])
    sizes = [joint_bias.shape[1], joint_bias.shape[1], mix_bias.size, lift_bias.size, drop_bias.size]
    all_bias = lax.all_gather(own_bias, BOTH, axis=0)
    parts, at = [], 0
    for size in sizes:
        parts.append(all_bias[:, at : at + size].reshape(-1).astype(F32))
        at += size
    bq, bv, bm, bl, bd = parts
    nf = bl.size // 512
    bias = jnp.concatenate(
        [jnp.concatenate([bl.reshape(nf, 512), jnp.zeros((4 - nf, 512), F32)]), bd[None], bm[None], bq[None], bv[None]]
    )

    shift = jnp.concatenate([bq, jnp.zeros_like(bq), bv])
    qkv = (mm(tok, joint_w) + shift).astype(BF)
    qkv3 = qkv.reshape(rows, length, 3 * width)
    ctx, lse = attend(starts, fill_lengths, seg, qkv3)
    lift_units = lift_w.reshape(width, nf, 512).transpose(1, 0, 2)
    out, gmid, gctx, glift, gdrop, gmix, gbias = feed(
        tok, ctx.reshape(n_tok, width), cot, mix_w, lift_units, drop_w.reshape(nf, 512, width), bias
    )
    gjoint = attend_back(
        starts, fill_lengths, seg, qkv3, lse, ctx, gctx.reshape(rows, length, width)
    ).reshape(n_tok, 3 * width)
    gjoint_w = lax.dot_general(tok, gjoint, (((0,), (0,)), ((), ())), preferred_element_type=F32)
    sums = jnp.sum(gjoint.astype(F32), axis=0)
    token_grad = gmid + mm(gjoint, joint_w, NT)

    glift_w = glift[:, :width].transpose(1, 0, 2).reshape(width, nf * 512)
    gdrop_w = gdrop.transpose(0, 2, 1).reshape(nf * 512, width)
    scatter = functools.partial(lax.psum_scatter, axis_name=BOTH, scatter_dimension=0, tiled=True)
    n_dev = all_bias.shape[0]
    packed = jnp.concatenate(
        [
            g.reshape(n_dev, -1)
            for g in (sums[:width], sums[2 * width :], gbias[5], gbias[:nf].reshape(-1), gbias[4])
        ],
        axis=1,
    )
    own = scatter(packed)[0]
    cuts, at = [], 0
    for size in sizes:
        cuts.append(own[at : at + size])
        at += size
    return (
        out.reshape(rows, length, width),
        token_grad.reshape(rows, length, width),
        scatter(gjoint_w),
        jnp.stack([cuts[0], cuts[1]]),
        scatter(gmix),
        cuts[2],
        scatter(glift_w),
        cuts[3],
        scatter(gdrop_w),
        cuts[4],
    )


def solution(mesh):
    wide = P(BOTH, None, None)
    rows = P(BOTH, None)
    flat = P(BOTH)
    bias = P(None, BOTH)
    in_specs = (wide, rows, flat, rows, bias, rows, flat, rows, flat, rows, flat, wide)
    out_specs = (wide, wide, rows, bias, rows, flat, rows, flat, rows, flat)
    fits = mesh.shape["gy"] == 8 and mesh.shape["gx"] == 4
    return jax.shard_map(remote_body if fits else body, mesh=mesh, in_specs=in_specs, out_specs=out_specs, check_vma=False)
```

```python
import functools
import math

import jax
import jax.numpy as jnp
from jax import lax
from jax.experimental import pallas as pl
from jax.experimental.pallas import tpu as pltpu
from jax.sharding import PartitionSpec as P

BF = jnp.bfloat16
F32 = jnp.float32
NT = (((1,), (1,)), ((), ()))
NN = (((1,), (0,)), ((), ()))
NEG = -float(2**30)
C0 = math.sqrt(2.0 / math.pi)
C1 = 0.044715
CUT = 2
VMEM_LIMIT = 60 * 2**20


def mm(a, b, dims=NN):
    return lax.dot_general(a, b, dims, preferred_element_type=F32)


def split_heads(x):
    lane = lax.broadcasted_iota(jnp.int32, x.shape, 1)
    zero = jnp.zeros_like(x)
    return jnp.concatenate([jnp.where(lane < 64, x, zero), jnp.where(lane < 64, zero, x)], axis=0)


def diag_blocks(y):
    return jnp.concatenate([y[:64, :128], y[64:, 128:]], axis=0)


def window(starts_ref, fill_ref, row, t, length):
    first = t * 128
    last = first + 127
    fill = fill_ref[row]
    lo = jnp.int32(0)
    hi = jnp.int32(length)
    for v in range(1, 6):
        s = starts_ref[row, v]
        lo = jnp.where(s <= first, jnp.maximum(lo, s), lo)
        hi = jnp.where(s > last, jnp.minimum(hi, s), hi)
    hi = jnp.minimum(hi, fill)
    alone = lo >= fill
    hi = jnp.where(last >= fill, jnp.maximum(hi, last + 1), hi)
    lo = jnp.where(alone, first, lo)
    lo_b = lo // 128
    return lo_b, (hi + 127) // 128 - lo_b


def ids_of(seg_ref, row, lanes):
    ids = seg_ref[:, lanes]
    mine = lax.broadcasted_iota(jnp.int32, ids.shape, 0) == row
    return jnp.sum(jnp.where(mine, ids.astype(F32), 0.0), axis=0, keepdims=True)


def write_mask(mask_ref, segk_ref, seg_ref, row, fill, t, lo_b, n):
    segq = ids_of(seg_ref, row, pl.ds(pl.multiple_of(t * 128, 128), 128))
    segq = jnp.broadcast_to(segq, (128, 128))
    qi = t * 128 + lax.broadcasted_iota(jnp.int32, (128, 128), 1)
    ki0 = lax.broadcasted_iota(jnp.int32, (128, 128), 0)
    for c in range(n):
        off = pl.multiple_of((lo_b + c) * 128, 128)
        ki = ki0 + off
        ok = ((segk_ref[pl.ds(off, 128), :] == segq) & (ki < fill)) | (ki == qi)
        mask_ref[c * 128 : (c + 1) * 128, :] = jnp.where(ok, 0.0, NEG)


def spread_segments(seg_ref, segk_ref, row, length):
    for b in range(length // 128):
        ids = ids_of(seg_ref, row, slice(b * 128, (b + 1) * 128))
        segk_ref[b * 128 : (b + 1) * 128, :] = jnp.broadcast_to(ids, (128, 128)).T


def attend_kernel(
    starts_ref, fill_ref, seg_ref, qkv_ref, ctx_ref, lse_ref, vt_ref, segk_ref, mask_ref, s_ref, p_ref, *, length
):
    row = pl.program_id(0)
    fill = fill_ref[row]
    spread_segments(seg_ref, segk_ref, row, length)
    for b in range(length // 128):
        for p in range(4):
            v = qkv_ref[0, b * 128 : (b + 1) * 128, 1024 + p * 128 : 1024 + (p + 1) * 128]
            vt_ref[p * 128 : (p + 1) * 128, b * 128 : (b + 1) * 128] = v.T

    def tile(t, lo_b, n):
        tq = pl.ds(pl.multiple_of(t * 128, 128), 128)
        win = pl.ds(pl.multiple_of(lo_b * 128, 128), n * 128)
        cuts = [(c, min(CUT, n - c)) for c in range(0, n, CUT)]
        tops, sums = [], []
        for p in range(4):
            lanes = slice(p * 128, (p + 1) * 128)
            qbd = split_heads(qkv_ref[0, tq, lanes] * jnp.asarray(0.125, BF))
            top = None
            for c, w in cuts:
                rows = pl.ds(pl.multiple_of((lo_b + c) * 128, 128), w * 128)
                s = mm(qkv_ref[0, rows, 512 + p * 128 : 512 + (p + 1) * 128], qbd, NT)
                mask = mask_ref[c * 128 : (c + w) * 128, :]
                s = s + jnp.concatenate([mask, mask], axis=1)
                s_ref[p, c * 128 : (c + w) * 128, :] = s
                part = jnp.max(s.reshape(w * 16, 8, 256), axis=0)
                top = part if top is None else jnp.maximum(top, part)
            tops.append(jnp.max(top, axis=0, keepdims=True))
        for p in range(4):
            total = None
            for c, w in cuts:
                e = jnp.exp(s_ref[p, c * 128 : (c + w) * 128, :] - tops[p])
                p_ref[p, c * 128 : (c + w) * 128, :] = e.astype(BF)
                part = jnp.sum(e.reshape(w * 16, 8, 256), axis=0)
                total = part if total is None else total + part
            sums.append(jnp.sum(total, axis=0, keepdims=True))
        for p in range(4):
            o = mm(vt_ref[p * 128 : (p + 1) * 128, win], p_ref[p, : n * 128, :]) * (1.0 / sums[p])
            ctx_ref[0, tq, p * 128 : (p + 1) * 128] = diag_blocks(o).T.astype(BF)
            lse_ref[0, p, pl.ds(t, 1), :] = tops[p] + jnp.log(sums[p])

    @pl.loop(0, length // 128)
    def _(t):
        lo_b, n = window(starts_ref, fill_ref, row, t, length)
        for k in range(1, length // 128 + 1):

            @pl.when(n == k)
            def _(k=k):
                write_mask(mask_ref, segk_ref, seg_ref, row, fill, t, lo_b, k)
                tile(t, lo_b, k)


def attend(starts, fill, seg, qkv):
    rows, length, _ = qkv.shape
    blocks = length // 128
    return pl.pallas_call(
        functools.partial(attend_kernel, length=length),
        grid_spec=pltpu.PrefetchScalarGridSpec(
            num_scalar_prefetch=2,
            grid=(rows,),
            in_specs=[
                pl.BlockSpec((rows, length), lambda r, *_: (0, 0)),
                pl.BlockSpec((1, length, 1536), lambda r, *_: (r, 0, 0)),
            ],
            out_specs=[
                pl.BlockSpec((1, length, 512), lambda r, *_: (r, 0, 0)),
                pl.BlockSpec((1, 4, blocks, 256), lambda r, *_: (r, 0, 0, 0)),
            ],
            scratch_shapes=[
                pltpu.VMEM((512, length), BF),
                pltpu.VMEM((length, 128), F32),
                pltpu.VMEM((length, 128), F32),
                pltpu.VMEM((4, length, 256), F32),
                pltpu.VMEM((4, length, 256), BF),
            ],
        ),
        out_shape=[
            jax.ShapeDtypeStruct((rows, length, 512), BF),
            jax.ShapeDtypeStruct((rows, 4, blocks, 256), F32),
        ],
        compiler_params=pltpu.CompilerParams(vmem_limit_bytes=VMEM_LIMIT),
        name="attend",
    )(starts, fill, seg, qkv)


def attend_back_kernel(
    starts_ref,
    fill_ref,
    seg_ref,
    qkv_ref,
    lse_ref,
    ctx_ref,
    do_ref,
    gmid_ref,
    jw_ref,
    pass_ref,
    out_ref,
    tg_ref,
    to_ref,
    kt_ref,
    segk_ref,
    mask_ref,
    dk_ref,
    dv_ref,
    p_ref,
    ds_ref,
    *,
    length,
):
    row = pl.program_id(0)
    fill = fill_ref[row]
    to_ref[...] = pass_ref[...]
    spread_segments(seg_ref, segk_ref, row, length)
    for b in range(length // 128):
        for p in range(4):
            k = qkv_ref[0, b * 128 : (b + 1) * 128, 512 + p * 128 : 512 + (p + 1) * 128]
            kt_ref[p * 128 : (p + 1) * 128, b * 128 : (b + 1) * 128] = k.T
    dk_ref[...] = jnp.zeros_like(dk_ref)
    dv_ref[...] = jnp.zeros_like(dv_ref)

    def tile(t, lo_b, n):
        tq = pl.ds(pl.multiple_of(t * 128, 128), 128)
        win = pl.ds(pl.multiple_of(lo_b * 128, 128), n * 128)
        ready = []
        for p in range(4):
            lanes = slice(p * 128, (p + 1) * 128)
            qbd = split_heads(qkv_ref[0, tq, lanes] * jnp.asarray(0.125, BF))
            do = do_ref[0, tq, lanes]
            prod = (do.astype(F32) * ctx_ref[0, tq, lanes].astype(F32)).T
            delta = jnp.concatenate(
                [jnp.sum(prod[:64], axis=0, keepdims=True), jnp.sum(prod[64:], axis=0, keepdims=True)], axis=1
            )
            ready.append((qbd, split_heads(do), delta, lse_ref[0, p, pl.ds(t, 1), :]))
        for c in range(0, n, CUT):
            w = min(CUT, n - c)
            rows = pl.ds(pl.multiple_of((lo_b + c) * 128, 128), w * 128)
            here = slice(c * 128, (c + w) * 128)
            for p in range(4):
                qbd, dobd, delta, lse = ready[p]
                s = mm(qkv_ref[0, rows, 512 + p * 128 : 512 + (p + 1) * 128], qbd, NT)
                dp = mm(qkv_ref[0, rows, 1024 + p * 128 : 1024 + (p + 1) * 128], dobd, NT)
                mask = mask_ref[here, :]
                e = jnp.exp(s + jnp.concatenate([mask, mask], axis=1) - lse)
                p_ref[p, here, :] = e.astype(BF)
                ds_ref[p, here, :] = (e * (dp - delta)).astype(BF)
            for p in range(4):
                qbd, dobd, _, _ = ready[p]
                lanes = slice(p * 128, (p + 1) * 128)
                dv_ref[rows, lanes] += mm(p_ref[p, here, :], dobd)
                dk_ref[rows, lanes] += mm(ds_ref[p, here, :], qbd)
        for p in range(4):
            lanes = slice(p * 128, (p + 1) * 128)
            dq = mm(kt_ref[lanes, win], ds_ref[p, : n * 128, :])
            out_ref[0, tq, lanes] = (diag_blocks(dq) * 0.125).T.astype(BF)

    @pl.loop(0, length // 128)
    def _(t):
        lo_b, n = window(starts_ref, fill_ref, row, t, length)
        for k in range(1, length // 128 + 1):

            @pl.when(n == k)
            def _(k=k):
                write_mask(mask_ref, segk_ref, seg_ref, row, fill, t, lo_b, k)
                tile(t, lo_b, k)

    for b in range(0, length, 256):
        rows = slice(b, b + 256)
        dk = dk_ref[rows, :].astype(BF)
        dv = dv_ref[rows, :].astype(BF)
        out_ref[0, rows, 512:1024] = dk
        out_ref[0, rows, 1024:1536] = dv
        total = gmid_ref[0, rows, :] + mm(out_ref[0, rows, 0:512], jw_ref[0], NT)
        tg_ref[0, rows, :] = total + mm(dk, jw_ref[1], NT) + mm(dv, jw_ref[2], NT)


def attend_back(starts, fill, seg, qkv, lse, ctx, do, gmid, joint, passed):
    rows, length, _ = qkv.shape
    blocks = length // 128
    wide = pl.BlockSpec((1, length, 512), lambda r, *_: (r, 0, 0))
    joined = pl.BlockSpec((1, length, 1536), lambda r, *_: (r, 0, 0))
    return pl.pallas_call(
        functools.partial(attend_back_kernel, length=length),
        grid_spec=pltpu.PrefetchScalarGridSpec(
            num_scalar_prefetch=2,
            grid=(rows,),
            in_specs=[
                pl.BlockSpec((rows, length), lambda r, *_: (0, 0)),
                joined,
                pl.BlockSpec((1, 4, blocks, 256), lambda r, *_: (r, 0, 0, 0)),
                wide,
                wide,
                wide,
                pl.BlockSpec((3, 512, 512), lambda r, *_: (0, 0, 0)),
                wide,
            ],
            out_specs=[joined, wide, wide],
            scratch_shapes=[
                pltpu.VMEM((512, length), BF),
                pltpu.VMEM((length, 128), F32),
                pltpu.VMEM((length, 128), F32),
                pltpu.VMEM((length, 512), F32),
                pltpu.VMEM((length, 512), F32),
                pltpu.VMEM((4, length, 256), BF),
                pltpu.VMEM((4, length, 256), BF),
            ],
        ),
        out_shape=[
            jax.ShapeDtypeStruct((rows, length, 1536), BF),
            jax.ShapeDtypeStruct((rows, length, 512), F32),
            jax.ShapeDtypeStruct(passed.shape, passed.dtype),
        ],
        compiler_params=pltpu.CompilerParams(vmem_limit_bytes=VMEM_LIMIT),
        name="attend_back",
    )(starts, fill, seg, qkv, lse, ctx, do, gmid, joint, passed)


def gelu_pair(x, grad):
    x2 = x * x
    h = 0.5 + 0.5 * jnp.tanh(x * (C0 + (C0 * C1) * x2))
    act = x * h
    slope = h + act * (1.0 - h) * (2.0 * C0 + (6.0 * C0 * C1) * x2)
    return act.astype(BF), (grad * slope).astype(BF)


def feed_kernel(
    tok_ref,
    ctx_ref,
    cot_ref,
    mix_ref,
    lift_ref,
    drop_ref,
    bias_ref,
    out_ref,
    gmid_ref,
    gctx_ref,
    glift_ref,
    gdrop_ref,
    gmix_ref,
    gbias_ref,
    hid_ref,
    hidt_ref,
    cott_ref,
    acc_ref,
    act_ref,
    gl_ref,
    *,
    tb,
):
    tokens, width = tok_ref.shape
    nf = lift_ref.shape[0]
    nb = tokens // tb
    ones = jnp.ones((16, tb), BF)

    @pl.loop(0, nb)
    def _(b):
        rows = pl.ds(pl.multiple_of(b * tb, tb), tb)
        mid = tok_ref[rows, :].astype(F32) + mm(ctx_ref[rows, :], mix_ref[...]) + bias_ref[5:6, :]
        acc_ref[rows, :] = mid + bias_ref[4:5, :]
        h = mid.astype(BF)
        hid_ref[rows, :] = h
        hidt_ref[0:width, rows] = h.T
        hidt_ref[width : width + 16, rows] = ones
        c = cot_ref[rows, :]
        cott_ref[:, rows] = c.T
        gmid_ref[rows, :] = c.astype(F32)

    def stage1(f, b):
        rows = pl.ds(b * tb, tb)
        for n in range(0, 512, 256):
            x = mm(hid_ref[rows, :], lift_ref[f, :, n : n + 256]) + bias_ref[pl.ds(f, 1), n : n + 256]
            grad = mm(cot_ref[rows, :], drop_ref[f, n : n + 256, :], NT)
            a, g = gelu_pair(x, grad)
            act_ref[b, :, n : n + 256] = a
            gl_ref[b, :, n : n + 256] = g

    def stage2(f, b):
        rows = pl.ds(b * tb, tb)
        act = act_ref[b]
        gl = gl_ref[b]
        acc_ref[rows, :] += mm(act, drop_ref[f])
        gmid_ref[rows, :] += mm(gl, lift_ref[f], NT)
        gd = mm(cott_ref[:, rows], act)
        gf = mm(hidt_ref[:, rows], gl)
        if b == 0:
            gdrop_ref[f] = gd
            glift_ref[f] = gf
        else:
            gdrop_ref[f] += gd
            glift_ref[f] += gf

    @pl.loop(0, nf)
    def _(f):
        stage1(f, 0)
        for b in range(1, nb):
            stage1(f, b)
            stage2(f, b - 1)
        stage2(f, nb - 1)

    gmix_ref[...] = jnp.zeros_like(gmix_ref)
    gbias_ref[...] = jnp.zeros_like(gbias_ref)

    @pl.loop(0, nb)
    def _(b):
        rows = pl.ds(pl.multiple_of(b * tb, tb), tb)
        out_ref[rows, :] = acc_ref[rows, :].astype(BF)
        gb = gmid_ref[rows, :].astype(BF)
        gctx_ref[rows, :] = mm(gb, mix_ref[...], NT).astype(BF)
        gmix_ref[...] += mm(ctx_ref[rows, :].T, gb)
        gbias_ref[5:6, :] += mm(ones, gb)[0:1]
        gbias_ref[4:5, :] += mm(ones, cot_ref[rows, :])[0:1]

    for f in range(nf):
        gbias_ref[f : f + 1, :] = glift_ref[f, width : width + 1, :]


def feed(tok, ctx, cot, mix, lift, drop, bias):
    tokens, width = tok.shape
    nf = lift.shape[0]
    tb = 512
    vmem = pl.BlockSpec(memory_space=pltpu.VMEM)
    return pl.pallas_call(
        functools.partial(feed_kernel, tb=tb),
        in_specs=[vmem] * 7,
        out_specs=[vmem] * 7,
        out_shape=[
            jax.ShapeDtypeStruct((tokens, width), BF),
            jax.ShapeDtypeStruct((tokens, width), F32),
            jax.ShapeDtypeStruct((tokens, width), BF),
            jax.ShapeDtypeStruct((nf, width + 16, 512), F32),
            jax.ShapeDtypeStruct((nf, width, 512), F32),
            jax.ShapeDtypeStruct((width, width), F32),
            jax.ShapeDtypeStruct((8, 512), F32),
        ],
        scratch_shapes=[
            pltpu.VMEM((tokens, width), BF),
            pltpu.VMEM((width + 16, tokens), BF),
            pltpu.VMEM((width, tokens), BF),
            pltpu.VMEM((tokens, width), F32),
            pltpu.VMEM((tokens // tb, tb, 512), BF),
            pltpu.VMEM((tokens // tb, tb, 512), BF),
        ],
        compiler_params=pltpu.CompilerParams(vmem_limit_bytes=VMEM_LIMIT),
        name="feed",
    )(tok, ctx, cot, mix, lift, drop, bias)


MESH = pl.DeviceIdType.MESH
GATHER_TICKS = (0, 6, 10, 14, 16)
REDUCE_TICKS = (0, 3, 8, 13, 17)
EARLY = 4


class Place:
    def __init__(self, nz):
        self.nz = nz
        self.z = lax.axis_index("gx")
        g = lax.axis_index("gy")
        self.c = g % 2
        self.x = (g // 2) % 2
        self.y = g // 4
        self.oc = 1 - self.c
        self.y1 = self.y + self.oc * (1 - 2 * self.y)
        self.x1 = self.x + self.c * (1 - 2 * self.x)
        self.y2 = self.y + self.c * (1 - 2 * self.y)
        self.x2 = self.x + self.oc * (1 - 2 * self.x)
        self.core = (self.z, self.y * 4 + self.x * 2 + self.oc)
        self.near1 = (self.z, self.y1 * 4 + self.x1 * 2 + self.c)
        self.near2 = (self.z, self.y2 * 4 + self.x2 * 2 + self.c)

    def at_z(self, z):
        return (z, self.y * 4 + self.x * 2 + self.c)

    def up(self, k):
        return (self.z + k) % self.nz

    def down(self, k):
        return (self.z + self.nz - k) % self.nz

    def greet(self):
        barrier = pltpu.get_barrier_semaphore()
        others = [self.core, self.near1, self.near2] + [self.at_z(self.up(k)) for k in range(1, self.nz)]
        for other in others:
            pl.semaphore_signal(barrier, inc=1, device_id=other, device_id_type=MESH)
        pl.semaphore_wait(barrier, len(others))


def remote(src, dst, send, recv, u, k, device):
    return pltpu.make_async_remote_copy(
        src_ref=src,
        dst_ref=dst,
        send_sem=send.at[u, k],
        recv_sem=recv.at[u, k],
        device_id=device,
        device_id_type=MESH,
    )


class Gather:
    def __init__(self, me, buf, send, recv, u):
        nz = me.nz
        own = buf.at[:, me.y, me.x, me.c]
        other = buf.at[:, me.y1, me.x1, me.c]
        mine = buf.at[me.z, me.y, me.x, me.c]
        half = buf.at[:, :, :, me.c]
        self.along_z = lambda: [remote(mine, mine, send, recv, u, k - 1, me.at_z(me.up(k))) for k in range(1, nz)]
        self.first = lambda: remote(own, own, send, recv, u, nz - 1, me.near1)
        self.second = lambda: remote(own, own, send, recv, u, nz, me.near2)
        self.passed = lambda: remote(other, other, send, recv, u, nz + 1, me.near2)
        self.core = lambda: remote(half, half, send, recv, u, nz + 2, me.core)

    def start(self):
        for copy in self.along_z():
            copy.start()

    def step1(self):
        for copy in self.along_z():
            copy.wait_recv()
        self.first().start()
        self.second().start()

    def step2(self):
        self.first().wait_recv()
        self.passed().start()

    def step3(self):
        self.second().wait_recv()
        self.passed().wait_recv()
        self.core().start()

    def step4(self):
        self.core().wait_recv()

    def finish(self):
        for copy in self.along_z() + [self.first(), self.second(), self.passed(), self.core()]:
            copy.wait_send()


class Reduce:
    def __init__(self, me, bufs, u, send, recv):
        self.me = me
        nz = me.nz
        self.sc, self.rc, self.s1, self.r1, self.s2, self.r2, self.sz, self.rz, self.hold = [b.at[u] for b in bufs]
        self.core = lambda: remote(self.sc, self.rc, send, recv, u, 0, me.core)
        self.first = lambda: remote(self.s1, self.r1, send, recv, u, 1, me.near2)
        self.second = lambda: remote(self.s2, self.r2, send, recv, u, 2, me.near1)
        self.along_z = lambda: [
            remote(self.sz.at[me.up(k)], self.rz.at[me.z], send, recv, u, 2 + k, me.at_z(me.up(k)))
            for k in range(1, nz)
        ]

    def start(self, unit):
        me = self.me
        self.sc[...] = unit[:, :, :, me.oc].astype(BF)
        self.core().start()

    def step1(self, unit):
        me = self.me
        self.core().wait_recv()

        def total(y, x):
            return unit[:, y, x, me.c] + self.rc[:, y, x].astype(F32)

        self.s1[0] = total(me.y2, me.x2).astype(BF)
        self.s1[1] = total(1 - me.y, 1 - me.x).astype(BF)
        self.first().start()
        self.hold[0] = total(me.y, me.x)
        self.hold[1] = total(me.y1, me.x1)

    def step2(self):
        self.first().wait_recv()
        self.s2[...] = (self.hold[1] + self.r1[1].astype(F32)).astype(BF)
        self.second().start()
        self.hold[0] = self.hold[0] + self.r1[0].astype(F32)

    def step3(self):
        self.second().wait_recv()
        total = self.hold[0] + self.r2[...].astype(F32)
        self.sz[...] = total.astype(BF)
        self.hold[0] = total
        for copy in self.along_z():
            copy.start()

    def step4(self):
        me = self.me
        for copy in self.along_z():
            copy.wait_recv()
        total = self.hold[0, me.z]
        for k in range(1, me.nz):
            total = total + self.rz[me.down(k)].astype(F32)
        return total

    def finish(self):
        for copy in [self.core(), self.first(), self.second()] + self.along_z():
            copy.wait_send()


def reduce_bufs(n, nz, w):
    return [
        pltpu.VMEM((n, nz, 2, 2, 16, w), BF),
        pltpu.VMEM((n, nz, 2, 2, 16, w), BF),
        pltpu.VMEM((n, 2, nz, 16, w), BF),
        pltpu.VMEM((n, 2, nz, 16, w), BF),
        pltpu.VMEM((n, nz, 16, w), BF),
        pltpu.VMEM((n, nz, 16, w), BF),
        pltpu.VMEM((n, nz, 16, w), BF),
        pltpu.VMEM((n, nz, 16, w), BF),
        pltpu.VMEM((n, 2, nz, 16, w), F32),
    ]


def sems(n, nz):
    return [pltpu.SemaphoreType.DMA((n, nz + 3)), pltpu.SemaphoreType.DMA((n, nz + 3))]


def unit_order():
    c = lax.broadcasted_iota(jnp.int32, (512, 512), 1)
    s = lax.broadcasted_iota(jnp.int32, (512, 512), 0)
    return jnp.where(s == ((c & 127) >> 4) * 64 + (c >> 7) * 16 + (c & 15), 1.0, 0.0).astype(BF)


def first_kernel(
    nz,
    tok_ref,
    joint_ref,
    mix_own_ref,
    lift_ref,
    drop_ref,
    bias_own_ref,
    seg_ref,
    qkv_ref,
    jw_ref,
    mix_ref,
    early_ref,
    bias_ref,
    starts_ref,
    bw_ref,
    send,
    recv,
):
    me = Place(nz)
    tokens, width = tok_ref.shape
    early = early_ref.shape[0]
    nf = drop_ref.shape[0] // 16
    here = (me.z, me.y, me.x, me.c)
    bw_ref[here] = bias_own_ref[...]
    for u in range(3):
        jw_ref[(u,) + here] = joint_ref[:, u * 512 : (u + 1) * 512]
    mix_ref[here] = mix_own_ref[...]
    me.greet()
    jobs = [Gather(me, bw_ref, send, recv, 0)]
    jobs += [Gather(me, jw_ref.at[u], send, recv, 1 + u) for u in range(3)]
    jobs += [Gather(me, mix_ref, send, recv, 4)]
    jobs += [Gather(me, early_ref.at[u], send, recv, 5 + u) for u in range(early)]
    events = []
    for u, job in enumerate(jobs):
        for k, when in enumerate(GATHER_TICKS):
            events.append((2 * u + when, k, u, (job.start, job.step1, job.step2, job.step3, job.step4)[k]))
    events.sort(key=lambda e: (e[0], -e[1]))
    n_early = 4
    for event in events[:n_early]:
        event[3]()
    rows = jnp.concatenate([lift_ref[:, u * 512 : (u + 1) * 512] for u in range(nf)], axis=0)
    rows = mm(rows, unit_order()).astype(BF)
    for f in range(early // 2):
        lift = jnp.concatenate([rows[16 * u : 16 * u + 16, 128 * f : 128 * f + 128] for u in range(nf)], axis=1)
        drop = drop_ref[16 * f : 16 * f + 16, :]
        early_ref[(2 * f,) + here] = lift
        early_ref[(2 * f + 1,) + here] = drop
    seg = seg_ref[...]
    lane = lax.broadcasted_iota(jnp.int32, starts_ref.shape, 1)
    starts = jnp.zeros(starts_ref.shape, jnp.int32)
    for v in range(1, 6):
        count = jnp.sum(jnp.where(seg < v, 1.0, 0.0), axis=1, keepdims=True).astype(jnp.int32)
        starts = jnp.where(lane == v, count, starts)
    starts_ref[...] = starts

    for _, k, u, run in events[n_early:]:
        run()
        if k < 4:
            continue
        u -= 1
        if u < 0:
            bias_ref[...] = bw_ref[...].reshape(512, 128).astype(F32).T[:8]
        elif u < 3:

            @pl.loop(0, tokens // 512)
            def _(b, u=u):
                rows = pl.ds(pl.multiple_of(b * 512, 512), 512)
                y = mm(tok_ref[rows, :], jw_ref[u].reshape(512, 512))
                if u == 0:
                    y = y + bias_ref[6:7, :]
                if u == 2:
                    y = y + bias_ref[7:8, :]
                qkv_ref[rows, u * 512 : (u + 1) * 512] = y.astype(BF)

    for job in jobs:
        job.finish()


def first(nz, tok, joint, mix, lift, drop, bias_own, seg):
    tokens = tok.shape[0]
    vmem = pl.BlockSpec(memory_space=pltpu.VMEM)
    unit = (nz, 2, 2, 2, 16, 512)
    return pl.pallas_call(
        functools.partial(first_kernel, nz),
        in_specs=[vmem] * 7,
        out_specs=[vmem] * 6,
        out_shape=[
            jax.ShapeDtypeStruct((tokens, 1536), BF),
            jax.ShapeDtypeStruct((3,) + unit, BF),
            jax.ShapeDtypeStruct(unit, BF),
            jax.ShapeDtypeStruct((EARLY,) + unit, BF),
            jax.ShapeDtypeStruct((8, 512), F32),
            jax.ShapeDtypeStruct((seg.shape[0], 128), jnp.int32),
        ],
        scratch_shapes=[pltpu.VMEM((nz, 2, 2, 2, 16, 128), BF)] + sems(5 + EARLY, nz),
        compiler_params=pltpu.CompilerParams(vmem_limit_bytes=VMEM_LIMIT, collective_id=1, has_side_effects=True),
        name="gather_joint",
    )(tok, joint, mix, lift, drop, bias_own, seg)


def middle_kernel(
    nz,
    tb,
    tok_ref,
    ctx_ref,
    cot_ref,
    mix_ref,
    early_ref,
    late_ref,
    bias_ref,
    out_ref,
    gmid_ref,
    gctx_ref,
    gmix_ref,
    gbias_ref,
    kept_ref,
    grad_ref,
    w_ref,
    hid_ref,
    hidt_ref,
    cott_ref,
    acc_ref,
    act_ref,
    gl_ref,
    gdt_ref,
    sum_ref,
    load_sem,
    rsend,
    rrecv,
    *bufs,
):
    me = Place(nz)
    tokens, width = tok_ref.shape
    nf = w_ref.shape[0] // 2
    nb = tokens // tb
    early = early_ref.shape[0]
    loads = [pltpu.make_async_copy(early_ref, w_ref.at[0:early], load_sem.at[0])]
    for u in range(early, 2 * nf):
        at = (u - early) * 512
        loads.append(pltpu.make_async_copy(late_ref.at[:, at : at + 512], w_ref.at[u], load_sem.at[u]))
    for load in loads:
        load.start()
    ones = jnp.ones((16, tb), BF)

    def reduces(f):
        return [Reduce(me, bufs, 2 * f + i, rsend, rrecv) for i in range(2)]

    me.greet()

    @pl.loop(0, nb)
    def _(b):
        rows = pl.ds(pl.multiple_of(b * tb, tb), tb)
        mid = tok_ref[rows, :].astype(F32) + mm(ctx_ref[rows, :], mix_ref[...]) + bias_ref[5:6, :]
        acc_ref[rows, :] = mid + bias_ref[4:5, :]
        h = mid.astype(BF)
        hid_ref[rows, :] = h
        hidt_ref[0:width, rows] = h.T
        hidt_ref[width : width + 16, rows] = ones
        c = cot_ref[rows, :]
        cott_ref[:, rows] = c.T
        gmid_ref[rows, :] = c.astype(F32)

    gbias_ref[...] = jnp.zeros_like(gbias_ref)
    for load in loads:
        load.wait()

    def stage1(f, b):
        rows = pl.ds(b * tb, tb)
        lw = w_ref[2 * f]
        dw = w_ref[2 * f + 1]
        for n in range(0, 512, 256):
            x = mm(hid_ref[rows, :], lw[:, n : n + 256]) + bias_ref[pl.ds(f, 1), n : n + 256]
            grad = mm(cot_ref[rows, :], dw[n : n + 256, :], NT)
            a, g = gelu_pair(x, grad)
            act_ref[b, :, n : n + 256] = a
            gl_ref[b, :, n : n + 256] = g

    def stage2(f, b):
        slot = f % 2
        rows = pl.ds(b * tb, tb)
        act = act_ref[b]
        gl = gl_ref[b]
        acc_ref[rows, :] += mm(act, w_ref[2 * f + 1])
        gmid_ref[rows, :] += mm(gl, w_ref[2 * f], NT)
        gd = mm(cott_ref[:, rows], act)
        gf = mm(hidt_ref[:, rows], gl)
        unit = gf[:width].reshape(nz, 2, 2, 2, 16, 512)
        if b == 0:
            gdt_ref[...] = gd
            sum_ref[slot, 0] = unit
        elif b < nb - 1:
            gdt_ref[...] += gd
            sum_ref[slot, 0] += unit
        else:
            sum_ref[slot, 1] = (gdt_ref[...] + gd).T.reshape(nz, 2, 2, 2, 16, 512)
            sum_ref[slot, 0] += unit
        gbias_ref[pl.ds(f, 1), :] += gf[width : width + 1]

    def reduce_step(f, k):
        slot = f % 2
        for i, job in enumerate(reduces(f)):
            if k == 0:
                job.start(sum_ref.at[slot, i])
            elif k == 1:
                job.step1(sum_ref.at[slot, i])
            elif k == 2:
                job.step2()
            elif k == 3:
                job.step3()
            else:
                grad_ref[2 * f + i] = job.step4()

    @pl.loop(0, nf)
    def _(f):
        for k in range(nb):

            @pl.when(f > 0)
            def _(k=k):
                if k == 0:
                    reduce_step(f - 1, 0)
                if k == 1:
                    reduce_step(f - 1, 1)
                if k == 3:
                    reduce_step(f - 1, 2)

            @pl.when(f > 1)
            def _(k=k):
                if k == 1:
                    reduce_step(f - 2, 3)
                if k == 3:
                    reduce_step(f - 2, 4)

            stage1(f, k)
            if k > 0:
                stage2(f, k - 1)
        stage2(f, nb - 1)

    gmix_ref[...] = jnp.zeros_like(gmix_ref)
    for b in range(nb):
        if b == 1:
            reduce_step(nf - 2, 3)
        rows = pl.ds(b * tb, tb)
        out_ref[rows, :] = acc_ref[rows, :].astype(BF)
        gb = gmid_ref[rows, :].astype(BF)
        gctx_ref[rows, :] = mm(gb, mix_ref[...], NT).astype(BF)
        gmix_ref[...] += mm(ctx_ref[rows, :].T, gb)
        gbias_ref[5:6, :] += mm(ones, gb)[0:1]
        gbias_ref[4:5, :] += mm(ones, cot_ref[rows, :])[0:1]
    kept_ref[...] = sum_ref[(nf - 1) % 2]
    reduce_step(nf - 2, 4)
    for f in range(nf - 1):
        for job in reduces(f):
            job.finish()


def middle(nz, tok, ctx, cot, mix, early, late, bias):
    tokens, width = tok.shape
    n = early.shape[0] + late.shape[1] // 512
    tb = tokens // 4
    vmem = pl.BlockSpec(memory_space=pltpu.VMEM)
    return pl.pallas_call(
        functools.partial(middle_kernel, nz, tb),
        in_specs=[vmem] * 4 + [pl.BlockSpec(memory_space=pl.ANY)] * 2 + [vmem],
        out_specs=[vmem] * 7,
        out_shape=[
            jax.ShapeDtypeStruct((tokens, width), BF),
            jax.ShapeDtypeStruct((tokens, width), F32),
            jax.ShapeDtypeStruct((tokens, width), BF),
            jax.ShapeDtypeStruct((width, width), F32),
            jax.ShapeDtypeStruct((8, 512), F32),
            jax.ShapeDtypeStruct((2, nz, 2, 2, 2, 16, 512), F32),
            jax.ShapeDtypeStruct((n - 2, 16, 512), F32),
        ],
        scratch_shapes=[
            pltpu.VMEM((n, 512, 512), BF),
            pltpu.VMEM((tokens, width), BF),
            pltpu.VMEM((width + 16, tokens), BF),
            pltpu.VMEM((width, tokens), BF),
            pltpu.VMEM((tokens, width), F32),
            pltpu.VMEM((4, tb, 512), BF),
            pltpu.VMEM((4, tb, 512), BF),
            pltpu.VMEM((width, 512), F32),
            pltpu.VMEM((2, 2, nz, 2, 2, 2, 16, 512), F32),
            pltpu.SemaphoreType.DMA((n,)),
        ]
        + sems(n - 2, nz)
        + reduce_bufs(n - 2, nz, 512),
        compiler_params=pltpu.CompilerParams(vmem_limit_bytes=VMEM_LIMIT, collective_id=2, has_side_effects=True),
        name="feed",
    )(tok, ctx, cot, mix, early, late, bias)


def last_kernel(
    nz,
    tok_ref,
    gj_ref,
    gmix_ref,
    gbias_ref,
    kept_ref,
    grad_ref,
    joint_ref,
    mix_ref,
    obias_ref,
    glift_ref,
    gdrop_ref,
    tokt_ref,
    sum_ref,
    bsum_ref,
    brow_ref,
    send,
    recv,
    bsend,
    brecv,
    *bufs,
):
    me = Place(nz)
    tokens, width = tok_ref.shape
    n = 7
    nf = glift_ref.shape[1] // 512
    me.greet()
    jobs = [Reduce(me, bufs[:9], u, send, recv) for u in range(n - 1)] + [Reduce(me, bufs[9:], 0, bsend, brecv)]
    units = [kept_ref.at[0], kept_ref.at[1], gmix_ref] + [sum_ref.at[j] for j in range(3)] + [bsum_ref]

    def begin(u):
        if u == n - 1:
            bsum_ref[...] = brow_ref[...].T.reshape(nz, 2, 2, 2, 16, 128)
        elif u > 2:
            if u == 3:

                @pl.loop(0, tokens // 512)
                def _(b):
                    rows = pl.ds(pl.multiple_of(b * 512, 512), 512)
                    tokt_ref[0:width, rows] = tok_ref[rows, :].T
                    tokt_ref[width : width + 16, rows] = jnp.ones((16, 512), BF)

                brow_ref[...] = jnp.zeros_like(brow_ref)
                brow_ref[0:8, :] = gbias_ref[...]
            g = mm(tokt_ref[...], gj_ref[:, (u - 3) * 512 : (u - 2) * 512])
            sum_ref[u - 3] = g[:width].reshape(nz, 2, 2, 2, 16, 512)
            if u != 4:
                at = 6 + (u - 3) // 2
                brow_ref[at : at + 1, :] = g[width : width + 1]
        jobs[u].start(units[u])

    def put_lift(last):
        g = jnp.concatenate(
            [
                jnp.concatenate(
                    [grad_ref[2 * f, :, 128 * u : 128 * u + 128] for f in range(nf - 1)]
                    + [last[:, 128 * u : 128 * u + 128]],
                    axis=1,
                )
                for u in range(nf)
            ],
            axis=0,
        )
        order = unit_order()
        high = g.astype(BF)
        rest = g - high.astype(F32)
        part = rest.astype(BF)
        low = (rest - part.astype(F32)).astype(BF)
        g = mm(high, order, NT) + mm(part, order, NT) + mm(low, order, NT)
        for u in range(nf):
            glift_ref[:, 512 * u : 512 * u + 512] = g[16 * u : 16 * u + 16]

    def end(u):
        total = jobs[u].step4()
        if u == 0:
            put_lift(total)
        elif u == 1:
            for f in range(nf - 1):
                gdrop_ref[16 * f : 16 * f + 16, :] = grad_ref[2 * f + 1]
            gdrop_ref[16 * nf - 16 : 16 * nf, :] = total
        elif u == 2:
            mix_ref[...] = total
        elif u < n - 1:
            joint_ref[:, (u - 3) * 512 : (u - 2) * 512] = total
        else:
            obias_ref[...] = total.T

    def run(u, k):
        if k == 0:
            begin(u)
        elif k == 1:
            jobs[u].step1(units[u])
        elif k == 2:
            jobs[u].step2()
        elif k == 3:
            jobs[u].step3()
        else:
            end(u)

    events = [(2 * u + when, k, u) for u in range(n) for k, when in enumerate(REDUCE_TICKS)]
    for _, k, u in sorted(events, key=lambda e: (e[0], -e[1])):
        run(u, k)
    for job in jobs:
        job.finish()


def last(nz, tok, gj, gmix, gbias, kept, grads):
    tokens, width = tok.shape
    n = grads.shape[0] + 2
    vmem = pl.BlockSpec(memory_space=pltpu.VMEM)
    return pl.pallas_call(
        functools.partial(last_kernel, nz),
        in_specs=[vmem] * 6,
        out_specs=[vmem] * 5,
        out_shape=[
            jax.ShapeDtypeStruct((16, 1536), F32),
            jax.ShapeDtypeStruct((16, 512), F32),
            jax.ShapeDtypeStruct((128, 16), F32),
            jax.ShapeDtypeStruct((16, n // 2 * 512), F32),
            jax.ShapeDtypeStruct((n // 2 * 16, 512), F32),
        ],
        scratch_shapes=[
            pltpu.VMEM((width + 16, tokens), BF),
            pltpu.VMEM((3, nz, 2, 2, 2, 16, 512), F32),
            pltpu.VMEM((nz, 2, 2, 2, 16, 128), F32),
            pltpu.VMEM((128, 512), F32),
        ]
        + sems(6, nz)
        + sems(1, nz)
        + reduce_bufs(6, nz, 512)
        + reduce_bufs(1, nz, 128),
        compiler_params=pltpu.CompilerParams(vmem_limit_bytes=VMEM_LIMIT, collective_id=3, has_side_effects=True),
        name="joint_grads",
    )(tok, gj, gmix.reshape(nz, 2, 2, 2, 16, 512), gbias, kept, grads)


def remote_body(
    tokens,
    segment_ids,
    fill_lengths,
    joint_weight,
    joint_bias,
    mix_weight,
    mix_bias,
    lift_weight,
    lift_bias,
    drop_weight,
    drop_bias,
    cotangent,
):
    rows, length, width = tokens.shape
    nz = lax.axis_size("gx")
    n_tok = rows * length
    tok = tokens.reshape(n_tok, width)
    nf = drop_weight.shape[0] // 16
    bias_own = jnp.concatenate([lift_bias.reshape(nf, 16), drop_bias[None], mix_bias[None], joint_bias])
    bias_own = jnp.pad(bias_own, ((0, 120), (0, 0))).T
    lift_own = lift_weight.reshape(16, -1, nf, 16)
    late = []
    for f in range(EARLY // 2, nf):
        late += [lift_own[:, :, f].reshape(16, 512), drop_weight[16 * f : 16 * f + 16]]
    late = lax.all_gather(jnp.concatenate(late, axis=1), BOTH, axis=0, tiled=True)
    qkv, joint_w, mix_w, early, bias, starts = first(
        nz, tok, joint_weight, mix_weight, lift_weight, drop_weight, bias_own, segment_ids
    )
    qkv3 = qkv.reshape(rows, length, 3 * width)
    ctx, lse = attend(starts, fill_lengths, segment_ids, qkv3)
    out, gmid, gctx, gmix, gbias, kept, grads = middle(
        nz, tok, ctx.reshape(n_tok, width), cotangent.reshape(n_tok, width), mix_w.reshape(width, width), early.reshape(EARLY, 512, 512), late, bias
    )
    gjoint, token_grad, out = attend_back(
        starts,
        fill_lengths,
        segment_ids,
        qkv3,
        lse,
        ctx,
        gctx.reshape(rows, length, width),
        gmid.reshape(rows, length, width),
        joint_w.reshape(3, width, width),
        out.reshape(rows, length, width),
    )
    gj, gm, gb, glift, gdrop = last(nz, tok, gjoint.reshape(n_tok, 3 * width), gmix, gbias, kept, grads)
    return (out, token_grad, gj, gb[6:8], gm, gb[5], glift, gb[:nf].reshape(-1), gdrop, gb[4])


BOTH = ("gx", "gy")


def body(
    tokens,
    segment_ids,
    fill_lengths,
    joint_weight,
    joint_bias,
    mix_weight,
    mix_bias,
    lift_weight,
    lift_bias,
    drop_weight,
    drop_bias,
    cotangent,
):
    rows, length, width = tokens.shape
    n_tok = rows * length
    tok = tokens.reshape(n_tok, width)
    cot = cotangent.reshape(n_tok, width)
    starts = jnp.sum(
        segment_ids[:, None, :] < jnp.arange(128, dtype=jnp.int32)[None, :, None], axis=-1, dtype=jnp.int32
    )

    joint_w = lax.all_gather(joint_weight, BOTH, axis=0, tiled=True)
    mix_w = lax.all_gather(mix_weight, BOTH, axis=0, tiled=True)
    lift_w = lax.all_gather(lift_weight, BOTH, axis=0, tiled=True)
    drop_w = lax.all_gather(drop_weight, BOTH, axis=0, tiled=True)
    own_bias = jnp.concatenate([joint_bias.reshape(-1), mix_bias, lift_bias, drop_bias])
    sizes = [joint_bias.shape[1], joint_bias.shape[1], mix_bias.size, lift_bias.size, drop_bias.size]
    all_bias = lax.all_gather(own_bias, BOTH, axis=0)
    parts, at = [], 0
    for size in sizes:
        parts.append(all_bias[:, at : at + size].reshape(-1).astype(F32))
        at += size
    bq, bv, bm, bl, bd = parts
    nf = bl.size // 512
    bias = jnp.concatenate(
        [jnp.concatenate([bl.reshape(nf, 512), jnp.zeros((4 - nf, 512), F32)]), bd[None], bm[None], bq[None], bv[None]]
    )

    shift = jnp.concatenate([bq, jnp.zeros_like(bq), bv])
    qkv = (mm(tok, joint_w) + shift).astype(BF)
    qkv3 = qkv.reshape(rows, length, 3 * width)
    ctx, lse = attend(starts, fill_lengths, segment_ids, qkv3)
    lift_units = lift_w.reshape(width, nf, 512).transpose(1, 0, 2)
    out, gmid, gctx, glift, gdrop, gmix, gbias = feed(
        tok, ctx.reshape(n_tok, width), cot, mix_w, lift_units, drop_w.reshape(nf, 512, width), bias
    )
    gjoint, token_grad, out = attend_back(
        starts,
        fill_lengths,
        segment_ids,
        qkv3,
        lse,
        ctx,
        gctx.reshape(rows, length, width),
        gmid.reshape(rows, length, width),
        joint_w.reshape(width, 3, width).transpose(1, 0, 2),
        out.reshape(rows, length, width),
    )
    gjoint = gjoint.reshape(n_tok, 3 * width)
    gjoint_w = lax.dot_general(tok, gjoint, (((0,), (0,)), ((), ())), preferred_element_type=F32)
    sums = jnp.sum(gjoint.astype(F32), axis=0)

    glift_w = glift[:, :width].transpose(1, 0, 2).reshape(width, nf * 512)
    gdrop_w = gdrop.transpose(0, 2, 1).reshape(nf * 512, width)
    scatter = functools.partial(lax.psum_scatter, axis_name=BOTH, scatter_dimension=0, tiled=True)
    n_dev = all_bias.shape[0]
    packed = jnp.concatenate(
        [
            g.reshape(n_dev, -1)
            for g in (sums[:width], sums[2 * width :], gbias[5], gbias[:nf].reshape(-1), gbias[4])
        ],
        axis=1,
    )
    own = scatter(packed)[0]
    cuts, at = [], 0
    for size in sizes:
        cuts.append(own[at : at + size])
        at += size
    return (
        out,
        token_grad,
        scatter(gjoint_w),
        jnp.stack([cuts[0], cuts[1]]),
        scatter(gmix),
        cuts[2],
        scatter(glift_w),
        cuts[3],
        scatter(gdrop_w),
        cuts[4],
    )


def solution(mesh):
    wide = P(BOTH, None, None)
    rows = P(BOTH, None)
    flat = P(BOTH)
    bias = P(None, BOTH)
    in_specs = (wide, rows, flat, rows, bias, rows, flat, rows, flat, rows, flat, wide)
    out_specs = (wide, wide, rows, bias, rows, flat, rows, flat, rows, flat)
    fits = mesh.shape["gy"] == 8 and mesh.shape["gx"] == 4
    return jax.shard_map(remote_body if fits else body, mesh=mesh, in_specs=in_specs, out_specs=out_specs, check_vma=False)
```

```python
import functools
import math

import jax
import jax.numpy as jnp
from jax import lax
from jax.experimental import pallas as pl
from jax.experimental.pallas import tpu as pltpu
from jax.sharding import PartitionSpec as P

BF = jnp.bfloat16
F32 = jnp.float32
NT = (((1,), (1,)), ((), ()))
NN = (((1,), (0,)), ((), ()))
NEG = -float(2**30)
C0 = math.sqrt(2.0 / math.pi)
C1 = 0.044715
CUT = 2
VMEM_LIMIT = 60 * 2**20


def mm(a, b, dims=NN):
    return lax.dot_general(a, b, dims, preferred_element_type=F32)


def split_heads(x):
    lane = lax.broadcasted_iota(jnp.int32, x.shape, 1)
    zero = jnp.zeros_like(x)
    return jnp.concatenate([jnp.where(lane < 64, x, zero), jnp.where(lane < 64, zero, x)], axis=0)


def diag_blocks(y):
    return jnp.concatenate([y[:64, :128], y[64:, 128:]], axis=0)


def window(starts_ref, fill_ref, row, t, length):
    first = t * 128
    last = first + 127
    fill = fill_ref[row]
    lo = jnp.int32(0)
    hi = jnp.int32(length)
    for v in range(1, 6):
        s = starts_ref[row, v]
        lo = jnp.where(s <= first, jnp.maximum(lo, s), lo)
        hi = jnp.where(s > last, jnp.minimum(hi, s), hi)
    hi = jnp.minimum(hi, fill)
    alone = lo >= fill
    hi = jnp.where(last >= fill, jnp.maximum(hi, last + 1), hi)
    lo = jnp.where(alone, first, lo)
    lo_b = lo // 128
    return lo_b, (hi + 127) // 128 - lo_b


def ids_of(seg_ref, row, lanes):
    ids = seg_ref[:, lanes]
    mine = lax.broadcasted_iota(jnp.int32, ids.shape, 0) == row
    return jnp.sum(jnp.where(mine, ids.astype(F32), 0.0), axis=0, keepdims=True)


def write_mask(mask_ref, segk_ref, seg_ref, row, fill, t, lo_b, n):
    segq = ids_of(seg_ref, row, pl.ds(pl.multiple_of(t * 128, 128), 128))
    segq = jnp.broadcast_to(segq, (128, 128))
    qi = t * 128 + lax.broadcasted_iota(jnp.int32, (128, 128), 1)
    ki0 = lax.broadcasted_iota(jnp.int32, (128, 128), 0)
    for c in range(n):
        off = pl.multiple_of((lo_b + c) * 128, 128)
        ki = ki0 + off
        ok = ((segk_ref[pl.ds(off, 128), :] == segq) & (ki < fill)) | (ki == qi)
        mask_ref[c * 128 : (c + 1) * 128, :] = jnp.where(ok, 0.0, NEG)


def spread_segments(seg_ref, segk_ref, row, length):
    for b in range(length // 128):
        ids = ids_of(seg_ref, row, slice(b * 128, (b + 1) * 128))
        segk_ref[b * 128 : (b + 1) * 128, :] = jnp.broadcast_to(ids, (128, 128)).T


def attend_kernel(
    starts_ref, fill_ref, seg_ref, qkv_ref, ctx_ref, lse_ref, vt_ref, segk_ref, mask_ref, s_ref, p_ref, *, length
):
    row = pl.program_id(0)
    fill = fill_ref[row]
    spread_segments(seg_ref, segk_ref, row, length)
    for b in range(length // 128):
        for p in range(4):
            v = qkv_ref[0, b * 128 : (b + 1) * 128, 1024 + p * 128 : 1024 + (p + 1) * 128]
            vt_ref[p * 128 : (p + 1) * 128, b * 128 : (b + 1) * 128] = v.T

    def tile(t, lo_b, n):
        tq = pl.ds(pl.multiple_of(t * 128, 128), 128)
        win = pl.ds(pl.multiple_of(lo_b * 128, 128), n * 128)
        cuts = [(c, min(CUT, n - c)) for c in range(0, n, CUT)]
        tops, sums = [], []
        for p in range(4):
            lanes = slice(p * 128, (p + 1) * 128)
            qbd = split_heads(qkv_ref[0, tq, lanes] * jnp.asarray(0.125, BF))
            top = None
            for c, w in cuts:
                rows = pl.ds(pl.multiple_of((lo_b + c) * 128, 128), w * 128)
                s = mm(qkv_ref[0, rows, 512 + p * 128 : 512 + (p + 1) * 128], qbd, NT)
                mask = mask_ref[c * 128 : (c + w) * 128, :]
                s = s + jnp.concatenate([mask, mask], axis=1)
                s_ref[p, c * 128 : (c + w) * 128, :] = s
                part = jnp.max(s.reshape(w * 16, 8, 256), axis=0)
                top = part if top is None else jnp.maximum(top, part)
            tops.append(jnp.max(top, axis=0, keepdims=True))
        for p in range(4):
            total = None
            for c, w in cuts:
                e = jnp.exp(s_ref[p, c * 128 : (c + w) * 128, :] - tops[p])
                p_ref[p, c * 128 : (c + w) * 128, :] = e.astype(BF)
                part = jnp.sum(e.reshape(w * 16, 8, 256), axis=0)
                total = part if total is None else total + part
            sums.append(jnp.sum(total, axis=0, keepdims=True))
        for p in range(4):
            o = mm(vt_ref[p * 128 : (p + 1) * 128, win], p_ref[p, : n * 128, :]) * (1.0 / sums[p])
            ctx_ref[0, tq, p * 128 : (p + 1) * 128] = diag_blocks(o).T.astype(BF)
            lse_ref[0, p, pl.ds(t, 1), :] = tops[p] + jnp.log(sums[p])

    @pl.loop(0, length // 128)
    def _(t):
        lo_b, n = window(starts_ref, fill_ref, row, t, length)
        for k in range(1, length // 128 + 1):

            @pl.when(n == k)
            def _(k=k):
                write_mask(mask_ref, segk_ref, seg_ref, row, fill, t, lo_b, k)
                tile(t, lo_b, k)


def attend(starts, fill, seg, qkv):
    rows, length, _ = qkv.shape
    blocks = length // 128
    return pl.pallas_call(
        functools.partial(attend_kernel, length=length),
        grid_spec=pltpu.PrefetchScalarGridSpec(
            num_scalar_prefetch=2,
            grid=(rows,),
            in_specs=[
                pl.BlockSpec((rows, length), lambda r, *_: (0, 0)),
                pl.BlockSpec((1, length, 1536), lambda r, *_: (r, 0, 0)),
            ],
            out_specs=[
                pl.BlockSpec((1, length, 512), lambda r, *_: (r, 0, 0)),
                pl.BlockSpec((1, 4, blocks, 256), lambda r, *_: (r, 0, 0, 0)),
            ],
            scratch_shapes=[
                pltpu.VMEM((512, length), BF),
                pltpu.VMEM((length, 128), F32),
                pltpu.VMEM((length, 128), F32),
                pltpu.VMEM((4, length, 256), F32),
                pltpu.VMEM((4, length, 256), BF),
            ],
        ),
        out_shape=[
            jax.ShapeDtypeStruct((rows, length, 512), BF),
            jax.ShapeDtypeStruct((rows, 4, blocks, 256), F32),
        ],
        compiler_params=pltpu.CompilerParams(vmem_limit_bytes=VMEM_LIMIT),
        name="attend",
    )(starts, fill, seg, qkv)


def attend_back_kernel(
    starts_ref,
    fill_ref,
    seg_ref,
    qkv_ref,
    lse_ref,
    ctx_ref,
    do_ref,
    gmid_ref,
    jw_ref,
    pass_ref,
    out_ref,
    tg_ref,
    to_ref,
    kt_ref,
    segk_ref,
    mask_ref,
    dk_ref,
    dv_ref,
    p_ref,
    ds_ref,
    *,
    length,
):
    row = pl.program_id(0)
    fill = fill_ref[row]
    to_ref[...] = pass_ref[...]
    spread_segments(seg_ref, segk_ref, row, length)
    for b in range(length // 128):
        for p in range(4):
            k = qkv_ref[0, b * 128 : (b + 1) * 128, 512 + p * 128 : 512 + (p + 1) * 128]
            kt_ref[p * 128 : (p + 1) * 128, b * 128 : (b + 1) * 128] = k.T
    dk_ref[...] = jnp.zeros_like(dk_ref)
    dv_ref[...] = jnp.zeros_like(dv_ref)

    def tile(t, lo_b, n):
        tq = pl.ds(pl.multiple_of(t * 128, 128), 128)
        win = pl.ds(pl.multiple_of(lo_b * 128, 128), n * 128)
        ready = []
        for p in range(4):
            lanes = slice(p * 128, (p + 1) * 128)
            qbd = split_heads(qkv_ref[0, tq, lanes] * jnp.asarray(0.125, BF))
            do = do_ref[0, tq, lanes]
            prod = (do.astype(F32) * ctx_ref[0, tq, lanes].astype(F32)).T
            delta = jnp.concatenate(
                [jnp.sum(prod[:64], axis=0, keepdims=True), jnp.sum(prod[64:], axis=0, keepdims=True)], axis=1
            )
            ready.append((qbd, split_heads(do), delta, lse_ref[0, p, pl.ds(t, 1), :]))
        for c in range(0, n, CUT):
            w = min(CUT, n - c)
            rows = pl.ds(pl.multiple_of((lo_b + c) * 128, 128), w * 128)
            here = slice(c * 128, (c + w) * 128)
            for p in range(4):
                qbd, dobd, delta, lse = ready[p]
                s = mm(qkv_ref[0, rows, 512 + p * 128 : 512 + (p + 1) * 128], qbd, NT)
                dp = mm(qkv_ref[0, rows, 1024 + p * 128 : 1024 + (p + 1) * 128], dobd, NT)
                mask = mask_ref[here, :]
                e = jnp.exp(s + jnp.concatenate([mask, mask], axis=1) - lse)
                p_ref[p, here, :] = e.astype(BF)
                ds_ref[p, here, :] = (e * (dp - delta)).astype(BF)
            for p in range(4):
                qbd, dobd, _, _ = ready[p]
                lanes = slice(p * 128, (p + 1) * 128)
                dv_ref[rows, lanes] += mm(p_ref[p, here, :], dobd)
                dk_ref[rows, lanes] += mm(ds_ref[p, here, :], qbd)
        for p in range(4):
            lanes = slice(p * 128, (p + 1) * 128)
            dq = mm(kt_ref[lanes, win], ds_ref[p, : n * 128, :])
            out_ref[0, tq, lanes] = (diag_blocks(dq) * 0.125).T.astype(BF)

    @pl.loop(0, length // 128)
    def _(t):
        lo_b, n = window(starts_ref, fill_ref, row, t, length)
        for k in range(1, length // 128 + 1):

            @pl.when(n == k)
            def _(k=k):
                write_mask(mask_ref, segk_ref, seg_ref, row, fill, t, lo_b, k)
                tile(t, lo_b, k)

    for b in range(0, length, 256):
        rows = slice(b, b + 256)
        dk = dk_ref[rows, :].astype(BF)
        dv = dv_ref[rows, :].astype(BF)
        out_ref[0, rows, 512:1024] = dk
        out_ref[0, rows, 1024:1536] = dv
        total = gmid_ref[0, rows, :] + mm(out_ref[0, rows, 0:512], jw_ref[0], NT)
        tg_ref[0, rows, :] = total + mm(dk, jw_ref[1], NT) + mm(dv, jw_ref[2], NT)


def attend_back(starts, fill, seg, qkv, lse, ctx, do, gmid, joint, passed):
    rows, length, _ = qkv.shape
    blocks = length // 128
    wide = pl.BlockSpec((1, length, 512), lambda r, *_: (r, 0, 0))
    joined = pl.BlockSpec((1, length, 1536), lambda r, *_: (r, 0, 0))
    return pl.pallas_call(
        functools.partial(attend_back_kernel, length=length),
        grid_spec=pltpu.PrefetchScalarGridSpec(
            num_scalar_prefetch=2,
            grid=(rows,),
            in_specs=[
                pl.BlockSpec((rows, length), lambda r, *_: (0, 0)),
                joined,
                pl.BlockSpec((1, 4, blocks, 256), lambda r, *_: (r, 0, 0, 0)),
                wide,
                wide,
                wide,
                pl.BlockSpec((3, 512, 512), lambda r, *_: (0, 0, 0)),
                wide,
            ],
            out_specs=[joined, wide, wide],
            scratch_shapes=[
                pltpu.VMEM((512, length), BF),
                pltpu.VMEM((length, 128), F32),
                pltpu.VMEM((length, 128), F32),
                pltpu.VMEM((length, 512), F32),
                pltpu.VMEM((length, 512), F32),
                pltpu.VMEM((4, length, 256), BF),
                pltpu.VMEM((4, length, 256), BF),
            ],
        ),
        out_shape=[
            jax.ShapeDtypeStruct((rows, length, 1536), BF),
            jax.ShapeDtypeStruct((rows, length, 512), F32),
            jax.ShapeDtypeStruct(passed.shape, passed.dtype),
        ],
        compiler_params=pltpu.CompilerParams(vmem_limit_bytes=VMEM_LIMIT),
        name="attend_back",
    )(starts, fill, seg, qkv, lse, ctx, do, gmid, joint, passed)


def gelu_pair(x, grad):
    x2 = x * x
    h = 0.5 + 0.5 * jnp.tanh(x * (C0 + (C0 * C1) * x2))
    act = x * h
    slope = h + act * (1.0 - h) * (2.0 * C0 + (6.0 * C0 * C1) * x2)
    return act.astype(BF), (grad * slope).astype(BF)


def feed_kernel(
    tok_ref,
    ctx_ref,
    cot_ref,
    mix_ref,
    lift_ref,
    drop_ref,
    bias_ref,
    out_ref,
    gmid_ref,
    gctx_ref,
    glift_ref,
    gdrop_ref,
    gmix_ref,
    gbias_ref,
    hid_ref,
    hidt_ref,
    cott_ref,
    acc_ref,
    act_ref,
    gl_ref,
    *,
    tb,
):
    tokens, width = tok_ref.shape
    nf = lift_ref.shape[0]
    nb = tokens // tb
    ones = jnp.ones((16, tb), BF)

    @pl.loop(0, nb)
    def _(b):
        rows = pl.ds(pl.multiple_of(b * tb, tb), tb)
        mid = tok_ref[rows, :].astype(F32) + mm(ctx_ref[rows, :], mix_ref[...]) + bias_ref[5:6, :]
        acc_ref[rows, :] = mid + bias_ref[4:5, :]
        h = mid.astype(BF)
        hid_ref[rows, :] = h
        hidt_ref[0:width, rows] = h.T
        hidt_ref[width : width + 16, rows] = ones
        c = cot_ref[rows, :]
        cott_ref[:, rows] = c.T
        gmid_ref[rows, :] = c.astype(F32)

    def stage1(f, b):
        rows = pl.ds(b * tb, tb)
        for n in range(0, 512, 256):
            x = mm(hid_ref[rows, :], lift_ref[f, :, n : n + 256]) + bias_ref[pl.ds(f, 1), n : n + 256]
            grad = mm(cot_ref[rows, :], drop_ref[f, n : n + 256, :], NT)
            a, g = gelu_pair(x, grad)
            act_ref[b, :, n : n + 256] = a
            gl_ref[b, :, n : n + 256] = g

    def stage2(f, b):
        rows = pl.ds(b * tb, tb)
        act = act_ref[b]
        gl = gl_ref[b]
        acc_ref[rows, :] += mm(act, drop_ref[f])
        gmid_ref[rows, :] += mm(gl, lift_ref[f], NT)
        gd = mm(cott_ref[:, rows], act)
        gf = mm(hidt_ref[:, rows], gl)
        if b == 0:
            gdrop_ref[f] = gd
            glift_ref[f] = gf
        else:
            gdrop_ref[f] += gd
            glift_ref[f] += gf

    @pl.loop(0, nf)
    def _(f):
        stage1(f, 0)
        for b in range(1, nb):
            stage1(f, b)
            stage2(f, b - 1)
        stage2(f, nb - 1)

    gmix_ref[...] = jnp.zeros_like(gmix_ref)
    gbias_ref[...] = jnp.zeros_like(gbias_ref)

    @pl.loop(0, nb)
    def _(b):
        rows = pl.ds(pl.multiple_of(b * tb, tb), tb)
        out_ref[rows, :] = acc_ref[rows, :].astype(BF)
        gb = gmid_ref[rows, :].astype(BF)
        gctx_ref[rows, :] = mm(gb, mix_ref[...], NT).astype(BF)
        gmix_ref[...] += mm(ctx_ref[rows, :].T, gb)
        gbias_ref[5:6, :] += mm(ones, gb)[0:1]
        gbias_ref[4:5, :] += mm(ones, cot_ref[rows, :])[0:1]

    for f in range(nf):
        gbias_ref[f : f + 1, :] = glift_ref[f, width : width + 1, :]


def feed(tok, ctx, cot, mix, lift, drop, bias):
    tokens, width = tok.shape
    nf = lift.shape[0]
    tb = 512
    vmem = pl.BlockSpec(memory_space=pltpu.VMEM)
    return pl.pallas_call(
        functools.partial(feed_kernel, tb=tb),
        in_specs=[vmem] * 7,
        out_specs=[vmem] * 7,
        out_shape=[
            jax.ShapeDtypeStruct((tokens, width), BF),
            jax.ShapeDtypeStruct((tokens, width), F32),
            jax.ShapeDtypeStruct((tokens, width), BF),
            jax.ShapeDtypeStruct((nf, width + 16, 512), F32),
            jax.ShapeDtypeStruct((nf, width, 512), F32),
            jax.ShapeDtypeStruct((width, width), F32),
            jax.ShapeDtypeStruct((8, 512), F32),
        ],
        scratch_shapes=[
            pltpu.VMEM((tokens, width), BF),
            pltpu.VMEM((width + 16, tokens), BF),
            pltpu.VMEM((width, tokens), BF),
            pltpu.VMEM((tokens, width), F32),
            pltpu.VMEM((tokens // tb, tb, 512), BF),
            pltpu.VMEM((tokens // tb, tb, 512), BF),
        ],
        compiler_params=pltpu.CompilerParams(vmem_limit_bytes=VMEM_LIMIT),
        name="feed",
    )(tok, ctx, cot, mix, lift, drop, bias)


MESH = pl.DeviceIdType.MESH
GATHER_TICKS = (0, 6, 10, 14, 16)
REDUCE_TICKS = (0, 3, 8, 13, 17)
GATHER_AT = ((1, 1), (3, 2), (6, 3), (8, 4))
REDUCE_AT = (0, 2, 5, 7, 9)
EARLY = 4


class Place:
    def __init__(self, nz):
        self.nz = nz
        self.z = lax.axis_index("gx")
        g = lax.axis_index("gy")
        self.c = g % 2
        self.x = (g // 2) % 2
        self.y = g // 4
        self.oc = 1 - self.c
        self.y1 = self.y + self.oc * (1 - 2 * self.y)
        self.x1 = self.x + self.c * (1 - 2 * self.x)
        self.y2 = self.y + self.c * (1 - 2 * self.y)
        self.x2 = self.x + self.oc * (1 - 2 * self.x)
        self.core = (self.z, self.y * 4 + self.x * 2 + self.oc)
        self.near1 = (self.z, self.y1 * 4 + self.x1 * 2 + self.c)
        self.near2 = (self.z, self.y2 * 4 + self.x2 * 2 + self.c)

    def at_z(self, z):
        return (z, self.y * 4 + self.x * 2 + self.c)

    def up(self, k):
        return (self.z + k) % self.nz

    def down(self, k):
        return (self.z + self.nz - k) % self.nz

    def greet(self):
        barrier = pltpu.get_barrier_semaphore()
        others = [self.core, self.near1, self.near2] + [self.at_z(self.up(k)) for k in range(1, self.nz)]
        for other in others:
            pl.semaphore_signal(barrier, inc=1, device_id=other, device_id_type=MESH)
        pl.semaphore_wait(barrier, len(others))


def remote(src, dst, send, recv, u, k, device):
    return pltpu.make_async_remote_copy(
        src_ref=src,
        dst_ref=dst,
        send_sem=send.at[u, k],
        recv_sem=recv.at[u, k],
        device_id=device,
        device_id_type=MESH,
    )


class Gather:
    def __init__(self, me, buf, send, recv, u):
        nz = me.nz
        own = buf.at[:, me.y, me.x, me.c]
        other = buf.at[:, me.y1, me.x1, me.c]
        mine = buf.at[me.z, me.y, me.x, me.c]
        half = buf.at[:, :, :, me.c]
        self.along_z = lambda: [remote(mine, mine, send, recv, u, k - 1, me.at_z(me.up(k))) for k in range(1, nz)]
        self.first = lambda: remote(own, own, send, recv, u, nz - 1, me.near1)
        self.second = lambda: remote(own, own, send, recv, u, nz, me.near2)
        self.passed = lambda: remote(other, other, send, recv, u, nz + 1, me.near2)
        self.core = lambda: remote(half, half, send, recv, u, nz + 2, me.core)

    def start(self):
        for copy in self.along_z():
            copy.start()

    def step1(self):
        for copy in self.along_z():
            copy.wait_recv()
        self.first().start()
        self.second().start()

    def step2(self):
        self.first().wait_recv()
        self.passed().start()

    def step3(self):
        self.second().wait_recv()
        self.passed().wait_recv()
        self.core().start()

    def step4(self):
        self.core().wait_recv()

    def finish(self):
        for copy in self.along_z() + [self.first(), self.second(), self.passed(), self.core()]:
            copy.wait_send()


class Reduce:
    def __init__(self, me, bufs, u, send, recv):
        self.me = me
        nz = me.nz
        self.sc, self.rc, self.s1, self.r1, self.s2, self.r2, self.sz, self.rz, self.hold = [b.at[u] for b in bufs]
        self.core = lambda: remote(self.sc, self.rc, send, recv, u, 0, me.core)
        self.first = lambda: remote(self.s1, self.r1, send, recv, u, 1, me.near2)
        self.second = lambda: remote(self.s2, self.r2, send, recv, u, 2, me.near1)
        self.along_z = lambda: [
            remote(self.sz.at[me.up(k)], self.rz.at[me.z], send, recv, u, 2 + k, me.at_z(me.up(k)))
            for k in range(1, nz)
        ]

    def start(self, unit):
        me = self.me
        self.sc[...] = unit[:, :, :, me.oc].astype(BF)
        self.core().start()

    def step1(self, unit):
        me = self.me
        self.core().wait_recv()

        def total(y, x):
            return unit[:, y, x, me.c] + self.rc[:, y, x].astype(F32)

        self.s1[0] = total(me.y2, me.x2).astype(BF)
        self.s1[1] = total(1 - me.y, 1 - me.x).astype(BF)
        self.first().start()
        self.hold[0] = total(me.y, me.x)
        self.hold[1] = total(me.y1, me.x1)

    def step2(self):
        self.first().wait_recv()
        self.s2[...] = (self.hold[1] + self.r1[1].astype(F32)).astype(BF)
        self.second().start()
        self.hold[0] = self.hold[0] + self.r1[0].astype(F32)

    def step3(self):
        self.second().wait_recv()
        total = self.hold[0] + self.r2[...].astype(F32)
        self.sz[...] = total.astype(BF)
        self.hold[0] = total
        for copy in self.along_z():
            copy.start()

    def step4(self):
        me = self.me
        for copy in self.along_z():
            copy.wait_recv()
        total = self.hold[0, me.z]
        for k in range(1, me.nz):
            total = total + self.rz[me.down(k)].astype(F32)
        return total

    def finish(self):
        for copy in [self.core(), self.first(), self.second()] + self.along_z():
            copy.wait_send()


def reduce_bufs(n, nz, w):
    return [
        pltpu.VMEM((n, nz, 2, 2, 16, w), BF),
        pltpu.VMEM((n, nz, 2, 2, 16, w), BF),
        pltpu.VMEM((n, 2, nz, 16, w), BF),
        pltpu.VMEM((n, 2, nz, 16, w), BF),
        pltpu.VMEM((n, nz, 16, w), BF),
        pltpu.VMEM((n, nz, 16, w), BF),
        pltpu.VMEM((n, nz, 16, w), BF),
        pltpu.VMEM((n, nz, 16, w), BF),
        pltpu.VMEM((n, 2, nz, 16, w), F32),
    ]


def sems(n, nz):
    return [pltpu.SemaphoreType.DMA((n, nz + 3)), pltpu.SemaphoreType.DMA((n, nz + 3))]


def unit_order():
    c = lax.broadcasted_iota(jnp.int32, (512, 512), 1)
    s = lax.broadcasted_iota(jnp.int32, (512, 512), 0)
    return jnp.where(s == ((c & 127) >> 4) * 64 + (c >> 7) * 16 + (c & 15), 1.0, 0.0).astype(BF)


def first_kernel(
    nz,
    tok_hbm,
    joint_ref,
    mix_own_ref,
    lift_ref,
    drop_ref,
    bl_ref,
    bd_ref,
    bm_ref,
    bj_ref,
    seg_ref,
    qkv_hbm,
    jw_hbm,
    mix_hbm,
    early_hbm,
    late_own_ref,
    bias_ref,
    starts_ref,
    tok_ref,
    qkv_ref,
    jw_ref,
    mix_ref,
    early_ref,
    bw_ref,
    line_ref,
    tok_sem,
    qkv_sem,
    unit_sem,
    send,
    recv,
):
    me = Place(nz)
    load = pltpu.make_async_copy(tok_hbm, tok_ref, tok_sem)
    load.start()
    tokens, width = tok_ref.shape
    early = early_ref.shape[0]
    nf = drop_ref.shape[0] // 16
    here = (me.z, me.y, me.x, me.c)
    line_ref[...] = jnp.zeros_like(line_ref)
    line_ref[0:1, 0 : 16 * nf] = bl_ref[...].astype(F32)
    line_ref[4:5, 0:16] = bd_ref[...].astype(F32)
    line_ref[5:6, 0:16] = bm_ref[...].astype(F32)
    line_ref[6:8, 0:16] = bj_ref[...].astype(F32)
    lift_line = line_ref[0:1, :]
    for f in range(1, nf):
        line_ref[f : f + 1, :] = pltpu.roll(lift_line, 128 - 16 * f, 1)
    bw_ref[here] = line_ref[...].T[:16].astype(BF)
    for u in range(3):
        jw_ref[(u,) + here] = joint_ref[:, u * 512 : (u + 1) * 512]
    mix_ref[here] = mix_own_ref[...]
    me.greet()
    jobs = [Gather(me, bw_ref, send, recv, 0)]
    jobs += [Gather(me, jw_ref.at[u], send, recv, 1 + u) for u in range(3)]
    jobs += [Gather(me, mix_ref, send, recv, 4)]
    jobs += [Gather(me, early_ref.at[u], send, recv, 5 + u) for u in range(early)]
    events = []
    for u, job in enumerate(jobs):
        for k, when in enumerate(GATHER_TICKS):
            events.append((2 * u + when, k, u, (job.start, job.step1, job.step2, job.step3, job.step4)[k]))
    events.sort(key=lambda e: (e[0], -e[1]))
    n_early = 4
    for event in events[:n_early]:
        event[3]()
    rows = jnp.concatenate([lift_ref[:, u * 512 : (u + 1) * 512] for u in range(nf)], axis=0)
    rows = mm(rows, unit_order()).astype(BF)
    for f in range(nf):
        lift = jnp.concatenate([rows[16 * u : 16 * u + 16, 128 * f : 128 * f + 128] for u in range(nf)], axis=1)
        drop = drop_ref[16 * f : 16 * f + 16, :]
        if 2 * f < early:
            early_ref[(2 * f,) + here] = lift
            early_ref[(2 * f + 1,) + here] = drop
        else:
            late_own_ref[2 * f - early] = lift
            late_own_ref[2 * f - early + 1] = drop
    seg = seg_ref[...]
    lane = lax.broadcasted_iota(jnp.int32, starts_ref.shape, 1)
    starts = jnp.zeros(starts_ref.shape, jnp.int32)
    for v in range(1, 6):
        count = jnp.sum(jnp.where(seg < v, 1.0, 0.0), axis=1, keepdims=True).astype(jnp.int32)
        starts = jnp.where(lane == v, count, starts)
    starts_ref[...] = starts

    gathered = [(jw_ref.at[u], jw_hbm.at[u]) for u in range(3)] + [(mix_ref, mix_hbm)]
    gathered += [(early_ref.at[u], early_hbm.at[u]) for u in range(early)]
    stores = [pltpu.make_async_copy(a, b, unit_sem.at[i]) for i, (a, b) in enumerate(gathered)]
    for u in range(3):
        columns = slice(u * 512, (u + 1) * 512)
        stores.append(pltpu.make_async_copy(qkv_ref.at[:, columns], qkv_hbm.at[:, columns], qkv_sem.at[u]))
    for _, k, u, run in events[n_early:]:
        run()
        if k < 4:
            continue
        u -= 1
        if u >= 0:
            stores[u].start()
        if u < 0:
            load.wait()
            bias_ref[...] = bw_ref[...].reshape(512, 128).astype(F32).T[:8]
        elif u < 3:

            @pl.loop(0, tokens // 512)
            def _(b, u=u):
                rows = pl.ds(pl.multiple_of(b * 512, 512), 512)
                y = mm(tok_ref[rows, :], jw_ref[u].reshape(512, 512))
                if u == 0:
                    y = y + bias_ref[6:7, :]
                if u == 2:
                    y = y + bias_ref[7:8, :]
                qkv_ref[rows, u * 512 : (u + 1) * 512] = y.astype(BF)

            stores[len(gathered) + u].start()

    for job in jobs:
        job.finish()
    for store in stores:
        store.wait()


def first(nz, tok, joint, mix, lift, drop, biases, seg):
    tokens = tok.shape[0]
    vmem = pl.BlockSpec(memory_space=pltpu.VMEM)
    hbm = pl.BlockSpec(memory_space=pl.ANY)
    unit = (nz, 2, 2, 2, 16, 512)
    return pl.pallas_call(
        functools.partial(first_kernel, nz),
        in_specs=[hbm] + [vmem] * 9,
        out_specs=[hbm] * 4 + [vmem] * 3,
        out_shape=[
            jax.ShapeDtypeStruct((tokens, 1536), BF),
            jax.ShapeDtypeStruct((3,) + unit, BF),
            jax.ShapeDtypeStruct(unit, BF),
            jax.ShapeDtypeStruct((EARLY,) + unit, BF),
            jax.ShapeDtypeStruct((drop.shape[0] // 8 - EARLY, 16, 512), BF),
            jax.ShapeDtypeStruct((8, 512), F32),
            jax.ShapeDtypeStruct((seg.shape[0], 128), jnp.int32),
        ],
        scratch_shapes=[
            pltpu.VMEM(tok.shape, BF),
            pltpu.VMEM((tokens, 1536), BF),
            pltpu.VMEM((3,) + unit, BF),
            pltpu.VMEM(unit, BF),
            pltpu.VMEM((EARLY,) + unit, BF),
            pltpu.VMEM((nz, 2, 2, 2, 16, 128), BF),
            pltpu.VMEM((128, 128), F32),
            pltpu.SemaphoreType.DMA,
            pltpu.SemaphoreType.DMA((3,)),
            pltpu.SemaphoreType.DMA((4 + EARLY,)),
        ]
        + sems(5 + EARLY, nz),
        compiler_params=pltpu.CompilerParams(vmem_limit_bytes=VMEM_LIMIT, collective_id=1, has_side_effects=True),
        name="gather_joint",
    )(tok, joint, mix, lift, drop, *biases, seg)


def middle_kernel(
    nz,
    tb,
    tok_hbm,
    ctx_hbm,
    cot_hbm,
    mix_ref,
    early_ref,
    late_ref,
    bias_ref,
    out_hbm,
    gmid_hbm,
    gctx_hbm,
    gmix_ref,
    gbias_ref,
    kept_ref,
    grad_ref,
    tok_ref,
    ctx_ref,
    cot_ref,
    out_ref,
    gmid_ref,
    gctx_ref,
    in_sem,
    out_sem,
    kept_sem,
    w_ref,
    hid_ref,
    hidt_ref,
    cott_ref,
    acc_ref,
    act_ref,
    gl_ref,
    gdt_ref,
    sum_ref,
    load_sem,
    gsend,
    grecv,
    rsend,
    rrecv,
    *bufs,
):
    me = Place(nz)
    tokens, width = tok_ref.shape
    nf = w_ref.shape[0] // 2
    nb = tokens // tb
    early = early_ref.shape[0]

    def moves(pairs, sem, b):
        rows = pl.ds(b * tb, tb)
        return [pltpu.make_async_copy(x.at[rows], y.at[rows], sem.at[i, b]) for i, (x, y) in enumerate(pairs)]

    ins = ((tok_hbm, tok_ref), (ctx_hbm, ctx_ref), (cot_hbm, cot_ref))
    outs = ((out_ref, out_hbm), (gmid_ref, gmid_hbm), (gctx_ref, gctx_hbm))
    for b in range(nb):
        for move in moves(ins, in_sem, b):
            move.start()
    load = pltpu.make_async_copy(early_ref, w_ref.at[0:early], load_sem)
    load.start()
    for u in range(early, 2 * nf):
        w_ref[u, me.z, me.y, me.x, me.c] = late_ref[u - early]
    ones = jnp.ones((16, tb), BF)

    late = [Gather(me, w_ref.at[u], gsend, grecv, u - early) for u in range(early, 2 * nf)]

    def gather_step(k):
        for job in late:
            (job.start, job.step1, job.step2, job.step3, job.step4)[k]()

    def reduces(f):
        return [Reduce(me, bufs, 2 * f + i, rsend, rrecv) for i in range(2)]

    me.greet()
    gather_step(0)

    for b in range(nb):
        for move in moves(ins, in_sem, b):
            move.wait()
        rows = pl.ds(b * tb, tb)
        mid = tok_ref[rows, :].astype(F32) + mm(ctx_ref[rows, :], mix_ref[...]) + bias_ref[5:6, :]
        acc_ref[rows, :] = mid + bias_ref[4:5, :]
        h = mid.astype(BF)
        hid_ref[rows, :] = h
        hidt_ref[0:width, rows] = h.T
        hidt_ref[width : width + 16, rows] = ones
        c = cot_ref[rows, :]
        cott_ref[:, rows] = c.T
        gmid_ref[rows, :] = c.astype(F32)

    gbias_ref[...] = jnp.zeros_like(gbias_ref)
    load.wait()

    def stage1(f, b):
        rows = pl.ds(b * tb, tb)
        lw = w_ref[2 * f].reshape(512, 512)
        dw = w_ref[2 * f + 1].reshape(512, 512)
        for n in range(0, 512, 256):
            x = mm(hid_ref[rows, :], lw[:, n : n + 256]) + bias_ref[pl.ds(f, 1), n : n + 256]
            grad = mm(cot_ref[rows, :], dw[n : n + 256, :], NT)
            a, g = gelu_pair(x, grad)
            act_ref[b, :, n : n + 256] = a
            gl_ref[b, :, n : n + 256] = g

    def stage2(f, b):
        slot = f % 2
        rows = pl.ds(b * tb, tb)
        act = act_ref[b]
        gl = gl_ref[b]
        acc_ref[rows, :] += mm(act, w_ref[2 * f + 1].reshape(512, 512))
        gmid_ref[rows, :] += mm(gl, w_ref[2 * f].reshape(512, 512), NT)
        gd = mm(cott_ref[:, rows], act)
        gf = mm(hidt_ref[:, rows], gl)
        unit = gf[:width].reshape(nz, 2, 2, 2, 16, 512)
        if b == 0:
            gdt_ref[...] = gd
            sum_ref[slot, 0] = unit
        elif b < nb - 1:
            gdt_ref[...] += gd
            sum_ref[slot, 0] += unit
        else:
            sum_ref[slot, 1] = (gdt_ref[...] + gd).T.reshape(nz, 2, 2, 2, 16, 512)
            sum_ref[slot, 0] += unit
        gbias_ref[pl.ds(f, 1), :] += gf[width : width + 1]

    def due(k):
        return [((d - k) // nb, step) for step, d in enumerate(REDUCE_AT) if d % nb == k][::-1]

    def reduce_step(f, k):
        slot = f % 2
        for i, job in enumerate(reduces(f)):
            if k == 0:
                job.start(sum_ref.at[slot, i])
            elif k == 1:
                job.step1(sum_ref.at[slot, i])
            elif k == 2:
                job.step2()
            elif k == 3:
                job.step3()
            else:
                grad_ref[2 * f + i] = job.step4()

    @pl.loop(0, nf)
    def _(f):
        for k in range(nb):
            for at, step in GATHER_AT:
                if at % nb == k:

                    @pl.when(f == at // nb)
                    def _(step=step):
                        gather_step(step)


            for back, step in due(k):

                @pl.when(f > back)
                def _(back=back, step=step):
                    reduce_step(f - 1 - back, step)

            stage1(f, k)
            if k > 0:
                stage2(f, k - 1)
        stage2(f, nb - 1)

    keep = pltpu.make_async_copy(sum_ref.at[(nf - 1) % 2], kept_ref, kept_sem)
    keep.start()
    gmix_ref[...] = jnp.zeros_like(gmix_ref)
    for b in range(nb):
        for back, step in due(b):
            if back > 0:
                reduce_step(nf - 1 - back, step)
        rows = pl.ds(b * tb, tb)
        out_ref[rows, :] = acc_ref[rows, :].astype(BF)
        gb = gmid_ref[rows, :].astype(BF)
        gctx_ref[rows, :] = mm(gb, mix_ref[...], NT).astype(BF)
        gmix_ref[...] += mm(ctx_ref[rows, :].T, gb)
        gbias_ref[5:6, :] += mm(ones, gb)[0:1]
        gbias_ref[4:5, :] += mm(ones, cot_ref[rows, :])[0:1]
        for move in moves(outs, out_sem, b):
            move.start()
    for more in range(1, 4):
        for b in range(nb):
            for back, step in due(b):
                if back > more and nf - 1 - back + more < nf - 1:
                    reduce_step(nf - 1 - back + more, step)
    keep.wait()
    for b in range(nb):
        for move in moves(outs, out_sem, b):
            move.wait()
    for job in late:
        job.finish()
    for f in range(nf - 1):
        for job in reduces(f):
            job.finish()


def middle(nz, tok, ctx, cot, mix, early, late, bias):
    tokens, width = tok.shape
    n = early.shape[0] + late.shape[0]
    tb = tokens // 4
    vmem = pl.BlockSpec(memory_space=pltpu.VMEM)
    hbm = pl.BlockSpec(memory_space=pl.ANY)
    return pl.pallas_call(
        functools.partial(middle_kernel, nz, tb),
        in_specs=[hbm] * 3 + [vmem, hbm, vmem, vmem],
        out_specs=[hbm] * 3 + [vmem, vmem, hbm, vmem],
        out_shape=[
            jax.ShapeDtypeStruct((tokens, width), BF),
            jax.ShapeDtypeStruct((tokens, width), F32),
            jax.ShapeDtypeStruct((tokens, width), BF),
            jax.ShapeDtypeStruct((width, width), F32),
            jax.ShapeDtypeStruct((8, 512), F32),
            jax.ShapeDtypeStruct((2, nz, 2, 2, 2, 16, 512), F32),
            jax.ShapeDtypeStruct((n - 2, 16, 512), F32),
        ],
        scratch_shapes=[
            pltpu.VMEM((tokens, width), BF),
            pltpu.VMEM((tokens, width), BF),
            pltpu.VMEM((tokens, width), BF),
            pltpu.VMEM((tokens, width), BF),
            pltpu.VMEM((tokens, width), F32),
            pltpu.VMEM((tokens, width), BF),
            pltpu.SemaphoreType.DMA((3, 4)),
            pltpu.SemaphoreType.DMA((3, 4)),
            pltpu.SemaphoreType.DMA,
            pltpu.VMEM((n, nz, 2, 2, 2, 16, 512), BF),
            pltpu.VMEM((tokens, width), BF),
            pltpu.VMEM((width + 16, tokens), BF),
            pltpu.VMEM((width, tokens), BF),
            pltpu.VMEM((tokens, width), F32),
            pltpu.VMEM((4, tb, 512), BF),
            pltpu.VMEM((4, tb, 512), BF),
            pltpu.VMEM((width, 512), F32),
            pltpu.VMEM((2, 2, nz, 2, 2, 2, 16, 512), F32),
            pltpu.SemaphoreType.DMA,
        ]
        + sems(late.shape[0], nz)
        + sems(n - 2, nz)
        + reduce_bufs(n - 2, nz, 512),
        compiler_params=pltpu.CompilerParams(vmem_limit_bytes=VMEM_LIMIT, collective_id=2, has_side_effects=True),
        name="feed",
    )(tok, ctx, cot, mix, early, late, bias)


def last_kernel(
    nz,
    tok_hbm,
    gj_hbm,
    gmix_ref,
    gbias_ref,
    kept_ref,
    grad_ref,
    joint_ref,
    mix_ref,
    obias_ref,
    glift_ref,
    gdrop_ref,
    tok_ref,
    gj_ref,
    tok_sem,
    gj_sem,
    tokt_ref,
    sum_ref,
    bsum_ref,
    brow_ref,
    send,
    recv,
    bsend,
    brecv,
    *bufs,
):
    me = Place(nz)
    tokens, width = tok_ref.shape
    tok_load = pltpu.make_async_copy(tok_hbm, tok_ref, tok_sem)
    tok_load.start()
    gj_loads = []
    for u in range(3):
        columns = slice(u * 512, (u + 1) * 512)
        gj_loads.append(pltpu.make_async_copy(gj_hbm.at[:, columns], gj_ref.at[:, columns], gj_sem.at[u]))
        gj_loads[u].start()
    n = 7
    nf = glift_ref.shape[1] // 512
    me.greet()
    jobs = [Reduce(me, bufs[:9], u, send, recv) for u in range(n - 1)] + [Reduce(me, bufs[9:], 0, bsend, brecv)]
    units = [kept_ref.at[0], kept_ref.at[1], gmix_ref] + [sum_ref.at[j] for j in range(3)] + [bsum_ref]

    def begin(u):
        if u == n - 1:
            bsum_ref[...] = brow_ref[...].T.reshape(nz, 2, 2, 2, 16, 128)
        elif u > 2:
            gj_loads[u - 3].wait()
            if u == 3:
                tok_load.wait()

                @pl.loop(0, tokens // 512)
                def _(b):
                    rows = pl.ds(pl.multiple_of(b * 512, 512), 512)
                    tokt_ref[0:width, rows] = tok_ref[rows, :].T
                    tokt_ref[width : width + 16, rows] = jnp.ones((16, 512), BF)

                brow_ref[...] = jnp.zeros_like(brow_ref)
                brow_ref[0:8, :] = gbias_ref[...]
            g = mm(tokt_ref[...], gj_ref[:, (u - 3) * 512 : (u - 2) * 512])
            sum_ref[u - 3] = g[:width].reshape(nz, 2, 2, 2, 16, 512)
            if u != 4:
                at = 6 + (u - 3) // 2
                brow_ref[at : at + 1, :] = g[width : width + 1]
        jobs[u].start(units[u])

    def put_lift(last):
        g = jnp.concatenate(
            [
                jnp.concatenate(
                    [grad_ref[2 * f, :, 128 * u : 128 * u + 128] for f in range(nf - 1)]
                    + [last[:, 128 * u : 128 * u + 128]],
                    axis=1,
                )
                for u in range(nf)
            ],
            axis=0,
        )
        order = unit_order()
        high = g.astype(BF)
        rest = g - high.astype(F32)
        part = rest.astype(BF)
        low = (rest - part.astype(F32)).astype(BF)
        g = mm(high, order, NT) + mm(part, order, NT) + mm(low, order, NT)
        for u in range(nf):
            glift_ref[:, 512 * u : 512 * u + 512] = g[16 * u : 16 * u + 16]

    def end(u):
        total = jobs[u].step4()
        if u == 0:
            put_lift(total)
        elif u == 1:
            for f in range(nf - 1):
                gdrop_ref[16 * f : 16 * f + 16, :] = grad_ref[2 * f + 1]
            gdrop_ref[16 * nf - 16 : 16 * nf, :] = total
        elif u == 2:
            mix_ref[...] = total
        elif u < n - 1:
            joint_ref[:, (u - 3) * 512 : (u - 2) * 512] = total
        else:
            obias_ref[...] = jnp.concatenate([total, jnp.zeros((112, 128), F32)], axis=0).T[:8]

    def run(u, k):
        if k == 0:
            begin(u)
        elif k == 1:
            jobs[u].step1(units[u])
        elif k == 2:
            jobs[u].step2()
        elif k == 3:
            jobs[u].step3()
        else:
            end(u)

    events = [(2 * u + when, k, u) for u in range(n) for k, when in enumerate(REDUCE_TICKS)]
    for _, k, u in sorted(events, key=lambda e: (e[0], -e[1])):
        run(u, k)
    for job in jobs:
        job.finish()


def last(nz, tok, gj, gmix, gbias, kept, grads):
    tokens, width = tok.shape
    n = grads.shape[0] + 2
    vmem = pl.BlockSpec(memory_space=pltpu.VMEM)
    hbm = pl.BlockSpec(memory_space=pl.ANY)
    return pl.pallas_call(
        functools.partial(last_kernel, nz),
        in_specs=[hbm] * 2 + [vmem] * 4,
        out_specs=[vmem] * 5,
        out_shape=[
            jax.ShapeDtypeStruct((16, 1536), F32),
            jax.ShapeDtypeStruct((16, 512), F32),
            jax.ShapeDtypeStruct((8, 128), F32),
            jax.ShapeDtypeStruct((16, n // 2 * 512), F32),
            jax.ShapeDtypeStruct((n // 2 * 16, 512), F32),
        ],
        scratch_shapes=[
            pltpu.VMEM((tokens, width), BF),
            pltpu.VMEM((tokens, 3 * width), BF),
            pltpu.SemaphoreType.DMA,
            pltpu.SemaphoreType.DMA((3,)),
            pltpu.VMEM((width + 16, tokens), BF),
            pltpu.VMEM((3, nz, 2, 2, 2, 16, 512), F32),
            pltpu.VMEM((nz, 2, 2, 2, 16, 128), F32),
            pltpu.VMEM((128, 512), F32),
        ]
        + sems(6, nz)
        + sems(1, nz)
        + reduce_bufs(6, nz, 512)
        + reduce_bufs(1, nz, 128),
        compiler_params=pltpu.CompilerParams(vmem_limit_bytes=VMEM_LIMIT, collective_id=3, has_side_effects=True),
        name="joint_grads",
    )(tok, gj, gmix.reshape(nz, 2, 2, 2, 16, 512), gbias, kept, grads)


def hand_out_kernel(*refs):
    half = (len(refs) - 5) // 2
    bias_ref = refs[half]
    outs = refs[half + 1 :]
    for a, b in zip(refs[:half], outs):
        b[...] = a[...]
    lift_ref, drop_ref, mix_ref, joint_ref = outs[half:]
    rows = bias_ref[...]
    nf = lift_ref.shape[1] // 16
    lane = lax.broadcasted_iota(jnp.int32, (1, 128), 1)
    line = rows[0:1]
    for f in range(1, nf):
        line = jnp.where(lane // 16 == f, pltpu.roll(rows[f : f + 1], 16 * f, 1), line)
    lift_ref[...] = line[:, : lift_ref.shape[1]]
    drop_ref[...] = rows[4:5, 0:16]
    mix_ref[...] = rows[5:6, 0:16]
    joint_ref[...] = rows[6:8, 0:16]


def hand_out(arrays, bias_rows, nf):
    vmem = pl.BlockSpec(memory_space=pltpu.VMEM)
    shapes = [a.shape for a in arrays] + [(1, 16 * nf), (1, 16), (1, 16), (2, 16)]
    return pl.pallas_call(
        hand_out_kernel,
        in_specs=[vmem] * (len(arrays) + 1),
        out_specs=[vmem] * len(shapes),
        out_shape=[jax.ShapeDtypeStruct(s, F32) for s in shapes],
        name="hand_out",
    )(*arrays, bias_rows)


def remote_body(
    tokens,
    segment_ids,
    fill_lengths,
    joint_weight,
    joint_bias,
    mix_weight,
    mix_bias,
    lift_weight,
    lift_bias,
    drop_weight,
    drop_bias,
    cotangent,
):
    rows, length, width = tokens.shape
    nz = lax.axis_size("gx")
    n_tok = rows * length
    tok = tokens.reshape(n_tok, width)
    nf = drop_weight.shape[0] // 16
    biases = (lift_bias[None], drop_bias[None], mix_bias[None], joint_bias)
    qkv, joint_w, mix_w, early, late, bias, starts = first(
        nz, tok, joint_weight, mix_weight, lift_weight, drop_weight, biases, segment_ids
    )
    qkv3 = qkv.reshape(rows, length, 3 * width)
    ctx, lse = attend(starts, fill_lengths, segment_ids, qkv3)
    out, gmid, gctx, gmix, gbias, kept, grads = middle(
        nz, tok, ctx.reshape(n_tok, width), cotangent.reshape(n_tok, width), mix_w.reshape(width, width), early, late, bias
    )
    gjoint, token_grad, out = attend_back(
        starts,
        fill_lengths,
        segment_ids,
        qkv3,
        lse,
        ctx,
        gctx.reshape(rows, length, width),
        gmid.reshape(rows, length, width),
        joint_w.reshape(3, width, width),
        out.reshape(rows, length, width),
    )
    gj, gm, gb, glift, gdrop = last(nz, tok, gjoint.reshape(n_tok, 3 * width), gmix, gbias, kept, grads)
    gj, gm, glift, gdrop, blift, bdrop, bmix, bjoint = hand_out((gj, gm, glift, gdrop), gb, nf)
    return (out, token_grad, gj, bjoint, gm, bmix[0], glift, blift[0], gdrop, bdrop[0])


BOTH = ("gx", "gy")


def body(
    tokens,
    segment_ids,
    fill_lengths,
    joint_weight,
    joint_bias,
    mix_weight,
    mix_bias,
    lift_weight,
    lift_bias,
    drop_weight,
    drop_bias,
    cotangent,
):
    rows, length, width = tokens.shape
    n_tok = rows * length
    tok = tokens.reshape(n_tok, width)
    cot = cotangent.reshape(n_tok, width)
    starts = jnp.sum(
        segment_ids[:, None, :] < jnp.arange(128, dtype=jnp.int32)[None, :, None], axis=-1, dtype=jnp.int32
    )

    joint_w = lax.all_gather(joint_weight, BOTH, axis=0, tiled=True)
    mix_w = lax.all_gather(mix_weight, BOTH, axis=0, tiled=True)
    lift_w = lax.all_gather(lift_weight, BOTH, axis=0, tiled=True)
    drop_w = lax.all_gather(drop_weight, BOTH, axis=0, tiled=True)
    own_bias = jnp.concatenate([joint_bias.reshape(-1), mix_bias, lift_bias, drop_bias])
    sizes = [joint_bias.shape[1], joint_bias.shape[1], mix_bias.size, lift_bias.size, drop_bias.size]
    all_bias = lax.all_gather(own_bias, BOTH, axis=0)
    parts, at = [], 0
    for size in sizes:
        parts.append(all_bias[:, at : at + size].reshape(-1).astype(F32))
        at += size
    bq, bv, bm, bl, bd = parts
    nf = bl.size // 512
    bias = jnp.concatenate(
        [jnp.concatenate([bl.reshape(nf, 512), jnp.zeros((4 - nf, 512), F32)]), bd[None], bm[None], bq[None], bv[None]]
    )

    shift = jnp.concatenate([bq, jnp.zeros_like(bq), bv])
    qkv = (mm(tok, joint_w) + shift).astype(BF)
    qkv3 = qkv.reshape(rows, length, 3 * width)
    ctx, lse = attend(starts, fill_lengths, segment_ids, qkv3)
    lift_units = lift_w.reshape(width, nf, 512).transpose(1, 0, 2)
    out, gmid, gctx, glift, gdrop, gmix, gbias = feed(
        tok, ctx.reshape(n_tok, width), cot, mix_w, lift_units, drop_w.reshape(nf, 512, width), bias
    )
    gjoint, token_grad, out = attend_back(
        starts,
        fill_lengths,
        segment_ids,
        qkv3,
        lse,
        ctx,
        gctx.reshape(rows, length, width),
        gmid.reshape(rows, length, width),
        joint_w.reshape(width, 3, width).transpose(1, 0, 2),
        out.reshape(rows, length, width),
    )
    gjoint = gjoint.reshape(n_tok, 3 * width)
    gjoint_w = lax.dot_general(tok, gjoint, (((0,), (0,)), ((), ())), preferred_element_type=F32)
    sums = jnp.sum(gjoint.astype(F32), axis=0)

    glift_w = glift[:, :width].transpose(1, 0, 2).reshape(width, nf * 512)
    gdrop_w = gdrop.transpose(0, 2, 1).reshape(nf * 512, width)
    scatter = functools.partial(lax.psum_scatter, axis_name=BOTH, scatter_dimension=0, tiled=True)
    n_dev = all_bias.shape[0]
    packed = jnp.concatenate(
        [
            g.reshape(n_dev, -1)
            for g in (sums[:width], sums[2 * width :], gbias[5], gbias[:nf].reshape(-1), gbias[4])
        ],
        axis=1,
    )
    own = scatter(packed)[0]
    cuts, at = [], 0
    for size in sizes:
        cuts.append(own[at : at + size])
        at += size
    return (
        out,
        token_grad,
        scatter(gjoint_w),
        jnp.stack([cuts[0], cuts[1]]),
        scatter(gmix),
        cuts[2],
        scatter(glift_w),
        cuts[3],
        scatter(gdrop_w),
        cuts[4],
    )


def solution(mesh):
    wide = P(BOTH, None, None)
    rows = P(BOTH, None)
    flat = P(BOTH)
    bias = P(None, BOTH)
    in_specs = (wide, rows, flat, rows, bias, rows, flat, rows, flat, rows, flat, wide)
    out_specs = (wide, wide, rows, bias, rows, flat, rows, flat, rows, flat)
    fits = mesh.shape["gy"] == 8 and mesh.shape["gx"] == 4
    return jax.shard_map(remote_body if fits else body, mesh=mesh, in_specs=in_specs, out_specs=out_specs, check_vma=False)
```

```python
import functools
import math

import jax
import jax.numpy as jnp
from jax import lax
from jax.experimental import pallas as pl
from jax.experimental.pallas import tpu as pltpu
from jax.sharding import PartitionSpec as P

BF = jnp.bfloat16
F32 = jnp.float32
NT = (((1,), (1,)), ((), ()))
NN = (((1,), (0,)), ((), ()))
NEG = -float(2**30)
C0 = math.sqrt(2.0 / math.pi)
C1 = 0.044715
WIDE = 5
CUT = 2
VMEM_LIMIT = 60 * 2**20


def mm(a, b, dims=NN):
    return lax.dot_general(a, b, dims, preferred_element_type=F32)


def lane(p, base):
    at = base + p * 128
    return pl.ds(at if isinstance(at, int) else pl.multiple_of(at, 128), 128)


def split_heads(x):
    lane = lax.broadcasted_iota(jnp.int32, x.shape, 1)
    zero = jnp.zeros_like(x)
    return jnp.concatenate([jnp.where(lane < 64, x, zero), jnp.where(lane < 64, zero, x)], axis=0)


def diag_blocks(y):
    return jnp.concatenate([y[:64, :128], y[64:, 128:]], axis=0)


def window(starts_ref, fill_ref, row, t, length):
    first = t * 128
    last = first + 127
    fill = fill_ref[row]
    lo = jnp.int32(0)
    hi = jnp.int32(length)
    for v in range(1, 6):
        s = starts_ref[row, v]
        lo = jnp.where(s <= first, jnp.maximum(lo, s), lo)
        hi = jnp.where(s > last, jnp.minimum(hi, s), hi)
    hi = jnp.minimum(hi, fill)
    alone = lo >= fill
    hi = jnp.where(last >= fill, jnp.maximum(hi, last + 1), hi)
    lo = jnp.where(alone, first, lo)
    lo_b = lo // 128
    return lo_b, (hi + 127) // 128 - lo_b


def ids_of(seg_ref, row, lanes):
    ids = seg_ref[:, lanes]
    mine = lax.broadcasted_iota(jnp.int32, ids.shape, 0) == row
    return jnp.sum(jnp.where(mine, ids.astype(F32), 0.0), axis=0, keepdims=True)


def write_mask(mask_ref, segk_ref, seg_ref, row, fill, t, lo_b, n):
    segq = ids_of(seg_ref, row, pl.ds(pl.multiple_of(t * 128, 128), 128))
    segq = jnp.broadcast_to(segq, (128, 128))
    qi = t * 128 + lax.broadcasted_iota(jnp.int32, (128, 128), 1)
    ki0 = lax.broadcasted_iota(jnp.int32, (128, 128), 0)
    for c in range(n):
        off = pl.multiple_of((lo_b + c) * 128, 128)
        ki = ki0 + off
        ok = ((segk_ref[pl.ds(off, 128), :] == segq) & (ki < fill)) | (ki == qi)
        mask_ref[c * 128 : (c + 1) * 128, :] = jnp.where(ok, 0.0, NEG)


def spread_segments(seg_ref, segk_ref, row, length):
    for b in range(length // 128):
        ids = ids_of(seg_ref, row, slice(b * 128, (b + 1) * 128))
        segk_ref[b * 128 : (b + 1) * 128, :] = jnp.broadcast_to(ids, (128, 128)).T


def attend_kernel(
    starts_ref, fill_ref, seg_ref, qkv_ref, ctx_ref, lse_ref, vt_ref, segk_ref, mask_ref, s_ref, p_ref, *, length
):
    row = pl.program_id(0)
    fill = fill_ref[row]
    spread_segments(seg_ref, segk_ref, row, length)
    for b in range(length // 128):
        for p in range(4):
            v = qkv_ref[0, b * 128 : (b + 1) * 128, 1024 + p * 128 : 1024 + (p + 1) * 128]
            vt_ref[p * 128 : (p + 1) * 128, b * 128 : (b + 1) * 128] = v.T

    def tile(t, lo_b, n):
        tq = pl.ds(pl.multiple_of(t * 128, 128), 128)
        win = pl.ds(pl.multiple_of(lo_b * 128, 128), n * 128)
        cuts = [(c, min(CUT, n - c)) for c in range(0, n, CUT)]
        tops, sums = [], []
        for p in range(4):
            lanes = slice(p * 128, (p + 1) * 128)
            qbd = split_heads(qkv_ref[0, tq, lanes] * jnp.asarray(0.125, BF))
            top = None
            for c, w in cuts:
                rows = pl.ds(pl.multiple_of((lo_b + c) * 128, 128), w * 128)
                s = mm(qkv_ref[0, rows, 512 + p * 128 : 512 + (p + 1) * 128], qbd, NT)
                mask = mask_ref[c * 128 : (c + w) * 128, :]
                s = s + jnp.concatenate([mask, mask], axis=1)
                s_ref[p, c * 128 : (c + w) * 128, :] = s
                part = jnp.max(s.reshape(w * 16, 8, 256), axis=0)
                top = part if top is None else jnp.maximum(top, part)
            tops.append(jnp.max(top, axis=0, keepdims=True))
        for p in range(4):
            total = None
            for c, w in cuts:
                e = jnp.exp(s_ref[p, c * 128 : (c + w) * 128, :] - tops[p])
                p_ref[p, c * 128 : (c + w) * 128, :] = e.astype(BF)
                part = jnp.sum(e.reshape(w * 16, 8, 256), axis=0)
                total = part if total is None else total + part
            sums.append(jnp.sum(total, axis=0, keepdims=True))
        for p in range(4):
            o = mm(vt_ref[p * 128 : (p + 1) * 128, win], p_ref[p, : n * 128, :]) * (1.0 / sums[p])
            ctx_ref[0, tq, p * 128 : (p + 1) * 128] = diag_blocks(o).T.astype(BF)
            lse_ref[0, p, pl.ds(t, 1), :] = tops[p] + jnp.log(sums[p])

    @pl.loop(0, length // 128)
    def _(t):
        lo_b, n = window(starts_ref, fill_ref, row, t, length)
        for k in range(1, length // 128 + 1):

            @pl.when(n == k)
            def _(k=k):
                write_mask(mask_ref, segk_ref, seg_ref, row, fill, t, lo_b, k)
                tile(t, lo_b, k)


def attend(starts, fill, seg, qkv):
    rows, length, _ = qkv.shape
    blocks = length // 128
    return pl.pallas_call(
        functools.partial(attend_kernel, length=length),
        grid_spec=pltpu.PrefetchScalarGridSpec(
            num_scalar_prefetch=2,
            grid=(rows,),
            in_specs=[
                pl.BlockSpec((rows, length), lambda r, *_: (0, 0)),
                pl.BlockSpec((1, length, 1536), lambda r, *_: (r, 0, 0)),
            ],
            out_specs=[
                pl.BlockSpec((1, length, 512), lambda r, *_: (r, 0, 0)),
                pl.BlockSpec((1, 4, blocks, 256), lambda r, *_: (r, 0, 0, 0)),
            ],
            scratch_shapes=[
                pltpu.VMEM((512, length), BF),
                pltpu.VMEM((length, 128), F32),
                pltpu.VMEM((length, 128), F32),
                pltpu.VMEM((4, length, 256), F32),
                pltpu.VMEM((4, length, 256), BF),
            ],
        ),
        out_shape=[
            jax.ShapeDtypeStruct((rows, length, 512), BF),
            jax.ShapeDtypeStruct((rows, 4, blocks, 256), F32),
        ],
        compiler_params=pltpu.CompilerParams(vmem_limit_bytes=VMEM_LIMIT),
        name="attend",
    )(starts, fill, seg, qkv)


def attend_back_kernel(
    starts_ref,
    fill_ref,
    seg_ref,
    qkv_ref,
    lse_ref,
    ctx_ref,
    do_ref,
    gmid_hbm,
    jw_hbm,
    pass_hbm,
    out_ref,
    tg_ref,
    to_hbm,
    gmid_ref,
    jw_ref,
    pass_ref,
    late_sem,
    kt_ref,
    segk_ref,
    mask_ref,
    dk_ref,
    dv_ref,
    p_ref,
    ds_ref,
    *,
    length,
):
    row = pl.program_id(0)
    fill = fill_ref[row]
    gmid_load = pltpu.make_async_copy(gmid_hbm.at[row], gmid_ref, late_sem.at[0])
    jw_load = pltpu.make_async_copy(jw_hbm, jw_ref, late_sem.at[1])
    pass_load = pltpu.make_async_copy(pass_hbm.at[row], pass_ref, late_sem.at[2])
    pass_store = pltpu.make_async_copy(pass_ref, to_hbm.at[row], late_sem.at[3])
    gmid_load.start()
    jw_load.start()
    pass_load.start()
    spread_segments(seg_ref, segk_ref, row, length)
    for b in range(length // 128):
        for p in range(4):
            k = qkv_ref[0, b * 128 : (b + 1) * 128, 512 + p * 128 : 512 + (p + 1) * 128]
            kt_ref[p * 128 : (p + 1) * 128, b * 128 : (b + 1) * 128] = k.T
    dk_ref[...] = jnp.zeros_like(dk_ref)
    dv_ref[...] = jnp.zeros_like(dv_ref)

    def tile(t, lo_b, n):
        tq = pl.ds(pl.multiple_of(t * 128, 128), 128)
        win = pl.ds(pl.multiple_of(lo_b * 128, 128), n * 128)

        def some(pairs):
            ready = []
            for i, p in enumerate(pairs):
                lanes = lane(p, 0)
                qbd = split_heads(qkv_ref[0, tq, lanes] * jnp.asarray(0.125, BF))
                do = do_ref[0, tq, lanes]
                prod = (do.astype(F32) * ctx_ref[0, tq, lanes].astype(F32)).T
                delta = jnp.concatenate(
                    [jnp.sum(prod[:64], axis=0, keepdims=True), jnp.sum(prod[64:], axis=0, keepdims=True)], axis=1
                )
                ready.append((qbd, split_heads(do), delta, lse_ref[0, p, pl.ds(t, 1), :]))
            for c in range(0, n, CUT):
                w = min(CUT, n - c)
                rows = pl.ds(pl.multiple_of((lo_b + c) * 128, 128), w * 128)
                here = slice(c * 128, (c + w) * 128)
                for i, p in enumerate(pairs):
                    qbd, dobd, delta, lse = ready[i]
                    s = mm(qkv_ref[0, rows, lane(p, 512)], qbd, NT)
                    dp = mm(qkv_ref[0, rows, lane(p, 1024)], dobd, NT)
                    mask = mask_ref[here, :]
                    e = jnp.exp(s + jnp.concatenate([mask, mask], axis=1) - lse)
                    p_ref[p, here, :] = e.astype(BF)
                    ds_ref[p, here, :] = (e * (dp - delta)).astype(BF)
                for i, p in enumerate(pairs):
                    qbd, dobd, _, _ = ready[i]
                    lanes = lane(p, 0)
                    dv_ref[rows, lanes] += mm(p_ref[p, here, :], dobd)
                    dk_ref[rows, lanes] += mm(ds_ref[p, here, :], qbd)
            for i, p in enumerate(pairs):
                lanes = lane(p, 0)
                dq = mm(kt_ref[lanes, win], ds_ref[p, : n * 128, :])
                out_ref[0, tq, lanes] = (diag_blocks(dq) * 0.125).T.astype(BF)

        if n > WIDE:

            @pl.loop(0, 2)
            def _(g):
                some([2 * g, 2 * g + 1])

        else:
            some(range(4))

    @pl.loop(0, length // 128)
    def _(t):
        lo_b, n = window(starts_ref, fill_ref, row, t, length)
        for k in range(1, length // 128 + 1):

            @pl.when(n == k)
            def _(k=k):
                write_mask(mask_ref, segk_ref, seg_ref, row, fill, t, lo_b, k)
                tile(t, lo_b, k)

    pass_load.wait()
    pass_store.start()
    gmid_load.wait()
    jw_load.wait()
    for b in range(0, length, 256):
        rows = slice(b, b + 256)
        dk = dk_ref[rows, :].astype(BF)
        dv = dv_ref[rows, :].astype(BF)
        out_ref[0, rows, 512:1024] = dk
        out_ref[0, rows, 1024:1536] = dv
        total = gmid_ref[rows, :] + mm(out_ref[0, rows, 0:512], jw_ref[0], NT)
        tg_ref[0, rows, :] = total + mm(dk, jw_ref[1], NT) + mm(dv, jw_ref[2], NT)
    pass_store.wait()


def attend_back(starts, fill, seg, qkv, lse, ctx, do, gmid, joint, passed):
    rows, length, _ = qkv.shape
    blocks = length // 128
    wide = pl.BlockSpec((1, length, 512), lambda r, *_: (r, 0, 0))
    joined = pl.BlockSpec((1, length, 1536), lambda r, *_: (r, 0, 0))
    hbm = pl.BlockSpec(memory_space=pl.ANY)
    return pl.pallas_call(
        functools.partial(attend_back_kernel, length=length),
        grid_spec=pltpu.PrefetchScalarGridSpec(
            num_scalar_prefetch=2,
            grid=(rows,),
            in_specs=[
                pl.BlockSpec((rows, length), lambda r, *_: (0, 0)),
                joined,
                pl.BlockSpec((1, 4, blocks, 256), lambda r, *_: (r, 0, 0, 0)),
                wide,
                wide,
                hbm,
                hbm,
                hbm,
            ],
            out_specs=[joined, wide, hbm],
            scratch_shapes=[
                pltpu.VMEM((length, 512), F32),
                pltpu.VMEM((3, 512, 512), BF),
                pltpu.VMEM((length, 512), BF),
                pltpu.SemaphoreType.DMA((4,)),
                pltpu.VMEM((512, length), BF),
                pltpu.VMEM((length, 128), F32),
                pltpu.VMEM((length, 128), F32),
                pltpu.VMEM((length, 512), F32),
                pltpu.VMEM((length, 512), F32),
                pltpu.VMEM((4, length, 256), BF),
                pltpu.VMEM((4, length, 256), BF),
            ],
        ),
        out_shape=[
            jax.ShapeDtypeStruct((rows, length, 1536), BF),
            jax.ShapeDtypeStruct((rows, length, 512), F32),
            jax.ShapeDtypeStruct(passed.shape, passed.dtype),
        ],
        compiler_params=pltpu.CompilerParams(vmem_limit_bytes=VMEM_LIMIT),
        name="attend_back",
    )(starts, fill, seg, qkv, lse, ctx, do, gmid, joint, passed)


def gelu_pair(x, grad):
    x2 = x * x
    h = 0.5 + 0.5 * jnp.tanh(x * (C0 + (C0 * C1) * x2))
    act = x * h
    slope = h + act * (1.0 - h) * (2.0 * C0 + (6.0 * C0 * C1) * x2)
    return act.astype(BF), (grad * slope).astype(BF)


def feed_kernel(
    tok_ref,
    ctx_ref,
    cot_ref,
    mix_ref,
    lift_ref,
    drop_ref,
    bias_ref,
    out_ref,
    gmid_ref,
    gctx_ref,
    glift_ref,
    gdrop_ref,
    gmix_ref,
    gbias_ref,
    hid_ref,
    hidt_ref,
    cott_ref,
    acc_ref,
    act_ref,
    gl_ref,
    *,
    tb,
):
    tokens, width = tok_ref.shape
    nf = lift_ref.shape[0]
    nb = tokens // tb
    ones = jnp.ones((16, tb), BF)

    @pl.loop(0, nb)
    def _(b):
        rows = pl.ds(pl.multiple_of(b * tb, tb), tb)
        mid = tok_ref[rows, :].astype(F32) + mm(ctx_ref[rows, :], mix_ref[...]) + bias_ref[5:6, :]
        acc_ref[rows, :] = mid + bias_ref[4:5, :]
        h = mid.astype(BF)
        hid_ref[rows, :] = h
        hidt_ref[0:width, rows] = h.T
        hidt_ref[width : width + 16, rows] = ones
        c = cot_ref[rows, :]
        cott_ref[:, rows] = c.T
        gmid_ref[rows, :] = c.astype(F32)

    def stage1(f, b):
        rows = pl.ds(b * tb, tb)
        for n in range(0, 512, 256):
            x = mm(hid_ref[rows, :], lift_ref[f, :, n : n + 256]) + bias_ref[pl.ds(f, 1), n : n + 256]
            grad = mm(cot_ref[rows, :], drop_ref[f, n : n + 256, :], NT)
            a, g = gelu_pair(x, grad)
            act_ref[b, :, n : n + 256] = a
            gl_ref[b, :, n : n + 256] = g

    def stage2(f, b):
        rows = pl.ds(b * tb, tb)
        act = act_ref[b]
        gl = gl_ref[b]
        acc_ref[rows, :] += mm(act, drop_ref[f])
        gmid_ref[rows, :] += mm(gl, lift_ref[f], NT)
        gd = mm(cott_ref[:, rows], act)
        gf = mm(hidt_ref[:, rows], gl)
        if b == 0:
            gdrop_ref[f] = gd
            glift_ref[f] = gf
        else:
            gdrop_ref[f] += gd
            glift_ref[f] += gf

    @pl.loop(0, nf)
    def _(f):
        stage1(f, 0)
        for b in range(1, nb):
            stage1(f, b)
            stage2(f, b - 1)
        stage2(f, nb - 1)

    gmix_ref[...] = jnp.zeros_like(gmix_ref)
    gbias_ref[...] = jnp.zeros_like(gbias_ref)

    @pl.loop(0, nb)
    def _(b):
        rows = pl.ds(pl.multiple_of(b * tb, tb), tb)
        out_ref[rows, :] = acc_ref[rows, :].astype(BF)
        gb = gmid_ref[rows, :].astype(BF)
        gctx_ref[rows, :] = mm(gb, mix_ref[...], NT).astype(BF)
        gmix_ref[...] += mm(ctx_ref[rows, :].T, gb)
        gbias_ref[5:6, :] += mm(ones, gb)[0:1]
        gbias_ref[4:5, :] += mm(ones, cot_ref[rows, :])[0:1]

    for f in range(nf):
        gbias_ref[f : f + 1, :] = glift_ref[f, width : width + 1, :]


def feed(tok, ctx, cot, mix, lift, drop, bias):
    tokens, width = tok.shape
    nf = lift.shape[0]
    tb = 512
    vmem = pl.BlockSpec(memory_space=pltpu.VMEM)
    return pl.pallas_call(
        functools.partial(feed_kernel, tb=tb),
        in_specs=[vmem] * 7,
        out_specs=[vmem] * 7,
        out_shape=[
            jax.ShapeDtypeStruct((tokens, width), BF),
            jax.ShapeDtypeStruct((tokens, width), F32),
            jax.ShapeDtypeStruct((tokens, width), BF),
            jax.ShapeDtypeStruct((nf, width + 16, 512), F32),
            jax.ShapeDtypeStruct((nf, width, 512), F32),
            jax.ShapeDtypeStruct((width, width), F32),
            jax.ShapeDtypeStruct((8, 512), F32),
        ],
        scratch_shapes=[
            pltpu.VMEM((tokens, width), BF),
            pltpu.VMEM((width + 16, tokens), BF),
            pltpu.VMEM((width, tokens), BF),
            pltpu.VMEM((tokens, width), F32),
            pltpu.VMEM((tokens // tb, tb, 512), BF),
            pltpu.VMEM((tokens // tb, tb, 512), BF),
        ],
        compiler_params=pltpu.CompilerParams(vmem_limit_bytes=VMEM_LIMIT),
        name="feed",
    )(tok, ctx, cot, mix, lift, drop, bias)


MESH = pl.DeviceIdType.MESH
GATHER_TICKS = (0, 8, 13, 18, 21)
REDUCE_TICKS = (0, 4, 11, 17, 22)
GATHER_AT = ((1, 1), (3, 2), (6, 3), (8, 4))
REDUCE_AT = (0, 2, 5, 7, 9)
SPLIT = 1
EARLY = 4


class Place:
    def __init__(self, nz):
        self.nz = nz
        self.z = lax.axis_index("gx")
        g = lax.axis_index("gy")
        self.c = g % 2
        self.x = (g // 2) % 2
        self.y = g // 4
        self.oc = 1 - self.c
        self.y1 = self.y + self.oc * (1 - 2 * self.y)
        self.x1 = self.x + self.c * (1 - 2 * self.x)
        self.y2 = self.y + self.c * (1 - 2 * self.y)
        self.x2 = self.x + self.oc * (1 - 2 * self.x)
        self.core = (self.z, self.y * 4 + self.x * 2 + self.oc)
        self.near1 = (self.z, self.y1 * 4 + self.x1 * 2 + self.c)
        self.near2 = (self.z, self.y2 * 4 + self.x2 * 2 + self.c)

    def at_z(self, z):
        return (z, self.y * 4 + self.x * 2 + self.c)

    def up(self, k):
        return (self.z + k) % self.nz

    def down(self, k):
        return (self.z + self.nz - k) % self.nz

    def greet(self):
        barrier = pltpu.get_barrier_semaphore()
        others = [self.core, self.near1, self.near2] + [self.at_z(self.up(k)) for k in range(1, self.nz)]
        for other in others:
            pl.semaphore_signal(barrier, inc=1, device_id=other, device_id_type=MESH)
        pl.semaphore_wait(barrier, len(others))


def remote(src, dst, send, recv, u, k, device):
    return pltpu.make_async_remote_copy(
        src_ref=src,
        dst_ref=dst,
        send_sem=send.at[u, k],
        recv_sem=recv.at[u, k],
        device_id=device,
        device_id_type=MESH,
    )


class Gather:
    def __init__(self, me, buf, send, recv, u):
        nz = me.nz
        own = buf.at[:, me.y, me.x, me.c]
        other = buf.at[:, me.y1, me.x1, me.c]
        mine = buf.at[me.z, me.y, me.x, me.c]
        half = buf.at[:, :, :, me.c]
        self.along_z = lambda: [remote(mine, mine, send, recv, u, k - 1, me.at_z(me.up(k))) for k in range(1, nz)]
        self.first = lambda: remote(own, own, send, recv, u, nz - 1, me.near1)
        self.second = lambda: remote(own, own, send, recv, u, nz, me.near2)
        self.passed = lambda: remote(other, other, send, recv, u, nz + 1, me.near2)
        self.core = lambda: remote(half, half, send, recv, u, nz + 2, me.core)

    def start(self):
        for copy in self.along_z():
            copy.start()

    def step1(self):
        for copy in self.along_z():
            copy.wait_recv()
        self.first().start()
        self.second().start()

    def step2(self):
        self.first().wait_recv()
        self.passed().start()

    def step3(self):
        self.second().wait_recv()
        self.passed().wait_recv()
        self.core().start()

    def step4(self):
        self.core().wait_recv()

    def finish(self):
        for copy in self.along_z() + [self.first(), self.second(), self.passed(), self.core()]:
            copy.wait_send()


class Reduce:
    def __init__(self, me, bufs, u, send, recv):
        self.me = me
        nz = me.nz
        self.sc, self.rc, self.s1, self.r1, self.s2, self.r2, self.sz, self.rz, self.hold = [b.at[u] for b in bufs]
        self.core = lambda: remote(self.sc, self.rc, send, recv, u, 0, me.core)
        self.first = lambda: remote(self.s1, self.r1, send, recv, u, 1, me.near2)
        self.second = lambda: remote(self.s2, self.r2, send, recv, u, 2, me.near1)
        self.along_z = lambda: [
            remote(self.sz.at[me.up(k)], self.rz.at[me.z], send, recv, u, 2 + k, me.at_z(me.up(k)))
            for k in range(1, nz)
        ]

    def start(self, unit):
        me = self.me
        self.sc[...] = unit[:, :, :, me.oc].astype(BF)
        self.core().start()

    def step1(self, unit):
        me = self.me
        self.core().wait_recv()

        def total(y, x):
            return unit[:, y, x, me.c] + self.rc[:, y, x].astype(F32)

        self.s1[0] = total(me.y2, me.x2).astype(BF)
        self.s1[1] = total(1 - me.y, 1 - me.x).astype(BF)
        self.first().start()
        self.hold[0] = total(me.y, me.x)
        self.hold[1] = total(me.y1, me.x1)

    def step2(self):
        self.first().wait_recv()
        self.s2[...] = (self.hold[1] + self.r1[1].astype(F32)).astype(BF)
        self.second().start()
        self.hold[0] = self.hold[0] + self.r1[0].astype(F32)

    def step3(self):
        self.second().wait_recv()
        total = self.hold[0] + self.r2[...].astype(F32)
        self.sz[...] = total.astype(BF)
        self.hold[0] = total
        for copy in self.along_z():
            copy.start()

    def step4(self):
        me = self.me
        for copy in self.along_z():
            copy.wait_recv()
        total = self.hold[0, me.z]
        for k in range(1, me.nz):
            total = total + self.rz[me.down(k)].astype(F32)
        return total

    def finish(self):
        for copy in [self.core(), self.first(), self.second()] + self.along_z():
            copy.wait_send()


def reduce_bufs(n, nz, w):
    return [
        pltpu.VMEM((n, nz, 2, 2, 16, w), BF),
        pltpu.VMEM((n, nz, 2, 2, 16, w), BF),
        pltpu.VMEM((n, 2, nz, 16, w), BF),
        pltpu.VMEM((n, 2, nz, 16, w), BF),
        pltpu.VMEM((n, nz, 16, w), BF),
        pltpu.VMEM((n, nz, 16, w), BF),
        pltpu.VMEM((n, nz, 16, w), BF),
        pltpu.VMEM((n, nz, 16, w), BF),
        pltpu.VMEM((n, 2, nz, 16, w), F32),
    ]


def sems(n, nz):
    return [pltpu.SemaphoreType.DMA((n, nz + 3)), pltpu.SemaphoreType.DMA((n, nz + 3))]


def unit_order():
    c = lax.broadcasted_iota(jnp.int32, (512, 512), 1)
    s = lax.broadcasted_iota(jnp.int32, (512, 512), 0)
    return jnp.where(s == ((c & 127) >> 4) * 64 + (c >> 7) * 16 + (c & 15), 1.0, 0.0).astype(BF)


def first_kernel(
    nz,
    tok_hbm,
    joint_ref,
    mix_own_ref,
    lift_ref,
    drop_ref,
    bl_ref,
    bd_ref,
    bm_ref,
    bj_ref,
    seg_ref,
    qkv_hbm,
    jw_hbm,
    mix_hbm,
    early_hbm,
    late_own_ref,
    bias_ref,
    starts_ref,
    tok_ref,
    qkv_ref,
    jw_ref,
    mix_ref,
    early_ref,
    bw_ref,
    line_ref,
    tok_sem,
    qkv_sem,
    unit_sem,
    send,
    recv,
):
    me = Place(nz)
    load = pltpu.make_async_copy(tok_hbm, tok_ref, tok_sem)
    load.start()
    tokens, width = tok_ref.shape
    early = early_ref.shape[0]
    nf = drop_ref.shape[0] // 16
    here = (me.z, me.y, me.x, me.c)
    line_ref[...] = jnp.zeros_like(line_ref)
    line_ref[0:1, 0 : 16 * nf] = bl_ref[...].astype(F32)
    line_ref[4:5, 0:16] = bd_ref[...].astype(F32)
    line_ref[5:6, 0:16] = bm_ref[...].astype(F32)
    line_ref[6:8, 0:16] = bj_ref[...].astype(F32)
    lift_line = line_ref[0:1, :]
    for f in range(1, nf):
        line_ref[f : f + 1, :] = pltpu.roll(lift_line, 128 - 16 * f, 1)
    bw_ref[here] = line_ref[...].T[:16].astype(BF)
    for u in range(3):
        jw_ref[(u,) + here] = joint_ref[:, u * 512 : (u + 1) * 512]
    mix_ref[here] = mix_own_ref[...]
    me.greet()
    jobs = [Gather(me, bw_ref, send, recv, 0)]
    jobs += [Gather(me, jw_ref.at[u], send, recv, 1 + u) for u in range(3)]
    jobs += [Gather(me, mix_ref, send, recv, 4)]
    jobs += [Gather(me, early_ref.at[u], send, recv, 5 + u) for u in range(early)]
    events = []
    for u, job in enumerate(jobs):
        for k, when in enumerate(GATHER_TICKS):
            events.append((2 * u + when, k, u, (job.start, job.step1, job.step2, job.step3, job.step4)[k]))
    events.sort(key=lambda e: (e[0], -e[1]))
    n_early = 4
    for event in events[:n_early]:
        event[3]()
    rows = jnp.concatenate([lift_ref[:, u * 512 : (u + 1) * 512] for u in range(nf)], axis=0)
    rows = mm(rows, unit_order()).astype(BF)
    for f in range(nf):
        lift = jnp.concatenate([rows[16 * u : 16 * u + 16, 128 * f : 128 * f + 128] for u in range(nf)], axis=1)
        drop = drop_ref[16 * f : 16 * f + 16, :]
        if 2 * f < early:
            early_ref[(2 * f,) + here] = lift
            early_ref[(2 * f + 1,) + here] = drop
        else:
            late_own_ref[2 * f - early] = lift
            late_own_ref[2 * f - early + 1] = drop
    seg = seg_ref[...]
    lane = lax.broadcasted_iota(jnp.int32, starts_ref.shape, 1)
    starts = jnp.zeros(starts_ref.shape, jnp.int32)
    for v in range(1, 6):
        count = jnp.sum(jnp.where(seg < v, 1.0, 0.0), axis=1, keepdims=True).astype(jnp.int32)
        starts = jnp.where(lane == v, count, starts)
    starts_ref[...] = starts

    gathered = [(jw_ref.at[u], jw_hbm.at[u]) for u in range(3)] + [(mix_ref, mix_hbm)]
    gathered += [(early_ref.at[u], early_hbm.at[u]) for u in range(early)]
    stores = [pltpu.make_async_copy(a, b, unit_sem.at[i]) for i, (a, b) in enumerate(gathered)]
    for u in range(3):
        columns = slice(u * 512, (u + 1) * 512)
        stores.append(pltpu.make_async_copy(qkv_ref.at[:, columns], qkv_hbm.at[:, columns], qkv_sem.at[u]))
    for _, k, u, run in events[n_early:]:
        run()
        if k < 4:
            continue
        u -= 1
        if u >= 0:
            stores[u].start()
        if u < 0:
            load.wait()
            bias_ref[...] = bw_ref[...].reshape(512, 128).astype(F32).T[:8]
        elif u < 3:

            @pl.loop(0, tokens // 512)
            def _(b, u=u):
                rows = pl.ds(pl.multiple_of(b * 512, 512), 512)
                y = mm(tok_ref[rows, :], jw_ref[u].reshape(512, 512))
                if u == 0:
                    y = y + bias_ref[6:7, :]
                if u == 2:
                    y = y + bias_ref[7:8, :]
                qkv_ref[rows, u * 512 : (u + 1) * 512] = y.astype(BF)

            stores[len(gathered) + u].start()

    for job in jobs:
        job.finish()
    for store in stores:
        store.wait()


def first(nz, tok, joint, mix, lift, drop, biases, seg):
    tokens = tok.shape[0]
    vmem = pl.BlockSpec(memory_space=pltpu.VMEM)
    hbm = pl.BlockSpec(memory_space=pl.ANY)
    unit = (nz, 2, 2, 2, 16, 512)
    return pl.pallas_call(
        functools.partial(first_kernel, nz),
        in_specs=[hbm] + [vmem] * 9,
        out_specs=[hbm] * 4 + [vmem] * 3,
        out_shape=[
            jax.ShapeDtypeStruct((tokens, 1536), BF),
            jax.ShapeDtypeStruct((3,) + unit, BF),
            jax.ShapeDtypeStruct(unit, BF),
            jax.ShapeDtypeStruct((EARLY,) + unit, BF),
            jax.ShapeDtypeStruct((drop.shape[0] // 8 - EARLY, 16, 512), BF),
            jax.ShapeDtypeStruct((8, 512), F32),
            jax.ShapeDtypeStruct((seg.shape[0], 128), jnp.int32),
        ],
        scratch_shapes=[
            pltpu.VMEM(tok.shape, BF),
            pltpu.VMEM((tokens, 1536), BF),
            pltpu.VMEM((3,) + unit, BF),
            pltpu.VMEM(unit, BF),
            pltpu.VMEM((EARLY,) + unit, BF),
            pltpu.VMEM((nz, 2, 2, 2, 16, 128), BF),
            pltpu.VMEM((128, 128), F32),
            pltpu.SemaphoreType.DMA,
            pltpu.SemaphoreType.DMA((3,)),
            pltpu.SemaphoreType.DMA((4 + EARLY,)),
        ]
        + sems(5 + EARLY, nz),
        compiler_params=pltpu.CompilerParams(vmem_limit_bytes=VMEM_LIMIT, collective_id=1, has_side_effects=True),
        name="gather_joint",
    )(tok, joint, mix, lift, drop, *biases, seg)


def middle_kernel(
    nz,
    tb,
    tok_hbm,
    ctx_hbm,
    cot_hbm,
    mix_ref,
    early_ref,
    late_ref,
    bias_ref,
    out_hbm,
    gmid_hbm,
    gctx_hbm,
    gmix_ref,
    gbias_ref,
    kept_ref,
    grad_ref,
    tok_ref,
    ctx_ref,
    cot_ref,
    out_ref,
    gmid_ref,
    gctx_ref,
    in_sem,
    out_sem,
    kept_sem,
    w_ref,
    hid_ref,
    hidt_ref,
    cott_ref,
    acc_ref,
    act_ref,
    gl_ref,
    gdt_ref,
    sum_ref,
    load_sem,
    gsend,
    grecv,
    rsend,
    rrecv,
    *bufs,
):
    me = Place(nz)
    tokens, width = tok_ref.shape
    nf = w_ref.shape[0] // 2
    nb = tokens // tb
    early = early_ref.shape[0]

    def moves(pairs, sem, b):
        rows = pl.ds(b * tb, tb)
        return [pltpu.make_async_copy(x.at[rows], y.at[rows], sem.at[i, b]) for i, (x, y) in enumerate(pairs)]

    ins = ((tok_hbm, tok_ref), (ctx_hbm, ctx_ref), (cot_hbm, cot_ref))
    outs = ((out_ref, out_hbm), (gmid_ref, gmid_hbm), (gctx_ref, gctx_hbm))
    for b in range(nb):
        for move in moves(ins, in_sem, b):
            move.start()
    load = pltpu.make_async_copy(early_ref, w_ref.at[0:early], load_sem)
    load.start()
    for u in range(early, 2 * nf):
        w_ref[u, me.z, me.y, me.x, me.c] = late_ref[u - early]
    ones = jnp.ones((16, tb), BF)

    late = [Gather(me, w_ref.at[u], gsend, grecv, u - early) for u in range(early, 2 * nf)]

    def gather_step(k):
        for job in late:
            (job.start, job.step1, job.step2, job.step3, job.step4)[k]()

    def reduces(f):
        return [Reduce(me, bufs, 2 * f + i, rsend, rrecv) for i in range(2)]

    me.greet()
    gather_step(0)

    for b in range(nb):
        for move in moves(ins, in_sem, b):
            move.wait()
        rows = pl.ds(b * tb, tb)
        mid = tok_ref[rows, :].astype(F32) + mm(ctx_ref[rows, :], mix_ref[...]) + bias_ref[5:6, :]
        acc_ref[rows, :] = mid + bias_ref[4:5, :]
        h = mid.astype(BF)
        hid_ref[rows, :] = h
        hidt_ref[0:width, rows] = h.T
        hidt_ref[width : width + 16, rows] = ones
        c = cot_ref[rows, :]
        cott_ref[:, rows] = c.T
        gmid_ref[rows, :] = c.astype(F32)

    gbias_ref[...] = jnp.zeros_like(gbias_ref)
    load.wait()

    def stage1(f, b, n, size):
        rows = pl.ds(b * tb, tb)
        lw = w_ref[2 * f].reshape(512, 512)
        dw = w_ref[2 * f + 1].reshape(512, 512)
        x = mm(hid_ref[rows, :], lw[:, n : n + size]) + bias_ref[pl.ds(f, 1), :][:, n : n + size]
        grad = mm(cot_ref[rows, :], dw[n : n + size, :], NT)
        a, g = gelu_pair(x, grad)
        act_ref[b, :, n : n + size] = a
        gl_ref[b, :, n : n + size] = g

    def stage2(f, b, part):
        slot = f % 2
        rows = pl.ds(b * tb, tb)
        if part == 0:
            acc_ref[rows, :] += mm(act_ref[b], w_ref[2 * f + 1].reshape(512, 512))
        elif part == 1:
            gmid_ref[rows, :] += mm(gl_ref[b], w_ref[2 * f].reshape(512, 512), NT)
        elif part == 2:
            gd = mm(cott_ref[:, rows], act_ref[b])
            if b == 0:
                gdt_ref[...] = gd
            elif b < nb - 1:
                gdt_ref[...] += gd
            else:
                sum_ref[slot, 1] = (gdt_ref[...] + gd).T.reshape(nz, 2, 2, 2, 16, 512)
        else:
            gf = mm(hidt_ref[:, rows], gl_ref[b])
            unit = gf[:width].reshape(nz, 2, 2, 2, 16, 512)
            if b == 0:
                sum_ref[slot, 0] = unit
            else:
                sum_ref[slot, 0] += unit
            gbias_ref[pl.ds(f, 1), :] += gf[width : width + 1]

    def work(f, k):
        for part in range(4):
            if k < nb and part % (4 // SPLIT) == 0:
                stage1(f, k, part // (4 // SPLIT) * (512 // SPLIT), 512 // SPLIT)
            if k > 0:
                stage2(f, k - 1, part)

    def due(k):
        return [((d - k) // nb, step) for step, d in enumerate(REDUCE_AT) if d % nb == k][::-1]

    def reduce_step(f, k):
        slot = f % 2
        for i, job in enumerate(reduces(f)):
            if k == 0:
                job.start(sum_ref.at[slot, i])
            elif k == 1:
                job.step1(sum_ref.at[slot, i])
            elif k == 2:
                job.step2()
            elif k == 3:
                job.step3()
            else:
                grad_ref[2 * f + i] = job.step4()

    @pl.loop(0, nf)
    def _(f):
        for k in range(nb):
            for at, step in GATHER_AT:
                if at % nb == k:

                    @pl.when(f == at // nb)
                    def _(step=step):
                        gather_step(step)


            for back, step in due(k):

                @pl.when(f > back)
                def _(back=back, step=step):
                    reduce_step(f - 1 - back, step)

            work(f, k)
        work(f, nb)

    keep = pltpu.make_async_copy(sum_ref.at[(nf - 1) % 2], kept_ref, kept_sem)
    keep.start()
    gmix_ref[...] = jnp.zeros_like(gmix_ref)
    for b in range(nb):
        for back, step in due(b):
            if back > 0:
                reduce_step(nf - 1 - back, step)
        rows = pl.ds(b * tb, tb)
        out_ref[rows, :] = acc_ref[rows, :].astype(BF)
        gb = gmid_ref[rows, :].astype(BF)
        gctx_ref[rows, :] = mm(gb, mix_ref[...], NT).astype(BF)
        gmix_ref[...] += mm(ctx_ref[rows, :].T, gb)
        gbias_ref[5:6, :] += mm(ones, gb)[0:1]
        gbias_ref[4:5, :] += mm(ones, cot_ref[rows, :])[0:1]
        for move in moves(outs, out_sem, b):
            move.start()
    for more in range(1, 4):
        for b in range(nb):
            for back, step in due(b):
                if back > more and nf - 1 - back + more < nf - 1:
                    reduce_step(nf - 1 - back + more, step)
    keep.wait()
    for b in range(nb):
        for move in moves(outs, out_sem, b):
            move.wait()
    for job in late:
        job.finish()
    for f in range(nf - 1):
        for job in reduces(f):
            job.finish()


def middle(nz, tok, ctx, cot, mix, early, late, bias):
    tokens, width = tok.shape
    n = early.shape[0] + late.shape[0]
    tb = tokens // 4
    vmem = pl.BlockSpec(memory_space=pltpu.VMEM)
    hbm = pl.BlockSpec(memory_space=pl.ANY)
    return pl.pallas_call(
        functools.partial(middle_kernel, nz, tb),
        in_specs=[hbm] * 3 + [vmem, hbm, vmem, vmem],
        out_specs=[hbm] * 3 + [vmem, vmem, hbm, vmem],
        out_shape=[
            jax.ShapeDtypeStruct((tokens, width), BF),
            jax.ShapeDtypeStruct((tokens, width), F32),
            jax.ShapeDtypeStruct((tokens, width), BF),
            jax.ShapeDtypeStruct((width, width), F32),
            jax.ShapeDtypeStruct((8, 512), F32),
            jax.ShapeDtypeStruct((2, nz, 2, 2, 2, 16, 512), F32),
            jax.ShapeDtypeStruct((n - 2, 16, 512), F32),
        ],
        scratch_shapes=[
            pltpu.VMEM((tokens, width), BF),
            pltpu.VMEM((tokens, width), BF),
            pltpu.VMEM((tokens, width), BF),
            pltpu.VMEM((tokens, width), BF),
            pltpu.VMEM((tokens, width), F32),
            pltpu.VMEM((tokens, width), BF),
            pltpu.SemaphoreType.DMA((3, 4)),
            pltpu.SemaphoreType.DMA((3, 4)),
            pltpu.SemaphoreType.DMA,
            pltpu.VMEM((n, nz, 2, 2, 2, 16, 512), BF),
            pltpu.VMEM((tokens, width), BF),
            pltpu.VMEM((width + 16, tokens), BF),
            pltpu.VMEM((width, tokens), BF),
            pltpu.VMEM((tokens, width), F32),
            pltpu.VMEM((4, tb, 512), BF),
            pltpu.VMEM((4, tb, 512), BF),
            pltpu.VMEM((width, 512), F32),
            pltpu.VMEM((2, 2, nz, 2, 2, 2, 16, 512), F32),
            pltpu.SemaphoreType.DMA,
        ]
        + sems(late.shape[0], nz)
        + sems(n - 2, nz)
        + reduce_bufs(n - 2, nz, 512),
        compiler_params=pltpu.CompilerParams(vmem_limit_bytes=VMEM_LIMIT, collective_id=2, has_side_effects=True),
        name="feed",
    )(tok, ctx, cot, mix, early, late, bias)


def last_kernel(
    nz,
    tok_hbm,
    gj_hbm,
    gmix_ref,
    gbias_ref,
    kept_ref,
    grad_ref,
    joint_ref,
    mix_ref,
    obias_ref,
    glift_ref,
    gdrop_ref,
    tok_ref,
    gj_ref,
    tok_sem,
    gj_sem,
    tokt_ref,
    sum_ref,
    bsum_ref,
    brow_ref,
    send,
    recv,
    bsend,
    brecv,
    *bufs,
):
    me = Place(nz)
    tokens, width = tok_ref.shape
    tok_load = pltpu.make_async_copy(tok_hbm, tok_ref, tok_sem)
    tok_load.start()
    gj_loads = []
    for u in range(3):
        columns = slice(u * 512, (u + 1) * 512)
        gj_loads.append(pltpu.make_async_copy(gj_hbm.at[:, columns], gj_ref.at[:, columns], gj_sem.at[u]))
        gj_loads[u].start()
    n = 7
    nf = glift_ref.shape[1] // 512
    me.greet()
    jobs = [Reduce(me, bufs[:9], u, send, recv) for u in range(n - 1)] + [Reduce(me, bufs[9:], 0, bsend, brecv)]
    units = [kept_ref.at[0], kept_ref.at[1], gmix_ref] + [sum_ref.at[j] for j in range(3)] + [bsum_ref]

    def begin(u):
        if u == n - 1:
            bsum_ref[...] = brow_ref[...].T.reshape(nz, 2, 2, 2, 16, 128)
        elif u > 2:
            gj_loads[u - 3].wait()
            if u == 3:
                tok_load.wait()

                @pl.loop(0, tokens // 512)
                def _(b):
                    rows = pl.ds(pl.multiple_of(b * 512, 512), 512)
                    tokt_ref[0:width, rows] = tok_ref[rows, :].T
                    tokt_ref[width : width + 16, rows] = jnp.ones((16, 512), BF)

                brow_ref[...] = jnp.zeros_like(brow_ref)
                brow_ref[0:8, :] = gbias_ref[...]
            g = mm(tokt_ref[...], gj_ref[:, (u - 3) * 512 : (u - 2) * 512])
            sum_ref[u - 3] = g[:width].reshape(nz, 2, 2, 2, 16, 512)
            if u != 4:
                at = 6 + (u - 3) // 2
                brow_ref[at : at + 1, :] = g[width : width + 1]
        jobs[u].start(units[u])

    def put_lift(last):
        g = jnp.concatenate(
            [
                jnp.concatenate(
                    [grad_ref[2 * f, :, 128 * u : 128 * u + 128] for f in range(nf - 1)]
                    + [last[:, 128 * u : 128 * u + 128]],
                    axis=1,
                )
                for u in range(nf)
            ],
            axis=0,
        )
        order = unit_order()
        high = g.astype(BF)
        rest = g - high.astype(F32)
        part = rest.astype(BF)
        low = (rest - part.astype(F32)).astype(BF)
        g = mm(high, order, NT) + mm(part, order, NT) + mm(low, order, NT)
        for u in range(nf):
            glift_ref[:, 512 * u : 512 * u + 512] = g[16 * u : 16 * u + 16]

    def end(u):
        total = jobs[u].step4()
        if u == 0:
            put_lift(total)
        elif u == 1:
            for f in range(nf - 1):
                gdrop_ref[16 * f : 16 * f + 16, :] = grad_ref[2 * f + 1]
            gdrop_ref[16 * nf - 16 : 16 * nf, :] = total
        elif u == 2:
            mix_ref[...] = total
        elif u < n - 1:
            joint_ref[:, (u - 3) * 512 : (u - 2) * 512] = total
        else:
            obias_ref[...] = jnp.concatenate([total, jnp.zeros((112, 128), F32)], axis=0).T[:8]

    def run(u, k):
        if k == 0:
            begin(u)
        elif k == 1:
            jobs[u].step1(units[u])
        elif k == 2:
            jobs[u].step2()
        elif k == 3:
            jobs[u].step3()
        else:
            end(u)

    events = [(2 * u + when, k, u) for u in range(n) for k, when in enumerate(REDUCE_TICKS)]
    for _, k, u in sorted(events, key=lambda e: (e[0], -e[1])):
        run(u, k)
    for job in jobs:
        job.finish()


def last(nz, tok, gj, gmix, gbias, kept, grads):
    tokens, width = tok.shape
    n = grads.shape[0] + 2
    vmem = pl.BlockSpec(memory_space=pltpu.VMEM)
    hbm = pl.BlockSpec(memory_space=pl.ANY)
    return pl.pallas_call(
        functools.partial(last_kernel, nz),
        in_specs=[hbm] * 2 + [vmem] * 4,
        out_specs=[vmem] * 5,
        out_shape=[
            jax.ShapeDtypeStruct((16, 1536), F32),
            jax.ShapeDtypeStruct((16, 512), F32),
            jax.ShapeDtypeStruct((8, 128), F32),
            jax.ShapeDtypeStruct((16, n // 2 * 512), F32),
            jax.ShapeDtypeStruct((n // 2 * 16, 512), F32),
        ],
        scratch_shapes=[
            pltpu.VMEM((tokens, width), BF),
            pltpu.VMEM((tokens, 3 * width), BF),
            pltpu.SemaphoreType.DMA,
            pltpu.SemaphoreType.DMA((3,)),
            pltpu.VMEM((width + 16, tokens), BF),
            pltpu.VMEM((3, nz, 2, 2, 2, 16, 512), F32),
            pltpu.VMEM((nz, 2, 2, 2, 16, 128), F32),
            pltpu.VMEM((128, 512), F32),
        ]
        + sems(6, nz)
        + sems(1, nz)
        + reduce_bufs(6, nz, 512)
        + reduce_bufs(1, nz, 128),
        compiler_params=pltpu.CompilerParams(vmem_limit_bytes=VMEM_LIMIT, collective_id=3, has_side_effects=True),
        name="joint_grads",
    )(tok, gj, gmix.reshape(nz, 2, 2, 2, 16, 512), gbias, kept, grads)


def hand_out_kernel(*refs):
    half = (len(refs) - 5) // 2
    bias_ref = refs[half]
    outs = refs[half + 1 :]
    for a, b in zip(refs[:half], outs):
        b[...] = a[...]
    lift_ref, drop_ref, mix_ref, joint_ref = outs[half:]
    rows = bias_ref[...]
    nf = lift_ref.shape[1] // 16
    lane = lax.broadcasted_iota(jnp.int32, (1, 128), 1)
    line = rows[0:1]
    for f in range(1, nf):
        line = jnp.where(lane // 16 == f, pltpu.roll(rows[f : f + 1], 16 * f, 1), line)
    lift_ref[...] = line[:, : lift_ref.shape[1]]
    drop_ref[...] = rows[4:5, 0:16]
    mix_ref[...] = rows[5:6, 0:16]
    joint_ref[...] = rows[6:8, 0:16]


def hand_out(arrays, bias_rows, nf):
    vmem = pl.BlockSpec(memory_space=pltpu.VMEM)
    shapes = [a.shape for a in arrays] + [(1, 16 * nf), (1, 16), (1, 16), (2, 16)]
    return pl.pallas_call(
        hand_out_kernel,
        in_specs=[vmem] * (len(arrays) + 1),
        out_specs=[vmem] * len(shapes),
        out_shape=[jax.ShapeDtypeStruct(s, F32) for s in shapes],
        name="hand_out",
    )(*arrays, bias_rows)


def remote_body(
    tokens,
    segment_ids,
    fill_lengths,
    joint_weight,
    joint_bias,
    mix_weight,
    mix_bias,
    lift_weight,
    lift_bias,
    drop_weight,
    drop_bias,
    cotangent,
):
    rows, length, width = tokens.shape
    nz = lax.axis_size("gx")
    n_tok = rows * length
    tok = tokens.reshape(n_tok, width)
    nf = drop_weight.shape[0] // 16
    biases = (lift_bias[None], drop_bias[None], mix_bias[None], joint_bias)
    qkv, joint_w, mix_w, early, late, bias, starts = first(
        nz, tok, joint_weight, mix_weight, lift_weight, drop_weight, biases, segment_ids
    )
    qkv3 = qkv.reshape(rows, length, 3 * width)
    ctx, lse = attend(starts, fill_lengths, segment_ids, qkv3)
    out, gmid, gctx, gmix, gbias, kept, grads = middle(
        nz, tok, ctx.reshape(n_tok, width), cotangent.reshape(n_tok, width), mix_w.reshape(width, width), early, late, bias
    )
    gjoint, token_grad, out = attend_back(
        starts,
        fill_lengths,
        segment_ids,
        qkv3,
        lse,
        ctx,
        gctx.reshape(rows, length, width),
        gmid.reshape(rows, length, width),
        joint_w.reshape(3, width, width),
        out.reshape(rows, length, width),
    )
    gj, gm, gb, glift, gdrop = last(nz, tok, gjoint.reshape(n_tok, 3 * width), gmix, gbias, kept, grads)
    gj, gm, glift, gdrop, blift, bdrop, bmix, bjoint = hand_out((gj, gm, glift, gdrop), gb, nf)
    return (out, token_grad, gj, bjoint, gm, bmix[0], glift, blift[0], gdrop, bdrop[0])


BOTH = ("gx", "gy")


def body(
    tokens,
    segment_ids,
    fill_lengths,
    joint_weight,
    joint_bias,
    mix_weight,
    mix_bias,
    lift_weight,
    lift_bias,
    drop_weight,
    drop_bias,
    cotangent,
):
    rows, length, width = tokens.shape
    n_tok = rows * length
    tok = tokens.reshape(n_tok, width)
    cot = cotangent.reshape(n_tok, width)
    starts = jnp.sum(
        segment_ids[:, None, :] < jnp.arange(128, dtype=jnp.int32)[None, :, None], axis=-1, dtype=jnp.int32
    )

    joint_w = lax.all_gather(joint_weight, BOTH, axis=0, tiled=True)
    mix_w = lax.all_gather(mix_weight, BOTH, axis=0, tiled=True)
    lift_w = lax.all_gather(lift_weight, BOTH, axis=0, tiled=True)
    drop_w = lax.all_gather(drop_weight, BOTH, axis=0, tiled=True)
    own_bias = jnp.concatenate([joint_bias.reshape(-1), mix_bias, lift_bias, drop_bias])
    sizes = [joint_bias.shape[1], joint_bias.shape[1], mix_bias.size, lift_bias.size, drop_bias.size]
    all_bias = lax.all_gather(own_bias, BOTH, axis=0)
    parts, at = [], 0
    for size in sizes:
        parts.append(all_bias[:, at : at + size].reshape(-1).astype(F32))
        at += size
    bq, bv, bm, bl, bd = parts
    nf = bl.size // 512
    bias = jnp.concatenate(
        [jnp.concatenate([bl.reshape(nf, 512), jnp.zeros((4 - nf, 512), F32)]), bd[None], bm[None], bq[None], bv[None]]
    )

    shift = jnp.concatenate([bq, jnp.zeros_like(bq), bv])
    qkv = (mm(tok, joint_w) + shift).astype(BF)
    qkv3 = qkv.reshape(rows, length, 3 * width)
    ctx, lse = attend(starts, fill_lengths, segment_ids, qkv3)
    lift_units = lift_w.reshape(width, nf, 512).transpose(1, 0, 2)
    out, gmid, gctx, glift, gdrop, gmix, gbias = feed(
        tok, ctx.reshape(n_tok, width), cot, mix_w, lift_units, drop_w.reshape(nf, 512, width), bias
    )
    gjoint, token_grad, out = attend_back(
        starts,
        fill_lengths,
        segment_ids,
        qkv3,
        lse,
        ctx,
        gctx.reshape(rows, length, width),
        gmid.reshape(rows, length, width),
        joint_w.reshape(width, 3, width).transpose(1, 0, 2),
        out.reshape(rows, length, width),
    )
    gjoint = gjoint.reshape(n_tok, 3 * width)
    gjoint_w = lax.dot_general(tok, gjoint, (((0,), (0,)), ((), ())), preferred_element_type=F32)
    sums = jnp.sum(gjoint.astype(F32), axis=0)

    glift_w = glift[:, :width].transpose(1, 0, 2).reshape(width, nf * 512)
    gdrop_w = gdrop.transpose(0, 2, 1).reshape(nf * 512, width)
    scatter = functools.partial(lax.psum_scatter, axis_name=BOTH, scatter_dimension=0, tiled=True)
    n_dev = all_bias.shape[0]
    packed = jnp.concatenate(
        [
            g.reshape(n_dev, -1)
            for g in (sums[:width], sums[2 * width :], gbias[5], gbias[:nf].reshape(-1), gbias[4])
        ],
        axis=1,
    )
    own = scatter(packed)[0]
    cuts, at = [], 0
    for size in sizes:
        cuts.append(own[at : at + size])
        at += size
    return (
        out,
        token_grad,
        scatter(gjoint_w),
        jnp.stack([cuts[0], cuts[1]]),
        scatter(gmix),
        cuts[2],
        scatter(glift_w),
        cuts[3],
        scatter(gdrop_w),
        cuts[4],
    )


def solution(mesh):
    wide = P(BOTH, None, None)
    rows = P(BOTH, None)
    flat = P(BOTH)
    bias = P(None, BOTH)
    in_specs = (wide, rows, flat, rows, bias, rows, flat, rows, flat, rows, flat, wide)
    out_specs = (wide, wide, rows, bias, rows, flat, rows, flat, rows, flat)
    fits = mesh.shape["gy"] == 8 and mesh.shape["gx"] == 4
    return jax.shard_map(remote_body if fits else body, mesh=mesh, in_specs=in_specs, out_specs=out_specs, check_vma=False)
```

```python
import functools
import math

import jax
import jax.numpy as jnp
from jax import lax
from jax.experimental import pallas as pl
from jax.experimental.pallas import tpu as pltpu
from jax.sharding import PartitionSpec as P

BF = jnp.bfloat16
F32 = jnp.float32
NT = (((1,), (1,)), ((), ()))
NN = (((1,), (0,)), ((), ()))
NEG = -float(2**30)
C0 = math.sqrt(2.0 / math.pi)
C1 = 0.044715
WIDE = 6
CUT = 2
VMEM_LIMIT = 60 * 2**20


def mm(a, b, dims=NN):
    return lax.dot_general(a, b, dims, preferred_element_type=F32)


def lane(p, base):
    at = base + p * 128
    return pl.ds(at if isinstance(at, int) else pl.multiple_of(at, 128), 128)


def split_heads(x):
    lane = lax.broadcasted_iota(jnp.int32, x.shape, 1)
    zero = jnp.zeros_like(x)
    return jnp.concatenate([jnp.where(lane < 64, x, zero), jnp.where(lane < 64, zero, x)], axis=0)


def diag_blocks(y):
    return jnp.concatenate([y[:64, :128], y[64:, 128:]], axis=0)


def window(starts_ref, fill_ref, row, t, length):
    first = t * 128
    last = first + 127
    fill = fill_ref[row]
    lo = jnp.int32(0)
    hi = jnp.int32(length)
    for v in range(1, 6):
        s = starts_ref[row, v]
        lo = jnp.where(s <= first, jnp.maximum(lo, s), lo)
        hi = jnp.where(s > last, jnp.minimum(hi, s), hi)
    hi = jnp.minimum(hi, fill)
    alone = lo >= fill
    hi = jnp.where(last >= fill, jnp.maximum(hi, last + 1), hi)
    lo = jnp.where(alone, first, lo)
    lo_b = lo // 128
    return lo_b, (hi + 127) // 128 - lo_b


def ids_of(seg_ref, row, lanes):
    ids = seg_ref[:, lanes]
    mine = lax.broadcasted_iota(jnp.int32, ids.shape, 0) == row
    return jnp.sum(jnp.where(mine, ids.astype(F32), 0.0), axis=0, keepdims=True)


def write_mask(mask_ref, segk_ref, seg_ref, row, fill, t, lo_b, n):
    segq = ids_of(seg_ref, row, pl.ds(pl.multiple_of(t * 128, 128), 128))
    segq = jnp.broadcast_to(segq, (128, 128))
    qi = t * 128 + lax.broadcasted_iota(jnp.int32, (128, 128), 1)
    ki0 = lax.broadcasted_iota(jnp.int32, (128, 128), 0)
    for c in range(n):
        off = pl.multiple_of((lo_b + c) * 128, 128)
        ki = ki0 + off
        ok = ((segk_ref[pl.ds(off, 128), :] == segq) & (ki < fill)) | (ki == qi)
        mask_ref[c * 128 : (c + 1) * 128, :] = jnp.where(ok, 0.0, NEG)


def spread_segments(seg_ref, segk_ref, row, length):
    for b in range(length // 128):
        ids = ids_of(seg_ref, row, slice(b * 128, (b + 1) * 128))
        segk_ref[b * 128 : (b + 1) * 128, :] = jnp.broadcast_to(ids, (128, 128)).T


def attend_kernel(
    starts_ref, fill_ref, seg_ref, qkv_ref, ctx_ref, lse_ref, vt_ref, segk_ref, mask_ref, s_ref, p_ref, *, length
):
    row = pl.program_id(0)
    fill = fill_ref[row]
    spread_segments(seg_ref, segk_ref, row, length)
    for b in range(length // 128):
        for p in range(4):
            v = qkv_ref[0, b * 128 : (b + 1) * 128, 1024 + p * 128 : 1024 + (p + 1) * 128]
            vt_ref[p * 128 : (p + 1) * 128, b * 128 : (b + 1) * 128] = v.T

    def tile(t, lo_b, n):
        tq = pl.ds(pl.multiple_of(t * 128, 128), 128)
        win = pl.ds(pl.multiple_of(lo_b * 128, 128), n * 128)
        cuts = [(c, min(CUT, n - c)) for c in range(0, n, CUT)]
        tops, sums = [], []
        for p in range(4):
            lanes = slice(p * 128, (p + 1) * 128)
            qbd = split_heads(qkv_ref[0, tq, lanes] * jnp.asarray(0.125, BF))
            top = None
            for c, w in cuts:
                rows = pl.ds(pl.multiple_of((lo_b + c) * 128, 128), w * 128)
                s = mm(qkv_ref[0, rows, 512 + p * 128 : 512 + (p + 1) * 128], qbd, NT)
                mask = mask_ref[c * 128 : (c + w) * 128, :]
                s = s + jnp.concatenate([mask, mask], axis=1)
                s_ref[p, c * 128 : (c + w) * 128, :] = s
                part = jnp.max(s.reshape(w * 16, 8, 256), axis=0)
                top = part if top is None else jnp.maximum(top, part)
            tops.append(jnp.max(top, axis=0, keepdims=True))
        for p in range(4):
            total = None
            for c, w in cuts:
                e = jnp.exp(s_ref[p, c * 128 : (c + w) * 128, :] - tops[p])
                p_ref[p, c * 128 : (c + w) * 128, :] = e.astype(BF)
                part = jnp.sum(e.reshape(w * 16, 8, 256), axis=0)
                total = part if total is None else total + part
            sums.append(jnp.sum(total, axis=0, keepdims=True))
        for p in range(4):
            o = mm(vt_ref[p * 128 : (p + 1) * 128, win], p_ref[p, : n * 128, :]) * (1.0 / sums[p])
            ctx_ref[0, tq, p * 128 : (p + 1) * 128] = diag_blocks(o).T.astype(BF)
            lse_ref[0, p, pl.ds(t, 1), :] = tops[p] + jnp.log(sums[p])

    @pl.loop(0, length // 128)
    def _(t):
        lo_b, n = window(starts_ref, fill_ref, row, t, length)
        for k in range(1, length // 128 + 1):

            @pl.when(n == k)
            def _(k=k):
                write_mask(mask_ref, segk_ref, seg_ref, row, fill, t, lo_b, k)
                tile(t, lo_b, k)


def attend(starts, fill, seg, qkv):
    rows, length, _ = qkv.shape
    blocks = length // 128
    return pl.pallas_call(
        functools.partial(attend_kernel, length=length),
        grid_spec=pltpu.PrefetchScalarGridSpec(
            num_scalar_prefetch=2,
            grid=(rows,),
            in_specs=[
                pl.BlockSpec((rows, length), lambda r, *_: (0, 0)),
                pl.BlockSpec((1, length, 1536), lambda r, *_: (r, 0, 0)),
            ],
            out_specs=[
                pl.BlockSpec((1, length, 512), lambda r, *_: (r, 0, 0)),
                pl.BlockSpec((1, 4, blocks, 256), lambda r, *_: (r, 0, 0, 0)),
            ],
            scratch_shapes=[
                pltpu.VMEM((512, length), BF),
                pltpu.VMEM((length, 128), F32),
                pltpu.VMEM((length, 128), F32),
                pltpu.VMEM((4, length, 256), F32),
                pltpu.VMEM((4, length, 256), BF),
            ],
        ),
        out_shape=[
            jax.ShapeDtypeStruct((rows, length, 512), BF),
            jax.ShapeDtypeStruct((rows, 4, blocks, 256), F32),
        ],
        compiler_params=pltpu.CompilerParams(vmem_limit_bytes=VMEM_LIMIT),
        name="attend",
    )(starts, fill, seg, qkv)


def attend_back_kernel(
    starts_ref,
    fill_ref,
    seg_ref,
    qkv_ref,
    lse_ref,
    ctx_ref,
    do_ref,
    gmid_hbm,
    jw_hbm,
    pass_hbm,
    out_ref,
    tg_ref,
    to_hbm,
    gmid_ref,
    jw_ref,
    pass_ref,
    late_sem,
    kt_ref,
    segk_ref,
    mask_ref,
    dk_ref,
    dv_ref,
    p_ref,
    ds_ref,
    *,
    length,
):
    row = pl.program_id(0)
    fill = fill_ref[row]
    gmid_load = pltpu.make_async_copy(gmid_hbm.at[row], gmid_ref, late_sem.at[0])
    jw_load = pltpu.make_async_copy(jw_hbm, jw_ref, late_sem.at[1])
    pass_load = pltpu.make_async_copy(pass_hbm.at[row], pass_ref, late_sem.at[2])
    pass_store = pltpu.make_async_copy(pass_ref, to_hbm.at[row], late_sem.at[3])
    gmid_load.start()
    jw_load.start()
    pass_load.start()
    spread_segments(seg_ref, segk_ref, row, length)
    for b in range(length // 128):
        for p in range(4):
            k = qkv_ref[0, b * 128 : (b + 1) * 128, 512 + p * 128 : 512 + (p + 1) * 128]
            kt_ref[p * 128 : (p + 1) * 128, b * 128 : (b + 1) * 128] = k.T
    dk_ref[...] = jnp.zeros_like(dk_ref)
    dv_ref[...] = jnp.zeros_like(dv_ref)

    def tile(t, lo_b, n):
        tq = pl.ds(pl.multiple_of(t * 128, 128), 128)
        win = pl.ds(pl.multiple_of(lo_b * 128, 128), n * 128)

        def some(pairs):
            ready = []
            for i, p in enumerate(pairs):
                lanes = lane(p, 0)
                qbd = split_heads(qkv_ref[0, tq, lanes] * jnp.asarray(0.125, BF))
                do = do_ref[0, tq, lanes]
                prod = (do.astype(F32) * ctx_ref[0, tq, lanes].astype(F32)).T
                delta = jnp.concatenate(
                    [jnp.sum(prod[:64], axis=0, keepdims=True), jnp.sum(prod[64:], axis=0, keepdims=True)], axis=1
                )
                ready.append((qbd, split_heads(do), delta, lse_ref[0, p, pl.ds(t, 1), :]))
            for c in range(0, n, CUT):
                w = min(CUT, n - c)
                rows = pl.ds(pl.multiple_of((lo_b + c) * 128, 128), w * 128)
                here = slice(c * 128, (c + w) * 128)
                for i, p in enumerate(pairs):
                    qbd, dobd, delta, lse = ready[i]
                    s = mm(qkv_ref[0, rows, lane(p, 512)], qbd, NT)
                    dp = mm(qkv_ref[0, rows, lane(p, 1024)], dobd, NT)
                    mask = mask_ref[here, :]
                    e = jnp.exp(s + jnp.concatenate([mask, mask], axis=1) - lse)
                    p_ref[p, here, :] = e.astype(BF)
                    ds_ref[p, here, :] = (e * (dp - delta)).astype(BF)
                for i, p in enumerate(pairs):
                    qbd, dobd, _, _ = ready[i]
                    lanes = lane(p, 0)
                    dv_ref[rows, lanes] += mm(p_ref[p, here, :], dobd)
                    dk_ref[rows, lanes] += mm(ds_ref[p, here, :], qbd)
            for i, p in enumerate(pairs):
                lanes = lane(p, 0)
                dq = mm(kt_ref[lanes, win], ds_ref[p, : n * 128, :])
                out_ref[0, tq, lanes] = (diag_blocks(dq) * 0.125).T.astype(BF)

        if n > WIDE:

            @pl.loop(0, 2)
            def _(g):
                some([2 * g, 2 * g + 1])

        else:
            some(range(4))

    @pl.loop(0, length // 128)
    def _(t):
        lo_b, n = window(starts_ref, fill_ref, row, t, length)
        for k in range(1, length // 128 + 1):

            @pl.when(n == k)
            def _(k=k):
                write_mask(mask_ref, segk_ref, seg_ref, row, fill, t, lo_b, k)
                tile(t, lo_b, k)

    pass_load.wait()
    pass_store.start()
    gmid_load.wait()
    jw_load.wait()
    for b in range(0, length, 256):
        rows = slice(b, b + 256)
        dk = dk_ref[rows, :].astype(BF)
        dv = dv_ref[rows, :].astype(BF)
        out_ref[0, rows, 512:1024] = dk
        out_ref[0, rows, 1024:1536] = dv
        total = gmid_ref[rows, :] + mm(out_ref[0, rows, 0:512], jw_ref[0], NT)
        tg_ref[0, rows, :] = total + mm(dk, jw_ref[1], NT) + mm(dv, jw_ref[2], NT)
    pass_store.wait()


def attend_back(starts, fill, seg, qkv, lse, ctx, do, gmid, joint, passed):
    rows, length, _ = qkv.shape
    blocks = length // 128
    wide = pl.BlockSpec((1, length, 512), lambda r, *_: (r, 0, 0))
    joined = pl.BlockSpec((1, length, 1536), lambda r, *_: (r, 0, 0))
    hbm = pl.BlockSpec(memory_space=pl.ANY)
    return pl.pallas_call(
        functools.partial(attend_back_kernel, length=length),
        grid_spec=pltpu.PrefetchScalarGridSpec(
            num_scalar_prefetch=2,
            grid=(rows,),
            in_specs=[
                pl.BlockSpec((rows, length), lambda r, *_: (0, 0)),
                joined,
                pl.BlockSpec((1, 4, blocks, 256), lambda r, *_: (r, 0, 0, 0)),
                wide,
                wide,
                hbm,
                hbm,
                hbm,
            ],
            out_specs=[joined, wide, hbm],
            scratch_shapes=[
                pltpu.VMEM((length, 512), F32),
                pltpu.VMEM((3, 512, 512), BF),
                pltpu.VMEM((length, 512), BF),
                pltpu.SemaphoreType.DMA((4,)),
                pltpu.VMEM((512, length), BF),
                pltpu.VMEM((length, 128), F32),
                pltpu.VMEM((length, 128), F32),
                pltpu.VMEM((length, 512), F32),
                pltpu.VMEM((length, 512), F32),
                pltpu.VMEM((4, length, 256), BF),
                pltpu.VMEM((4, length, 256), BF),
            ],
        ),
        out_shape=[
            jax.ShapeDtypeStruct((rows, length, 1536), BF),
            jax.ShapeDtypeStruct((rows, length, 512), F32),
            jax.ShapeDtypeStruct(passed.shape, passed.dtype),
        ],
        compiler_params=pltpu.CompilerParams(vmem_limit_bytes=VMEM_LIMIT),
        name="attend_back",
    )(starts, fill, seg, qkv, lse, ctx, do, gmid, joint, passed)


def gelu_pair(x, grad):
    x2 = x * x
    h = 0.5 + 0.5 * jnp.tanh(x * (C0 + (C0 * C1) * x2))
    act = x * h
    slope = h + act * (1.0 - h) * (2.0 * C0 + (6.0 * C0 * C1) * x2)
    return act.astype(BF), (grad * slope).astype(BF)


def feed_kernel(
    tok_ref,
    ctx_ref,
    cot_ref,
    mix_ref,
    lift_ref,
    drop_ref,
    bias_ref,
    out_ref,
    gmid_ref,
    gctx_ref,
    glift_ref,
    gdrop_ref,
    gmix_ref,
    gbias_ref,
    hid_ref,
    hidt_ref,
    cott_ref,
    acc_ref,
    act_ref,
    gl_ref,
    *,
    tb,
):
    tokens, width = tok_ref.shape
    nf = lift_ref.shape[0]
    nb = tokens // tb
    ones = jnp.ones((16, tb), BF)

    @pl.loop(0, nb)
    def _(b):
        rows = pl.ds(pl.multiple_of(b * tb, tb), tb)
        mid = tok_ref[rows, :].astype(F32) + mm(ctx_ref[rows, :], mix_ref[...]) + bias_ref[5:6, :]
        acc_ref[rows, :] = mid + bias_ref[4:5, :]
        h = mid.astype(BF)
        hid_ref[rows, :] = h
        hidt_ref[0:width, rows] = h.T
        hidt_ref[width : width + 16, rows] = ones
        c = cot_ref[rows, :]
        cott_ref[:, rows] = c.T
        gmid_ref[rows, :] = c.astype(F32)

    def stage1(f, b):
        rows = pl.ds(b * tb, tb)
        for n in range(0, 512, 256):
            x = mm(hid_ref[rows, :], lift_ref[f, :, n : n + 256]) + bias_ref[pl.ds(f, 1), n : n + 256]
            grad = mm(cot_ref[rows, :], drop_ref[f, n : n + 256, :], NT)
            a, g = gelu_pair(x, grad)
            act_ref[b, :, n : n + 256] = a
            gl_ref[b, :, n : n + 256] = g

    def stage2(f, b):
        rows = pl.ds(b * tb, tb)
        act = act_ref[b]
        gl = gl_ref[b]
        acc_ref[rows, :] += mm(act, drop_ref[f])
        gmid_ref[rows, :] += mm(gl, lift_ref[f], NT)
        gd = mm(cott_ref[:, rows], act)
        gf = mm(hidt_ref[:, rows], gl)
        if b == 0:
            gdrop_ref[f] = gd
            glift_ref[f] = gf
        else:
            gdrop_ref[f] += gd
            glift_ref[f] += gf

    @pl.loop(0, nf)
    def _(f):
        stage1(f, 0)
        for b in range(1, nb):
            stage1(f, b)
            stage2(f, b - 1)
        stage2(f, nb - 1)

    gmix_ref[...] = jnp.zeros_like(gmix_ref)
    gbias_ref[...] = jnp.zeros_like(gbias_ref)

    @pl.loop(0, nb)
    def _(b):
        rows = pl.ds(pl.multiple_of(b * tb, tb), tb)
        out_ref[rows, :] = acc_ref[rows, :].astype(BF)
        gb = gmid_ref[rows, :].astype(BF)
        gctx_ref[rows, :] = mm(gb, mix_ref[...], NT).astype(BF)
        gmix_ref[...] += mm(ctx_ref[rows, :].T, gb)
        gbias_ref[5:6, :] += mm(ones, gb)[0:1]
        gbias_ref[4:5, :] += mm(ones, cot_ref[rows, :])[0:1]

    for f in range(nf):
        gbias_ref[f : f + 1, :] = glift_ref[f, width : width + 1, :]


def feed(tok, ctx, cot, mix, lift, drop, bias):
    tokens, width = tok.shape
    nf = lift.shape[0]
    tb = 512
    vmem = pl.BlockSpec(memory_space=pltpu.VMEM)
    return pl.pallas_call(
        functools.partial(feed_kernel, tb=tb),
        in_specs=[vmem] * 7,
        out_specs=[vmem] * 7,
        out_shape=[
            jax.ShapeDtypeStruct((tokens, width), BF),
            jax.ShapeDtypeStruct((tokens, width), F32),
            jax.ShapeDtypeStruct((tokens, width), BF),
            jax.ShapeDtypeStruct((nf, width + 16, 512), F32),
            jax.ShapeDtypeStruct((nf, width, 512), F32),
            jax.ShapeDtypeStruct((width, width), F32),
            jax.ShapeDtypeStruct((8, 512), F32),
        ],
        scratch_shapes=[
            pltpu.VMEM((tokens, width), BF),
            pltpu.VMEM((width + 16, tokens), BF),
            pltpu.VMEM((width, tokens), BF),
            pltpu.VMEM((tokens, width), F32),
            pltpu.VMEM((tokens // tb, tb, 512), BF),
            pltpu.VMEM((tokens // tb, tb, 512), BF),
        ],
        compiler_params=pltpu.CompilerParams(vmem_limit_bytes=VMEM_LIMIT),
        name="feed",
    )(tok, ctx, cot, mix, lift, drop, bias)


MESH = pl.DeviceIdType.MESH
GATHER_TICKS = (0, 8, 13, 18, 21)
REDUCE_TICKS = (0, 4, 11, 17, 22)
GATHER_AT = ((1, 1), (3, 2), (6, 3), (8, 4))
REDUCE_AT = (0, 2, 5, 7, 9)
SPLIT = 1
EARLY = 4


class Place:
    def __init__(self, nz):
        self.nz = nz
        self.z = lax.axis_index("gx")
        g = lax.axis_index("gy")
        self.c = g % 2
        self.x = (g // 2) % 2
        self.y = g // 4
        self.oc = 1 - self.c
        self.y1 = self.y + self.oc * (1 - 2 * self.y)
        self.x1 = self.x + self.c * (1 - 2 * self.x)
        self.y2 = self.y + self.c * (1 - 2 * self.y)
        self.x2 = self.x + self.oc * (1 - 2 * self.x)
        self.core = (self.z, self.y * 4 + self.x * 2 + self.oc)
        self.near1 = (self.z, self.y1 * 4 + self.x1 * 2 + self.c)
        self.near2 = (self.z, self.y2 * 4 + self.x2 * 2 + self.c)

    def at_z(self, z):
        return (z, self.y * 4 + self.x * 2 + self.c)

    def up(self, k):
        return (self.z + k) % self.nz

    def down(self, k):
        return (self.z + self.nz - k) % self.nz

    def greet(self):
        barrier = pltpu.get_barrier_semaphore()
        others = [self.core, self.near1, self.near2] + [self.at_z(self.up(k)) for k in range(1, self.nz)]
        for other in others:
            pl.semaphore_signal(barrier, inc=1, device_id=other, device_id_type=MESH)
        pl.semaphore_wait(barrier, len(others))


def remote(src, dst, send, recv, u, k, device):
    return pltpu.make_async_remote_copy(
        src_ref=src,
        dst_ref=dst,
        send_sem=send.at[u, k],
        recv_sem=recv.at[u, k],
        device_id=device,
        device_id_type=MESH,
    )


class Gather:
    def __init__(self, me, buf, send, recv, u):
        nz = me.nz
        own = buf.at[:, me.y, me.x, me.c]
        other = buf.at[:, me.y1, me.x1, me.c]
        mine = buf.at[me.z, me.y, me.x, me.c]
        half = buf.at[:, :, :, me.c]
        self.along_z = lambda: [remote(mine, mine, send, recv, u, k - 1, me.at_z(me.up(k))) for k in range(1, nz)]
        self.first = lambda: remote(own, own, send, recv, u, nz - 1, me.near1)
        self.second = lambda: remote(own, own, send, recv, u, nz, me.near2)
        self.passed = lambda: remote(other, other, send, recv, u, nz + 1, me.near2)
        self.core = lambda: remote(half, half, send, recv, u, nz + 2, me.core)

    def start(self):
        for copy in self.along_z():
            copy.start()

    def step1(self):
        for copy in self.along_z():
            copy.wait_recv()
        self.first().start()
        self.second().start()

    def step2(self):
        self.first().wait_recv()
        self.passed().start()

    def step3(self):
        self.second().wait_recv()
        self.passed().wait_recv()
        self.core().start()

    def step4(self):
        self.core().wait_recv()

    def finish(self):
        for copy in self.along_z() + [self.first(), self.second(), self.passed(), self.core()]:
            copy.wait_send()


class Reduce:
    def __init__(self, me, bufs, u, send, recv):
        self.me = me
        nz = me.nz
        self.sc, self.rc, self.s1, self.r1, self.s2, self.r2, self.sz, self.rz, self.hold = [b.at[u] for b in bufs]
        self.core = lambda: remote(self.sc, self.rc, send, recv, u, 0, me.core)
        self.first = lambda: remote(self.s1, self.r1, send, recv, u, 1, me.near2)
        self.second = lambda: remote(self.s2, self.r2, send, recv, u, 2, me.near1)
        self.along_z = lambda: [
            remote(self.sz.at[me.up(k)], self.rz.at[me.z], send, recv, u, 2 + k, me.at_z(me.up(k)))
            for k in range(1, nz)
        ]

    def start(self, unit):
        me = self.me
        self.sc[...] = unit[:, :, :, me.oc].astype(BF)
        self.core().start()

    def step1(self, unit):
        me = self.me
        self.core().wait_recv()

        def total(y, x):
            return unit[:, y, x, me.c] + self.rc[:, y, x].astype(F32)

        self.s1[0] = total(me.y2, me.x2).astype(BF)
        self.s1[1] = total(1 - me.y, 1 - me.x).astype(BF)
        self.first().start()
        self.hold[0] = total(me.y, me.x)
        self.hold[1] = total(me.y1, me.x1)

    def step2(self):
        self.first().wait_recv()
        self.s2[...] = (self.hold[1] + self.r1[1].astype(F32)).astype(BF)
        self.second().start()
        self.hold[0] = self.hold[0] + self.r1[0].astype(F32)

    def step3(self):
        self.second().wait_recv()
        total = self.hold[0] + self.r2[...].astype(F32)
        self.sz[...] = total.astype(BF)
        self.hold[0] = total
        for copy in self.along_z():
            copy.start()

    def step4(self):
        me = self.me
        for copy in self.along_z():
            copy.wait_recv()
        total = self.hold[0, me.z]
        for k in range(1, me.nz):
            total = total + self.rz[me.down(k)].astype(F32)
        return total

    def finish(self):
        for copy in [self.core(), self.first(), self.second()] + self.along_z():
            copy.wait_send()


def reduce_bufs(n, nz, w):
    return [
        pltpu.VMEM((n, nz, 2, 2, 16, w), BF),
        pltpu.VMEM((n, nz, 2, 2, 16, w), BF),
        pltpu.VMEM((n, 2, nz, 16, w), BF),
        pltpu.VMEM((n, 2, nz, 16, w), BF),
        pltpu.VMEM((n, nz, 16, w), BF),
        pltpu.VMEM((n, nz, 16, w), BF),
        pltpu.VMEM((n, nz, 16, w), BF),
        pltpu.VMEM((n, nz, 16, w), BF),
        pltpu.VMEM((n, 2, nz, 16, w), F32),
    ]


def sems(n, nz):
    return [pltpu.SemaphoreType.DMA((n, nz + 3)), pltpu.SemaphoreType.DMA((n, nz + 3))]


def unit_order():
    c = lax.broadcasted_iota(jnp.int32, (512, 512), 1)
    s = lax.broadcasted_iota(jnp.int32, (512, 512), 0)
    return jnp.where(s == ((c & 127) >> 4) * 64 + (c >> 7) * 16 + (c & 15), 1.0, 0.0).astype(BF)


def first_kernel(
    nz,
    tok_hbm,
    joint_ref,
    mix_own_ref,
    lift_ref,
    drop_ref,
    bl_ref,
    bd_ref,
    bm_ref,
    bj_ref,
    seg_ref,
    qkv_hbm,
    jw_hbm,
    mix_hbm,
    early_hbm,
    late_own_ref,
    bias_ref,
    starts_ref,
    tok_ref,
    qkv_ref,
    jw_ref,
    mix_ref,
    early_ref,
    bw_ref,
    line_ref,
    tok_sem,
    qkv_sem,
    unit_sem,
    send,
    recv,
):
    me = Place(nz)
    load = pltpu.make_async_copy(tok_hbm, tok_ref, tok_sem)
    load.start()
    tokens, width = tok_ref.shape
    early = early_ref.shape[0]
    nf = drop_ref.shape[0] // 16
    here = (me.z, me.y, me.x, me.c)
    line_ref[...] = jnp.zeros_like(line_ref)
    line_ref[0:1, 0 : 16 * nf] = bl_ref[...].astype(F32)
    line_ref[4:5, 0:16] = bd_ref[...].astype(F32)
    line_ref[5:6, 0:16] = bm_ref[...].astype(F32)
    line_ref[6:8, 0:16] = bj_ref[...].astype(F32)
    lift_line = line_ref[0:1, :]
    for f in range(1, nf):
        line_ref[f : f + 1, :] = pltpu.roll(lift_line, 128 - 16 * f, 1)
    bw_ref[here] = line_ref[...].T[:16].astype(BF)
    for u in range(3):
        jw_ref[(u,) + here] = joint_ref[:, u * 512 : (u + 1) * 512]
    mix_ref[here] = mix_own_ref[...]
    me.greet()
    jobs = [Gather(me, bw_ref, send, recv, 0)]
    jobs += [Gather(me, jw_ref.at[u], send, recv, 1 + u) for u in range(3)]
    jobs += [Gather(me, mix_ref, send, recv, 4)]
    jobs += [Gather(me, early_ref.at[u], send, recv, 5 + u) for u in range(early)]
    events = []
    for u, job in enumerate(jobs):
        for k, when in enumerate(GATHER_TICKS):
            events.append((2 * u + when, k, u, (job.start, job.step1, job.step2, job.step3, job.step4)[k]))
    events.sort(key=lambda e: (e[0], -e[1]))
    n_early = 4
    for event in events[:n_early]:
        event[3]()
    rows = jnp.concatenate([lift_ref[:, u * 512 : (u + 1) * 512] for u in range(nf)], axis=0)
    rows = mm(rows, unit_order()).astype(BF)
    for f in range(nf):
        lift = jnp.concatenate([rows[16 * u : 16 * u + 16, 128 * f : 128 * f + 128] for u in range(nf)], axis=1)
        drop = drop_ref[16 * f : 16 * f + 16, :]
        if 2 * f < early:
            early_ref[(2 * f,) + here] = lift
            early_ref[(2 * f + 1,) + here] = drop
        else:
            late_own_ref[2 * f - early] = lift
            late_own_ref[2 * f - early + 1] = drop
    seg = seg_ref[...]
    lane = lax.broadcasted_iota(jnp.int32, starts_ref.shape, 1)
    starts = jnp.zeros(starts_ref.shape, jnp.int32)
    for v in range(1, 6):
        count = jnp.sum(jnp.where(seg < v, 1.0, 0.0), axis=1, keepdims=True).astype(jnp.int32)
        starts = jnp.where(lane == v, count, starts)
    starts_ref[...] = starts

    gathered = [(jw_ref.at[u], jw_hbm.at[u]) for u in range(3)] + [(mix_ref, mix_hbm)]
    gathered += [(early_ref.at[u], early_hbm.at[u]) for u in range(early)]
    stores = [pltpu.make_async_copy(a, b, unit_sem.at[i]) for i, (a, b) in enumerate(gathered)]
    for u in range(3):
        columns = slice(u * 512, (u + 1) * 512)
        stores.append(pltpu.make_async_copy(qkv_ref.at[:, columns], qkv_hbm.at[:, columns], qkv_sem.at[u]))
    for _, k, u, run in events[n_early:]:
        run()
        if k < 4:
            continue
        u -= 1
        if u >= 0:
            stores[u].start()
        if u < 0:
            load.wait()
            bias_ref[...] = bw_ref[...].reshape(512, 128).astype(F32).T[:8]
        elif u < 3:

            @pl.loop(0, tokens // 512)
            def _(b, u=u):
                rows = pl.ds(pl.multiple_of(b * 512, 512), 512)
                y = mm(tok_ref[rows, :], jw_ref[u].reshape(512, 512))
                if u == 0:
                    y = y + bias_ref[6:7, :]
                if u == 2:
                    y = y + bias_ref[7:8, :]
                qkv_ref[rows, u * 512 : (u + 1) * 512] = y.astype(BF)

            stores[len(gathered) + u].start()

    for job in jobs:
        job.finish()
    for store in stores:
        store.wait()


def first(nz, tok, joint, mix, lift, drop, biases, seg):
    tokens = tok.shape[0]
    vmem = pl.BlockSpec(memory_space=pltpu.VMEM)
    hbm = pl.BlockSpec(memory_space=pl.ANY)
    unit = (nz, 2, 2, 2, 16, 512)
    return pl.pallas_call(
        functools.partial(first_kernel, nz),
        in_specs=[hbm] + [vmem] * 9,
        out_specs=[hbm] * 4 + [vmem] * 3,
        out_shape=[
            jax.ShapeDtypeStruct((tokens, 1536), BF),
            jax.ShapeDtypeStruct((3,) + unit, BF),
            jax.ShapeDtypeStruct(unit, BF),
            jax.ShapeDtypeStruct((EARLY,) + unit, BF),
            jax.ShapeDtypeStruct((drop.shape[0] // 8 - EARLY, 16, 512), BF),
            jax.ShapeDtypeStruct((8, 512), F32),
            jax.ShapeDtypeStruct((seg.shape[0], 128), jnp.int32),
        ],
        scratch_shapes=[
            pltpu.VMEM(tok.shape, BF),
            pltpu.VMEM((tokens, 1536), BF),
            pltpu.VMEM((3,) + unit, BF),
            pltpu.VMEM(unit, BF),
            pltpu.VMEM((EARLY,) + unit, BF),
            pltpu.VMEM((nz, 2, 2, 2, 16, 128), BF),
            pltpu.VMEM((128, 128), F32),
            pltpu.SemaphoreType.DMA,
            pltpu.SemaphoreType.DMA((3,)),
            pltpu.SemaphoreType.DMA((4 + EARLY,)),
        ]
        + sems(5 + EARLY, nz),
        compiler_params=pltpu.CompilerParams(vmem_limit_bytes=VMEM_LIMIT, collective_id=1, has_side_effects=True),
        name="gather_joint",
    )(tok, joint, mix, lift, drop, *biases, seg)


def middle_kernel(
    nz,
    tb,
    tok_hbm,
    ctx_hbm,
    cot_hbm,
    mix_ref,
    early_ref,
    late_ref,
    bias_ref,
    out_hbm,
    gmid_hbm,
    gctx_hbm,
    gmix_ref,
    gbias_ref,
    kept_ref,
    grad_ref,
    tok_ref,
    ctx_ref,
    cot_ref,
    out_ref,
    gmid_ref,
    gctx_ref,
    in_sem,
    out_sem,
    kept_sem,
    w_ref,
    hid_ref,
    hidt_ref,
    cott_ref,
    acc_ref,
    act_ref,
    gl_ref,
    gdt_ref,
    sum_ref,
    load_sem,
    gsend,
    grecv,
    rsend,
    rrecv,
    *bufs,
):
    me = Place(nz)
    tokens, width = tok_ref.shape
    nf = w_ref.shape[0] // 2
    nb = tokens // tb
    early = early_ref.shape[0]

    def moves(pairs, sem, b):
        rows = pl.ds(b * tb, tb)
        return [pltpu.make_async_copy(x.at[rows], y.at[rows], sem.at[i, b]) for i, (x, y) in enumerate(pairs)]

    ins = ((tok_hbm, tok_ref), (ctx_hbm, ctx_ref), (cot_hbm, cot_ref))
    outs = ((out_ref, out_hbm), (gmid_ref, gmid_hbm), (gctx_ref, gctx_hbm))
    for b in range(nb):
        for move in moves(ins, in_sem, b):
            move.start()
    load = pltpu.make_async_copy(early_ref, w_ref.at[0:early], load_sem)
    load.start()
    for u in range(early, 2 * nf):
        w_ref[u, me.z, me.y, me.x, me.c] = late_ref[u - early]
    ones = jnp.ones((16, tb), BF)

    late = [Gather(me, w_ref.at[u], gsend, grecv, u - early) for u in range(early, 2 * nf)]

    def gather_step(k):
        for job in late:
            (job.start, job.step1, job.step2, job.step3, job.step4)[k]()

    def reduces(f):
        return [Reduce(me, bufs, 2 * f + i, rsend, rrecv) for i in range(2)]

    me.greet()
    gather_step(0)

    for b in range(nb):
        for move in moves(ins, in_sem, b):
            move.wait()
        rows = pl.ds(b * tb, tb)
        mid = tok_ref[rows, :].astype(F32) + mm(ctx_ref[rows, :], mix_ref[...]) + bias_ref[5:6, :]
        acc_ref[rows, :] = mid + bias_ref[4:5, :]
        h = mid.astype(BF)
        hid_ref[rows, :] = h
        hidt_ref[0:width, rows] = h.T
        hidt_ref[width : width + 16, rows] = ones
        c = cot_ref[rows, :]
        cott_ref[:, rows] = c.T
        gmid_ref[rows, :] = c.astype(F32)

    gbias_ref[...] = jnp.zeros_like(gbias_ref)
    load.wait()

    def stage1(f, b, n, size):
        rows = pl.ds(b * tb, tb)
        lw = w_ref[2 * f].reshape(512, 512)
        dw = w_ref[2 * f + 1].reshape(512, 512)
        x = mm(hid_ref[rows, :], lw[:, n : n + size]) + bias_ref[pl.ds(f, 1), :][:, n : n + size]
        grad = mm(cot_ref[rows, :], dw[n : n + size, :], NT)
        a, g = gelu_pair(x, grad)
        act_ref[b, :, n : n + size] = a
        gl_ref[b, :, n : n + size] = g

    def stage2(f, b, part):
        slot = f % 2
        rows = pl.ds(b * tb, tb)
        if part == 0:
            acc_ref[rows, :] += mm(act_ref[b], w_ref[2 * f + 1].reshape(512, 512))
        elif part == 1:
            gmid_ref[rows, :] += mm(gl_ref[b], w_ref[2 * f].reshape(512, 512), NT)
        elif part == 2:
            gd = mm(cott_ref[:, rows], act_ref[b])
            if b == 0:
                gdt_ref[...] = gd
            elif b < nb - 1:
                gdt_ref[...] += gd
            else:
                sum_ref[slot, 1] = (gdt_ref[...] + gd).T.reshape(nz, 2, 2, 2, 16, 512)
        else:
            gf = mm(hidt_ref[:, rows], gl_ref[b])
            unit = gf[:width].reshape(nz, 2, 2, 2, 16, 512)
            if b == 0:
                sum_ref[slot, 0] = unit
            else:
                sum_ref[slot, 0] += unit
            gbias_ref[pl.ds(f, 1), :] += gf[width : width + 1]

    def work(f, k):
        for part in range(4):
            if k < nb and part % (4 // SPLIT) == 0:
                stage1(f, k, part // (4 // SPLIT) * (512 // SPLIT), 512 // SPLIT)
            if k > 0:
                stage2(f, k - 1, part)

    def due(k):
        return [((d - k) // nb, step) for step, d in enumerate(REDUCE_AT) if d % nb == k][::-1]

    def reduce_step(f, k):
        slot = f % 2
        for i, job in enumerate(reduces(f)):
            if k == 0:
                job.start(sum_ref.at[slot, i])
            elif k == 1:
                job.step1(sum_ref.at[slot, i])
            elif k == 2:
                job.step2()
            elif k == 3:
                job.step3()
            else:
                grad_ref[2 * f + i] = job.step4()

    @pl.loop(0, nf)
    def _(f):
        for k in range(nb):
            for at, step in GATHER_AT:
                if at % nb == k:

                    @pl.when(f == at // nb)
                    def _(step=step):
                        gather_step(step)


            for back, step in due(k):

                @pl.when(f > back)
                def _(back=back, step=step):
                    reduce_step(f - 1 - back, step)

            work(f, k)
        work(f, nb)

    keep = pltpu.make_async_copy(sum_ref.at[(nf - 1) % 2], kept_ref, kept_sem)
    keep.start()
    gmix_ref[...] = jnp.zeros_like(gmix_ref)
    for b in range(nb):
        for back, step in due(b):
            if back > 0:
                reduce_step(nf - 1 - back, step)
        rows = pl.ds(b * tb, tb)
        out_ref[rows, :] = acc_ref[rows, :].astype(BF)
        gb = gmid_ref[rows, :].astype(BF)
        gctx_ref[rows, :] = mm(gb, mix_ref[...], NT).astype(BF)
        gmix_ref[...] += mm(ctx_ref[rows, :].T, gb)
        gbias_ref[5:6, :] += mm(ones, gb)[0:1]
        gbias_ref[4:5, :] += mm(ones, cot_ref[rows, :])[0:1]
        for move in moves(outs, out_sem, b):
            move.start()
    for more in range(1, 4):
        for b in range(nb):
            for back, step in due(b):
                if back > more and nf - 1 - back + more < nf - 1:
                    reduce_step(nf - 1 - back + more, step)
    keep.wait()
    for b in range(nb):
        for move in moves(outs, out_sem, b):
            move.wait()
    for job in late:
        job.finish()
    for f in range(nf - 1):
        for job in reduces(f):
            job.finish()


def middle(nz, tok, ctx, cot, mix, early, late, bias):
    tokens, width = tok.shape
    n = early.shape[0] + late.shape[0]
    tb = tokens // 4
    vmem = pl.BlockSpec(memory_space=pltpu.VMEM)
    hbm = pl.BlockSpec(memory_space=pl.ANY)
    return pl.pallas_call(
        functools.partial(middle_kernel, nz, tb),
        in_specs=[hbm] * 3 + [vmem, hbm, vmem, vmem],
        out_specs=[hbm] * 3 + [vmem, vmem, hbm, vmem],
        out_shape=[
            jax.ShapeDtypeStruct((tokens, width), BF),
            jax.ShapeDtypeStruct((tokens, width), F32),
            jax.ShapeDtypeStruct((tokens, width), BF),
            jax.ShapeDtypeStruct((width, width), F32),
            jax.ShapeDtypeStruct((8, 512), F32),
            jax.ShapeDtypeStruct((2, nz, 2, 2, 2, 16, 512), F32),
            jax.ShapeDtypeStruct((n - 2, 16, 512), F32),
        ],
        scratch_shapes=[
            pltpu.VMEM((tokens, width), BF),
            pltpu.VMEM((tokens, width), BF),
            pltpu.VMEM((tokens, width), BF),
            pltpu.VMEM((tokens, width), BF),
            pltpu.VMEM((tokens, width), F32),
            pltpu.VMEM((tokens, width), BF),
            pltpu.SemaphoreType.DMA((3, 4)),
            pltpu.SemaphoreType.DMA((3, 4)),
            pltpu.SemaphoreType.DMA,
            pltpu.VMEM((n, nz, 2, 2, 2, 16, 512), BF),
            pltpu.VMEM((tokens, width), BF),
            pltpu.VMEM((width + 16, tokens), BF),
            pltpu.VMEM((width, tokens), BF),
            pltpu.VMEM((tokens, width), F32),
            pltpu.VMEM((4, tb, 512), BF),
            pltpu.VMEM((4, tb, 512), BF),
            pltpu.VMEM((width, 512), F32),
            pltpu.VMEM((2, 2, nz, 2, 2, 2, 16, 512), F32),
            pltpu.SemaphoreType.DMA,
        ]
        + sems(late.shape[0], nz)
        + sems(n - 2, nz)
        + reduce_bufs(n - 2, nz, 512),
        compiler_params=pltpu.CompilerParams(vmem_limit_bytes=VMEM_LIMIT, collective_id=2, has_side_effects=True),
        name="feed",
    )(tok, ctx, cot, mix, early, late, bias)


def last_kernel(
    nz,
    tok_hbm,
    gj_hbm,
    gmix_ref,
    gbias_ref,
    kept_ref,
    grad_ref,
    joint_ref,
    mix_ref,
    obias_ref,
    glift_ref,
    gdrop_ref,
    tok_ref,
    gj_ref,
    tok_sem,
    gj_sem,
    tokt_ref,
    sum_ref,
    bsum_ref,
    brow_ref,
    send,
    recv,
    bsend,
    brecv,
    *bufs,
):
    me = Place(nz)
    tokens, width = tok_ref.shape
    tok_load = pltpu.make_async_copy(tok_hbm, tok_ref, tok_sem)
    tok_load.start()
    gj_loads = []
    for u in range(3):
        columns = slice(u * 512, (u + 1) * 512)
        gj_loads.append(pltpu.make_async_copy(gj_hbm.at[:, columns], gj_ref.at[:, columns], gj_sem.at[u]))
        gj_loads[u].start()
    n = 7
    nf = glift_ref.shape[1] // 512
    me.greet()
    jobs = [Reduce(me, bufs[:9], u, send, recv) for u in range(n - 1)] + [Reduce(me, bufs[9:], 0, bsend, brecv)]
    units = [kept_ref.at[0], kept_ref.at[1], gmix_ref] + [sum_ref.at[j] for j in range(3)] + [bsum_ref]

    def begin(u):
        if u == n - 1:
            bsum_ref[...] = brow_ref[...].T.reshape(nz, 2, 2, 2, 16, 128)
        elif u > 2:
            gj_loads[u - 3].wait()
            if u == 3:
                tok_load.wait()

                @pl.loop(0, tokens // 512)
                def _(b):
                    rows = pl.ds(pl.multiple_of(b * 512, 512), 512)
                    tokt_ref[0:width, rows] = tok_ref[rows, :].T
                    tokt_ref[width : width + 16, rows] = jnp.ones((16, 512), BF)

                brow_ref[...] = jnp.zeros_like(brow_ref)
                brow_ref[0:8, :] = gbias_ref[...]
            g = mm(tokt_ref[...], gj_ref[:, (u - 3) * 512 : (u - 2) * 512])
            sum_ref[u - 3] = g[:width].reshape(nz, 2, 2, 2, 16, 512)
            if u != 4:
                at = 6 + (u - 3) // 2
                brow_ref[at : at + 1, :] = g[width : width + 1]
        jobs[u].start(units[u])

    def put_lift(last):
        g = jnp.concatenate(
            [
                jnp.concatenate(
                    [grad_ref[2 * f, :, 128 * u : 128 * u + 128] for f in range(nf - 1)]
                    + [last[:, 128 * u : 128 * u + 128]],
                    axis=1,
                )
                for u in range(nf)
            ],
            axis=0,
        )
        order = unit_order()
        high = g.astype(BF)
        rest = g - high.astype(F32)
        part = rest.astype(BF)
        low = (rest - part.astype(F32)).astype(BF)
        g = mm(high, order, NT) + mm(part, order, NT) + mm(low, order, NT)
        for u in range(nf):
            glift_ref[:, 512 * u : 512 * u + 512] = g[16 * u : 16 * u + 16]

    def end(u):
        total = jobs[u].step4()
        if u == 0:
            put_lift(total)
        elif u == 1:
            for f in range(nf - 1):
                gdrop_ref[16 * f : 16 * f + 16, :] = grad_ref[2 * f + 1]
            gdrop_ref[16 * nf - 16 : 16 * nf, :] = total
        elif u == 2:
            mix_ref[...] = total
        elif u < n - 1:
            joint_ref[:, (u - 3) * 512 : (u - 2) * 512] = total
        else:
            obias_ref[...] = jnp.concatenate([total, jnp.zeros((112, 128), F32)], axis=0).T[:8]

    def run(u, k):
        if k == 0:
            begin(u)
        elif k == 1:
            jobs[u].step1(units[u])
        elif k == 2:
            jobs[u].step2()
        elif k == 3:
            jobs[u].step3()
        else:
            end(u)

    events = [(2 * u + when, k, u) for u in range(n) for k, when in enumerate(REDUCE_TICKS)]
    for _, k, u in sorted(events, key=lambda e: (e[0], -e[1])):
        run(u, k)
    for job in jobs:
        job.finish()


def last(nz, tok, gj, gmix, gbias, kept, grads):
    tokens, width = tok.shape
    n = grads.shape[0] + 2
    vmem = pl.BlockSpec(memory_space=pltpu.VMEM)
    hbm = pl.BlockSpec(memory_space=pl.ANY)
    return pl.pallas_call(
        functools.partial(last_kernel, nz),
        in_specs=[hbm] * 2 + [vmem] * 4,
        out_specs=[vmem] * 5,
        out_shape=[
            jax.ShapeDtypeStruct((16, 1536), F32),
            jax.ShapeDtypeStruct((16, 512), F32),
            jax.ShapeDtypeStruct((8, 128), F32),
            jax.ShapeDtypeStruct((16, n // 2 * 512), F32),
            jax.ShapeDtypeStruct((n // 2 * 16, 512), F32),
        ],
        scratch_shapes=[
            pltpu.VMEM((tokens, width), BF),
            pltpu.VMEM((tokens, 3 * width), BF),
            pltpu.SemaphoreType.DMA,
            pltpu.SemaphoreType.DMA((3,)),
            pltpu.VMEM((width + 16, tokens), BF),
            pltpu.VMEM((3, nz, 2, 2, 2, 16, 512), F32),
            pltpu.VMEM((nz, 2, 2, 2, 16, 128), F32),
            pltpu.VMEM((128, 512), F32),
        ]
        + sems(6, nz)
        + sems(1, nz)
        + reduce_bufs(6, nz, 512)
        + reduce_bufs(1, nz, 128),
        compiler_params=pltpu.CompilerParams(vmem_limit_bytes=VMEM_LIMIT, collective_id=3, has_side_effects=True),
        name="joint_grads",
    )(tok, gj, gmix.reshape(nz, 2, 2, 2, 16, 512), gbias, kept, grads)


def hand_out_kernel(*refs):
    half = (len(refs) - 5) // 2
    bias_ref = refs[half]
    outs = refs[half + 1 :]
    for a, b in zip(refs[:half], outs):
        b[...] = a[...]
    lift_ref, drop_ref, mix_ref, joint_ref = outs[half:]
    rows = bias_ref[...]
    nf = lift_ref.shape[1] // 16
    lane = lax.broadcasted_iota(jnp.int32, (1, 128), 1)
    line = rows[0:1]
    for f in range(1, nf):
        line = jnp.where(lane // 16 == f, pltpu.roll(rows[f : f + 1], 16 * f, 1), line)
    lift_ref[...] = line[:, : lift_ref.shape[1]]
    drop_ref[...] = rows[4:5, 0:16]
    mix_ref[...] = rows[5:6, 0:16]
    joint_ref[...] = rows[6:8, 0:16]


def hand_out(arrays, bias_rows, nf):
    vmem = pl.BlockSpec(memory_space=pltpu.VMEM)
    shapes = [a.shape for a in arrays] + [(1, 16 * nf), (1, 16), (1, 16), (2, 16)]
    return pl.pallas_call(
        hand_out_kernel,
        in_specs=[vmem] * (len(arrays) + 1),
        out_specs=[vmem] * len(shapes),
        out_shape=[jax.ShapeDtypeStruct(s, F32) for s in shapes],
        name="hand_out",
    )(*arrays, bias_rows)


def remote_body(
    tokens,
    segment_ids,
    fill_lengths,
    joint_weight,
    joint_bias,
    mix_weight,
    mix_bias,
    lift_weight,
    lift_bias,
    drop_weight,
    drop_bias,
    cotangent,
):
    rows, length, width = tokens.shape
    nz = lax.axis_size("gx")
    n_tok = rows * length
    tok = tokens.reshape(n_tok, width)
    nf = drop_weight.shape[0] // 16
    biases = (lift_bias[None], drop_bias[None], mix_bias[None], joint_bias)
    qkv, joint_w, mix_w, early, late, bias, starts = first(
        nz, tok, joint_weight, mix_weight, lift_weight, drop_weight, biases, segment_ids
    )
    qkv3 = qkv.reshape(rows, length, 3 * width)
    ctx, lse = attend(starts, fill_lengths, segment_ids, qkv3)
    out, gmid, gctx, gmix, gbias, kept, grads = middle(
        nz, tok, ctx.reshape(n_tok, width), cotangent.reshape(n_tok, width), mix_w.reshape(width, width), early, late, bias
    )
    gjoint, token_grad, out = attend_back(
        starts,
        fill_lengths,
        segment_ids,
        qkv3,
        lse,
        ctx,
        gctx.reshape(rows, length, width),
        gmid.reshape(rows, length, width),
        joint_w.reshape(3, width, width),
        out.reshape(rows, length, width),
    )
    gj, gm, gb, glift, gdrop = last(nz, tok, gjoint.reshape(n_tok, 3 * width), gmix, gbias, kept, grads)
    gj, gm, glift, gdrop, blift, bdrop, bmix, bjoint = hand_out((gj, gm, glift, gdrop), gb, nf)
    return (out, token_grad, gj, bjoint, gm, bmix[0], glift, blift[0], gdrop, bdrop[0])


BOTH = ("gx", "gy")


def body(
    tokens,
    segment_ids,
    fill_lengths,
    joint_weight,
    joint_bias,
    mix_weight,
    mix_bias,
    lift_weight,
    lift_bias,
    drop_weight,
    drop_bias,
    cotangent,
):
    rows, length, width = tokens.shape
    n_tok = rows * length
    tok = tokens.reshape(n_tok, width)
    cot = cotangent.reshape(n_tok, width)
    starts = jnp.sum(
        segment_ids[:, None, :] < jnp.arange(128, dtype=jnp.int32)[None, :, None], axis=-1, dtype=jnp.int32
    )

    joint_w = lax.all_gather(joint_weight, BOTH, axis=0, tiled=True)
    mix_w = lax.all_gather(mix_weight, BOTH, axis=0, tiled=True)
    lift_w = lax.all_gather(lift_weight, BOTH, axis=0, tiled=True)
    drop_w = lax.all_gather(drop_weight, BOTH, axis=0, tiled=True)
    own_bias = jnp.concatenate([joint_bias.reshape(-1), mix_bias, lift_bias, drop_bias])
    sizes = [joint_bias.shape[1], joint_bias.shape[1], mix_bias.size, lift_bias.size, drop_bias.size]
    all_bias = lax.all_gather(own_bias, BOTH, axis=0)
    parts, at = [], 0
    for size in sizes:
        parts.append(all_bias[:, at : at + size].reshape(-1).astype(F32))
        at += size
    bq, bv, bm, bl, bd = parts
    nf = bl.size // 512
    bias = jnp.concatenate(
        [jnp.concatenate([bl.reshape(nf, 512), jnp.zeros((4 - nf, 512), F32)]), bd[None], bm[None], bq[None], bv[None]]
    )

    shift = jnp.concatenate([bq, jnp.zeros_like(bq), bv])
    qkv = (mm(tok, joint_w) + shift).astype(BF)
    qkv3 = qkv.reshape(rows, length, 3 * width)
    ctx, lse = attend(starts, fill_lengths, segment_ids, qkv3)
    lift_units = lift_w.reshape(width, nf, 512).transpose(1, 0, 2)
    out, gmid, gctx, glift, gdrop, gmix, gbias = feed(
        tok, ctx.reshape(n_tok, width), cot, mix_w, lift_units, drop_w.reshape(nf, 512, width), bias
    )
    gjoint, token_grad, out = attend_back(
        starts,
        fill_lengths,
        segment_ids,
        qkv3,
        lse,
        ctx,
        gctx.reshape(rows, length, width),
        gmid.reshape(rows, length, width),
        joint_w.reshape(width, 3, width).transpose(1, 0, 2),
        out.reshape(rows, length, width),
    )
    gjoint = gjoint.reshape(n_tok, 3 * width)
    gjoint_w = lax.dot_general(tok, gjoint, (((0,), (0,)), ((), ())), preferred_element_type=F32)
    sums = jnp.sum(gjoint.astype(F32), axis=0)

    glift_w = glift[:, :width].transpose(1, 0, 2).reshape(width, nf * 512)
    gdrop_w = gdrop.transpose(0, 2, 1).reshape(nf * 512, width)
    scatter = functools.partial(lax.psum_scatter, axis_name=BOTH, scatter_dimension=0, tiled=True)
    n_dev = all_bias.shape[0]
    packed = jnp.concatenate(
        [
            g.reshape(n_dev, -1)
            for g in (sums[:width], sums[2 * width :], gbias[5], gbias[:nf].reshape(-1), gbias[4])
        ],
        axis=1,
    )
    own = scatter(packed)[0]
    cuts, at = [], 0
    for size in sizes:
        cuts.append(own[at : at + size])
        at += size
    return (
        out,
        token_grad,
        scatter(gjoint_w),
        jnp.stack([cuts[0], cuts[1]]),
        scatter(gmix),
        cuts[2],
        scatter(glift_w),
        cuts[3],
        scatter(gdrop_w),
        cuts[4],
    )


def solution(mesh):
    wide = P(BOTH, None, None)
    rows = P(BOTH, None)
    flat = P(BOTH)
    bias = P(None, BOTH)
    in_specs = (wide, rows, flat, rows, bias, rows, flat, rows, flat, rows, flat, wide)
    out_specs = (wide, wide, rows, bias, rows, flat, rows, flat, rows, flat)
    fits = mesh.shape["gy"] == 8 and mesh.shape["gx"] == 4
    return jax.shard_map(remote_body if fits else body, mesh=mesh, in_specs=in_specs, out_specs=out_specs, check_vma=False)
```
